32 devices in a mesh: dp: 8 (over z, y), tensor: 4 (over x, core).
Axes of the slice: x: 2, y: 2, z: 4, core: 2. Of those that a mesh axis runs over, the one named last changes fastest.
Arguments:
- tokens: bfloat16 [4096, 768], P(('dp', 'tensor')), may hold values from -6 to 6
- doc_start: int32 [4096], P('dp'), may hold values from 0 to 511, as said below
- routes: int32 [4096, 2], P(('dp', 'tensor')), may hold values from 0 to 7, all different within a row; in each aligned block of 128 rows (0 to 127, 128 to 255, ...) at most 48 rows name the same one
- gain_attn: float32 [768], replicated, may hold values from 0.5 to 1.5
- w_qkv: bfloat16 [768, 3, 768], P('dp', None, 'tensor'), may hold values from -0.21875 to 0.21875
- w_out: bfloat16 [768, 768], P('dp', 'tensor'), may hold values from -1.25 to 1.25
- rel_bias: float32 [32, 12], replicated, may hold values from -4 to 4
- gain_ffn: float32 [768], replicated, may hold values from 0.5 to 1.5
- router: bfloat16 [768, 8], replicated, may hold values from -0.15625 to 0.15625
- w_in: bfloat16 [8, 768, 3072], P('dp', None, 'tensor'), may hold values from -0.21875 to 0.21875
- w_exp_out: bfloat16 [8, 3072, 768], P('dp', 'tensor'), may hold values from -0.109375 to 0.109375
- out_grad: bfloat16 [4096, 768], P(('dp', 'tensor')), may hold values from -6 to 6
Outputs:
- mixed_out: bfloat16 [4096, 768], P(('dp', 'tensor'))
- input_grad: bfloat16 [4096, 768], P(('dp', 'tensor'))
- grad_gain_attn: float32 [768], replicated
- grad_w_qkv: float32 [768, 3, 768], P('dp', None, 'tensor')
- grad_w_out: float32 [768, 768], P('dp', 'tensor')
- grad_rel_bias: float32 [32, 12], replicated
- grad_gain_ffn: float32 [768], replicated
- grad_router: float32 [768, 8], replicated
- grad_w_in: float32 [8, 768, 3072], P('dp', None, 'tensor')
- grad_w_exp_out: float32 [8, 3072, 768], P('dp', 'tensor')
The draws below stay inside these ranges and needn't reach their ends.
Inputs may be any that keep to these rules, and one draw needn't show every extreme that they name: `doc_start`: the position, within the group of 512 tokens of its index of dp, at which a token's document begins; a group holds one or two documents, the first of half of 512 tokens or more. `routes`: a token's two experts differ; among the 128 rows of one device no expert is named by more than 48 rows, a bound that some block reaches.
All inputs are finite; a program needn't handle non-finite values.
Results may differ from the reference program's by a relative error of at most 0.012.
Values may be sent and summed in bfloat16 or wider, within the bound.
No kernel may reach another device: no remote copies, remote signals or barrier semaphores. Data moves between devices by JAX's collectives and lax.ppermute only.
A program may use at most 128 MiB of HBM per device.

```python
import math
import jax
import jax.numpy as jnp
import numpy as np
from jax import lax

D = 768
HEADS = 12
HDIM = 64
FF = 3072
BUCKETS = 32
TOP = 2
TOK_DEV = 128
EXPERTS = 8
TOK_GRP = 512
TOKENS = 4096
CAP = 48


def draw_doc_start(key, part):
    key = jax.random.fold_in(key, 11)
    split_key, pick_key = jax.random.split(key)
    groups = TOKENS // TOK_GRP
    split = jax.random.randint(split_key, (groups, 1), TOK_GRP // 2, TOK_GRP + 1)
    chosen = jax.random.randint(pick_key, (), 0, groups)
    group_ids = jnp.arange(groups, dtype=jnp.int32)[:, None]
    split = jnp.where(group_ids == chosen, TOK_GRP - 1, split)
    place = jnp.arange(TOK_GRP, dtype=jnp.int32)[None, :]
    starts = jnp.where(place < split, 0, split)
    return starts.reshape(TOKENS).astype(jnp.int32)


def with_spikes(values, key, source, target, blocks, factor):
    owner, partner = [(jnp.arange(values.shape[axis_at]) // (values.shape[axis_at] // blocks)).reshape([-1 if axis == axis_at else 1 for axis in range(values.ndim)]) for axis_at in (source, target)]
    chosen = jax.random.permutation(key, blocks)[partner]
    strong = (owner == chosen) | (owner == (partner + blocks // 2) % blocks)
    return jnp.where(strong, factor * values, values)


def steps_of(own_key, extent, cuts, least, top_value):
    loudness = 1.0
    for axis_at, parts in cuts:
        draws = jax.random.uniform(jax.random.fold_in(jax.random.fold_in(own_key, 6), axis_at), (parts,), jnp.float32, least / len(cuts), top_value / len(cuts))
        loudness = loudness * jnp.repeat(jnp.exp(draws), extent[axis_at] // parts).reshape((-1,) + (1,) * (len(extent) - 1 - axis_at))
    return loudness


def routed_block(rng, own, number, rows, amount, top, reach, lean):
    order = jax.random.permutation(rng, amount)
    packed, common = shares(amount, rows * top, reach, lean, True), shares(amount, rows * top, reach, lean, False)
    places = jnp.arange(amount)

    def named(sizes, offset_by):
        used = int((sizes > 0).sum())
        fixed = max(1, used // 4)
        moved = fixed + (places - fixed + offset_by * (used - fixed)) % max(1, amount - fixed)
        return jnp.zeros((amount,), jnp.int32).at[order[jnp.where(places < fixed, places, moved)]].set(jnp.asarray(sizes, jnp.int32))

    sizes = jnp.where(number % 4 == 0, named(packed, number // 4), named(common, number - number // 4 - 1))
    mixed = jax.random.permutation(jax.random.fold_in(own, 3), amount)
    giver, receiver = mixed[0:amount // 2 * 2:2], mixed[1:amount // 2 * 2:2]
    margin = jnp.minimum(sizes[giver] - 1, reach - sizes[receiver]) // 2
    margin = jnp.where((giver == order[0]) | (receiver == order[0]) | (sizes[receiver] == 0), 0, jnp.maximum(margin, 0))
    moved = jax.random.randint(jax.random.fold_in(own, 4), (amount // 2,), 0, 1 << 20) % (margin + 1)
    sizes = sizes.at[giver].add(-moved).at[receiver].add(moved)
    members = jnp.searchsorted(jnp.cumsum(sizes), jnp.arange(rows * top), side="right").astype(jnp.int32)
    grid = members.reshape(top, rows).T
    grid = grid[jax.random.permutation(jax.random.fold_in(own, 1), rows)]
    offset_by = jax.random.randint(jax.random.fold_in(own, 2), (rows, 1), 0, top)
    return jnp.take_along_axis(grid, (jnp.arange(top)[None, :] + offset_by) % top, axis=1)


def shares(amount, total, reach, slope, full):
    loads = [(1 << 20) // math.isqrt(standing ** slope) + 1 for standing in range(1, amount + 1)]
    largest = reach if full else min(reach, max(-(-total // amount), total * loads[0] // sum(loads)))
    least = 1 if total - largest >= amount - 1 else 0
    counts, surplus = [largest] + [least] * (amount - 1), total - largest - least * (amount - 1)
    while surplus > 0:
        movable = [i for i in range(1, amount) if counts[i] < largest] or [i for i in range(1, amount) if counts[i] < reach]
        whole, budget = sum([loads[i] for i in movable]), surplus
        for i in movable:
            more = min(reach - counts[i], max(1, budget * loads[i] // whole), surplus)
            counts[i] = counts[i] + more
            surplus = surplus - more
    return np.array(counts)


def bell_draw(stream_key, extent, width, limit, cuts=(), kind=jnp.bfloat16):
    values = jax.random.normal(stream_key, extent, jnp.float32) * width
    if len(cuts) > 0:
        values = steps_of(stream_key, extent, cuts, -0.22, 0.18) * values
    return jnp.clip(values, min=-limit, max=limit).astype(kind)


def noise_with(key, shape, scale, limit, shards, heavy, kind=jnp.bfloat16):
    entries = scale * jax.random.normal(key, shape, jnp.float32)
    if shards:
        entries = entries * steps_of(key, shape, shards, -0.22, 0.18)
    return jnp.clip(with_spikes(entries, jax.random.fold_in(key, 3), *heavy), -limit, limit).astype(kind)


def setup_inputs(seed: int = 0) -> dict:
    streams_of = jax.random.split(jax.random.key(seed), 13)
    tokens = noise_with(streams_of[0], (TOKENS, D), 1.0, 6.0, ((0, 32),), (0, 1, 32, 2.75))
    doc_start = draw_doc_start(jax.random.fold_in(streams_of[12], 71), 0)
    routes_keys = jax.random.split(jax.random.fold_in(streams_of[2], 1), TOKENS // TOK_DEV)
    routes_turns = jax.random.permutation(jax.random.fold_in(streams_of[2], 3), TOKENS // TOK_DEV)
    routes = jax.vmap(lambda own, number: routed_block(jax.random.fold_in(streams_of[2], 2), own, number, TOK_DEV, EXPERTS, TOP, CAP, 1))(routes_keys, routes_turns).reshape((TOKENS, TOP))
    gain_attn = jnp.clip(1.0 + 0.1 * jax.random.normal(streams_of[3], (D,), jnp.float32), 0.5, 1.5)
    w_qkv = bell_draw(streams_of[4], (D, 3, HEADS * HDIM), D ** -0.5, 0.21875, ((0, 8), (2, 4)))
    w_out = bell_draw(streams_of[5], (D, HEADS * HDIM), (HEADS * HDIM // 32) ** -0.5, 1.25, ((0, 8), (1, 4)))
    rel_bias = bell_draw(streams_of[6], (BUCKETS, HEADS), 1.0, 4.0, (), jnp.float32)
    gain_ffn = jnp.clip(1.0 + 0.1 * jax.random.normal(streams_of[7], (D,), jnp.float32), 0.5, 1.5)
    router = bell_draw(streams_of[8], (D, EXPERTS), 0.027, 0.15625)
    w_in = bell_draw(streams_of[9], (EXPERTS, D, FF), D ** -0.5, 0.21875, ((0, 8), (2, 4)))
    w_exp_out = bell_draw(streams_of[10], (EXPERTS, FF, D), FF ** -0.5, 0.109375, ((0, 8), (1, 4)))
    out_grad = noise_with(streams_of[11], (TOKENS, D), 1.0, 6.0, ((0, 32),), (0, 1, 32, 2.75))
    return dict(tokens=tokens, doc_start=doc_start, routes=routes, gain_attn=gain_attn, w_qkv=w_qkv, w_out=w_out, rel_bias=rel_bias, gain_ffn=gain_ffn, router=router, w_in=w_in, w_exp_out=w_exp_out, out_grad=out_grad)


LIMITS = np.array([19, 21, 24, 27, 31, 35, 40, 46, 52, 59, 67, 77, 87, 99, 113], np.int32)
HIGHEST_PRECISION = lax.Precision.HIGHEST

@jax.custom_vjp
def low(v):
    return lax.optimization_barrier(v.astype(jnp.bfloat16)).astype(jnp.float32)

@jax.custom_vjp
def low_back(v):
    return v

def low_keep(v):
    return (low(v), None)

def low_pass(kept, grad):
    return (grad,)

def back_keep(v):
    return (v, None)

def back_low(kept, grad):
    return (low(grad),)
low.defvjp(low_keep, low_pass)
low_back.defvjp(back_keep, back_low)

def bucket_ids(length):
    place = jnp.arange(length, dtype=jnp.int32)
    distance = jnp.maximum(place[:, None] - place[None, :], 0)
    beyond = lax.optimization_barrier(jnp.sum((distance[:, :, None] >= jnp.asarray(LIMITS)[None, None, :]).astype(jnp.int32), axis=2))
    return jnp.where(distance < 16, distance, 16 + beyond).astype(jnp.int32)

def attend_group(item, rel_bias):
    projected, starts = item
    length = projected.shape[0]
    queries, keys_all, values_all = (projected[:, 0], projected[:, 1], projected[:, 2])
    bias_grid = jnp.transpose(rel_bias[bucket_ids(length)], (2, 0, 1))
    raw = jnp.einsum('ihd,jhd->hij', queries, keys_all, precision=HIGHEST_PRECISION) * HDIM ** (-0.5) + bias_grid
    raw = low_back(raw)
    place = jnp.arange(length, dtype=jnp.int32)
    allowed = (place[None, :] <= place[:, None]) & (place[None, :] >= starts[:, None])
    attention = jax.nn.softmax(jnp.where(allowed[None], raw, -1000000000.0), axis=-1)
    attended = jnp.einsum('hij,jhd->ihd', low(attention), values_all, precision=HIGHEST_PRECISION)
    return low_back(low(attended)).reshape(length, -1)

def expert(item):
    slot_rows, weight_in, weight_out = item
    pre_act = low_back(jnp.dot(slot_rows, weight_in, precision=HIGHEST_PRECISION))
    hidden = low(jax.nn.gelu(pre_act, approximate=True))
    return low_back(low(jnp.dot(hidden, weight_out, precision=HIGHEST_PRECISION)))

def layer(tokens, gain_attn, w_qkv, w_out, rel_bias, gain_ffn, router, w_in, w_exp_out, doc_start, routes, table, filled, route_pos):
    scale_one = lax.rsqrt(lax.optimization_barrier(jnp.mean(tokens * tokens, axis=1, keepdims=True)) + 1e-06)
    normed_one = low(tokens * scale_one * gain_attn)
    projected = low_back(low(jnp.einsum('td,dcf->tcf', normed_one, w_qkv, precision=HIGHEST_PRECISION)))
    groups = tokens.shape[0] // TOK_GRP
    projected = projected.reshape(groups, TOK_GRP, 3, HEADS, HDIM)
    attended = lax.map(jax.checkpoint(lambda item: attend_group(item, rel_bias)), (projected, doc_start.reshape(groups, TOK_GRP)))
    attended = attended.reshape(tokens.shape[0], HEADS * HDIM)
    mixed = tokens + low_back(jnp.einsum('tf,df->td', attended, w_out, precision=HIGHEST_PRECISION))
    scale_two = lax.rsqrt(lax.optimization_barrier(jnp.mean(mixed * mixed, axis=1, keepdims=True)) + 1e-06)
    normed_two = low(mixed * scale_two * gain_ffn)
    logits = jnp.dot(normed_two, router, precision=HIGHEST_PRECISION)
    gates = jax.nn.softmax(jnp.take_along_axis(logits, routes, axis=1), axis=1)
    slot_rows = low_back(normed_two[table] * filled[:, :, None])
    outputs = lax.map(jax.checkpoint(expert), (slot_rows, w_in, w_exp_out))
    picked = outputs[routes, route_pos]
    return mixed + lax.optimization_barrier(jnp.sum(gates[:, :, None] * picked, axis=1))

def reference(tokens, doc_start, routes, gain_attn, w_qkv, w_out, rel_bias, gain_ffn, router, w_in, w_exp_out, out_grad):
    blocks = TOKENS // TOK_DEV
    per_block = TOK_DEV * TOP
    expert_ids = routes.reshape(blocks, per_block).astype(jnp.int32)
    member = (expert_ids[:, :, None] == jnp.arange(EXPERTS, dtype=jnp.int32)[None, None, :]).astype(jnp.int32)
    slot_rank = lax.optimization_barrier(jnp.sum(member * (jnp.cumsum(member, axis=1).astype(jnp.int32) - 1), axis=2)).astype(jnp.int32)
    block_ids = jnp.arange(blocks, dtype=jnp.int32)[:, None]
    position = (block_ids * CAP + slot_rank).astype(jnp.int32)
    token_ids = (block_ids * TOK_DEV + jnp.arange(per_block, dtype=jnp.int32)[None, :] // TOP).astype(jnp.int32)
    table = jnp.zeros((EXPERTS, blocks * CAP), jnp.int32).at[expert_ids, position].set(token_ids)
    filled = jnp.zeros((EXPERTS, blocks * CAP), jnp.float32).at[expert_ids, position].set(1.0)
    route_pos = position.reshape(TOKENS, TOP)
    floats = [item.astype(jnp.float32) for item in (tokens, gain_attn, w_qkv, w_out, rel_bias, gain_ffn, router, w_in, w_exp_out)]

    def closed(*weights):
        return layer(*weights, doc_start, routes, table, filled, route_pos)
    result, pull = jax.vjp(closed, *floats)
    grads = pull(out_grad.astype(jnp.float32))
    return (result.astype(jnp.bfloat16), grads[0].astype(jnp.bfloat16), grads[1], grads[2], grads[3], grads[4], grads[5], grads[6], grads[7], grads[8])
```

```python
import functools

import jax
import jax.numpy as jnp
import numpy as np
from jax import lax
from jax.experimental import pallas as pl
from jax.experimental.pallas import tpu as pltpu
from jax.sharding import PartitionSpec as P

HEADS = 12
HDIM = 64
BUCKETS = 32
ROWS = 128
GATE_LANES = 128

LIMITS = np.array([19, 21, 24, 27, 31, 35, 40, 46, 52, 59, 67, 77, 87, 99, 113], np.int32)
HIGHEST = lax.Precision.HIGHEST
F32 = jnp.float32
BF16 = jnp.bfloat16
VMEM_BYTES = 48 * 1024 * 1024

NN = (((1,), (0,)), ((), ()))
NT = (((1,), (1,)), ((), ()))
TN = (((0,), (0,)), ((), ()))


def dot(left, right, dims=NN, precision=None):
    return lax.dot_general(left, right, dims, preferred_element_type=F32, precision=precision)


def iota(shape, axis):
    return lax.broadcasted_iota(jnp.int32, shape, axis)


def bucket_of(distance):
    bucket = jnp.minimum(distance, 16)
    for limit in LIMITS:
        bucket = bucket + (distance >= int(limit)).astype(jnp.int32)
    return bucket


def in_three(value):
    high = value.astype(BF16)
    rest = value - high.astype(F32)
    middle = rest.astype(BF16)
    low = (rest - middle.astype(F32)).astype(BF16)
    return high, middle, low


def three_lanes(value):
    high, middle, low = in_three(value)
    lane = iota((value.shape[0], GATE_LANES), 1)
    zero = jnp.zeros((value.shape[0], GATE_LANES), F32)
    spread = jnp.where(
        lane == 0,
        high.astype(F32),
        jnp.where(lane == 1, middle.astype(F32), jnp.where(lane == 2, low.astype(F32), zero)),
    )
    return spread.astype(BF16)


def lanes_sum(lanes):
    return jnp.sum(lanes.astype(F32), axis=1, keepdims=True)


def pick(columns, at):
    return columns[:, at : at + 1]


def call(kernel, outs, scratch, args, smem=0, flops=0, name=None):
    spec_vmem = pl.BlockSpec(memory_space=pltpu.VMEM)
    spec_smem = pl.BlockSpec(memory_space=pltpu.SMEM)
    moved = sum(a.size * a.dtype.itemsize for a in list(args) + list(outs))
    return pl.pallas_call(
        kernel,
        out_shape=[jax.ShapeDtypeStruct(o.shape, o.dtype) for o in outs],
        in_specs=[spec_smem] * smem + [spec_vmem] * (len(args) - smem),
        out_specs=[spec_vmem] * len(outs),
        scratch_shapes=scratch,
        compiler_params=pltpu.CompilerParams(vmem_limit_bytes=VMEM_BYTES),
        cost_estimate=pl.CostEstimate(flops=flops, bytes_accessed=moved, transcendentals=0),
        name=name,
    )(*args)


def struct(shape, dtype):
    return jax.ShapeDtypeStruct(shape, dtype)


def slots_kernel(capacity, routes_ref, grad_ref, slot_ref, out_ref):
    tokens = routes_ref.shape[0]
    slots = out_ref.shape[0]
    experts = slots // capacity
    routes = routes_ref[...]
    first, second = routes[:, 0:1], routes[:, 1:2]
    lane = iota((tokens, experts), 1)
    one_first = (first == lane).astype(F32)
    one_second = (second == lane).astype(F32)
    member = (one_first + one_second).astype(BF16)
    below = (iota((tokens, tokens), 1) < iota((tokens, tokens), 0)).astype(F32).astype(BF16)
    earlier = dot(below, member)
    slot_first = first * capacity + jnp.sum(one_first * earlier, axis=1, keepdims=True).astype(
        jnp.int32
    )
    slot_second = second * capacity + jnp.sum(one_second * earlier, axis=1, keepdims=True).astype(
        jnp.int32
    )
    wide = iota((tokens, 128), 1)
    slot_ref[...] = jnp.where(wide == 0, slot_first, slot_second)
    places = iota((tokens, slots), 1)
    chosen = ((slot_first == places) | (slot_second == places)).astype(F32).astype(BF16)
    out_ref[...] = dot(chosen, grad_ref[...], TN).astype(BF16)


def bias_tiles(rel_ref, first_head, heads):
    column = iota((8, 256), 1)
    distance = (ROWS - column) & 255
    bucket = bucket_of(distance)
    tiles = []
    for head in range(heads):
        line = jnp.zeros((8, 256), F32)
        for b in range(BUCKETS):
            line = jnp.where(bucket == b, rel_ref[b, first_head + head], line)
        wide = jnp.broadcast_to(line[0:1, :], (ROWS, 256))
        tiles.append(pltpu.roll(wide, 0, 1, stride=1, stride_axis=0))
    return tiles


def masked_scores(query, keys, tile, far, starts, block):
    width = (block + 1) * ROWS
    raw = dot(query, keys, NT) * HDIM**-0.5
    if block == 0:
        bias = tile[:, ROWS:]
    elif block == 1:
        bias = tile
    else:
        bias = jnp.concatenate([jnp.full((ROWS, width - 2 * ROWS), far, F32), tile], axis=1)
    column = iota((ROWS, width), 1)
    row = iota((ROWS, width), 0) + block * ROWS
    allowed = (column <= row) & (column >= starts)
    return jnp.where(allowed, raw + bias, -1e9)


def forward_kernel(parts, pieces, heads, *refs):
    place_ref, start_ref, rel_ref = refs[:3]
    weights = refs[3 : 3 + parts]
    rows = refs[3 + parts : 3 + parts + pieces]
    gain_ref, doc_ref = refs[3 + parts + pieces : 5 + parts + pieces]
    weight_out, row_out, proj_out, att_out, lse_out, keep_out, send_out = refs[
        5 + parts + pieces : 12 + parts + pieces
    ]
    piece = place_ref[1]
    cols = heads * HDIM
    for at in range(parts):
        depth = weights[at].shape[0]
        weight_out[pl.ds(pl.multiple_of(start_ref[at], 16), depth), :] = weights[at][...]
    for at in range(pieces):
        row_out[pl.ds(pl.multiple_of((piece ^ at) * ROWS, ROWS), ROWS), :] = rows[at][...]
    x = row_out[...].astype(F32)
    scale = lax.rsqrt(jnp.mean(x * x, axis=1, keepdims=True) + 1e-6)
    normed = (x * scale * gain_ref[...]).astype(BF16)
    proj_out[...] = dot(normed, weight_out[:, : 3 * cols]).astype(BF16)
    tiles = bias_tiles(rel_ref, piece * heads, heads)
    blocks = x.shape[0] // ROWS
    proj = proj_out[...]
    wide = iota((ROWS, 128), 1)
    for block in range(blocks):
        here = slice(block * ROWS, (block + 1) * ROWS)
        upto = slice(0, (block + 1) * ROWS)
        starts = doc_ref[here, :]
        done = []
        kept = jnp.zeros((ROWS, 128), F32)
        for head in range(heads):
            at = head * HDIM
            query = proj[here, at : at + HDIM]
            keys = proj[upto, cols + at : cols + at + HDIM]
            values = proj[upto, 2 * cols + at : 2 * cols + at + HDIM]
            far = rel_ref[BUCKETS - 1, piece * heads + head]
            scores = masked_scores(query, keys, tiles[head], far, starts, block)
            peak = jnp.max(scores, axis=1, keepdims=True)
            shifted = jnp.exp(scores - peak)
            total = jnp.sum(shifted, axis=1, keepdims=True)
            attention = (shifted * (1.0 / total)).astype(BF16)
            done.append(dot(attention, values).astype(BF16))
            kept = jnp.where(wide == head, peak + jnp.log(total), kept)
        att_out[here, :] = jnp.concatenate(done, axis=1)
        lse_out[here, :] = kept
    weight_last = weight_out[:, 3 * cols :]
    for at in range(pieces):
        mine = att_out[pl.ds(pl.multiple_of((piece ^ at) * ROWS, ROWS), ROWS), :]
        product = dot(mine, weight_last, NT)
        if at % 2 == 0:
            keep_out[at // 2] = product
        else:
            send_out[at // 2] = product.astype(BF16)


def dispatch_kernel(
    own_ref,
    part_ref,
    near_ref,
    far_ref,
    gain_ref,
    router_ref,
    routes_ref,
    slot_ref,
    mixed_ref,
    normed_ref,
    gates_ref,
    out_ref,
):
    width = own_ref.shape[1]
    tokens = own_ref.shape[0]
    slots = out_ref.shape[0]
    mixed = own_ref[...].astype(F32) + (
        part_ref[...] + near_ref[...].astype(F32) + far_ref[...].astype(F32)
    )
    mixed_ref[...] = mixed
    scale = lax.rsqrt(jnp.mean(mixed * mixed, axis=1, keepdims=True) + 1e-6)
    normed = (mixed * scale * gain_ref[...]).astype(BF16)
    normed_ref[...] = normed
    logits = dot(normed, router_ref[...])
    routes = routes_ref[...]
    lane = iota(logits.shape, 1)
    one = jnp.sum(jnp.where(routes[:, 0:1] == lane, logits, 0.0), axis=1, keepdims=True)
    two = jnp.sum(jnp.where(routes[:, 1:2] == lane, logits, 0.0), axis=1, keepdims=True)
    peak = jnp.maximum(one, two)
    one, two = jnp.exp(one - peak), jnp.exp(two - peak)
    total = one + two
    one, two = one / total, two / total
    wide = iota((tokens, 128), 1)
    gates_ref[...] = jnp.where(wide == 0, one, two)
    places = iota((tokens, slots), 1)
    slot = slot_ref[...]
    first = (slot[:, 0:1] == places).astype(F32).astype(BF16)
    second = (slot[:, 1:2] == places).astype(F32).astype(BF16)
    out_ref[:, :width] = dot(first + second, normed, TN).astype(BF16)
    gate_slots = dot(first, three_lanes(one), TN) + dot(second, three_lanes(two), TN)
    out_ref[:, width:] = gate_slots.astype(BF16)


def gelu_and_slope(x):
    inner = 0.7978845608028654 * (x + 0.044715 * (x * x * x))
    bend = jnp.tanh(inner)
    half = 0.5 * (1.0 + bend)
    slope = half + 0.5 * x * (1.0 - bend * bend) * (
        0.7978845608028654 * (1.0 + 3 * 0.044715 * (x * x))
    )
    return x * half, slope


def expert_kernel(
    own_ref,
    mate_ref,
    in_one,
    in_two,
    back_one,
    back_two,
    hidden_one,
    hidden_two,
    slope_one,
    slope_two,
    keep_ref,
    send_ref,
    total,
    gate_total,
):
    step = pl.program_id(0)
    rows = own_ref.shape[0]
    width = in_one.shape[0]

    @pl.when(step == 0)
    def _():
        total[...] = jnp.zeros_like(total)
        gate_total[...] = jnp.zeros_like(gate_total)

    for side, source in enumerate((own_ref, mate_ref)):
        here = slice(side * rows, (side + 1) * rows)
        slot_rows = source[:, :width]
        gate = lanes_sum(source[:, width:])
        for weights, back, hidden_out, slope_out in (
            (in_one, back_one, hidden_one, slope_one),
            (in_two, back_two, hidden_two, slope_two),
        ):
            pre = dot(slot_rows, weights[...])
            hidden, slope = gelu_and_slope(pre)
            hidden = hidden.astype(BF16)
            pulled = back[here, :]
            pre_grad = (pulled * gate * slope).astype(BF16)
            hidden_out[here, :] = hidden
            slope_out[here, :] = pre_grad
            total[here, :] += dot(pre_grad, weights[...], NT)
            gate_total[here, :] += jnp.sum(hidden.astype(F32) * pulled, axis=1, keepdims=True)

    @pl.when(step == pl.num_programs(0) - 1)
    def _():
        keep_ref[:, :width] = total[:rows, :]
        keep_ref[:, width:] = gate_total[:rows, :]
        send_ref[:, :width] = total[rows:, :].astype(BF16)
        send_ref[:, width:] = three_lanes(gate_total[rows:, 0:1])


def run_experts(own, mate, in_one, in_two, back_one, back_two):
    rows, payload = own.shape
    width, hidden = in_one.shape
    tile = 256
    steps = hidden // tile
    whole = lambda shape: pl.BlockSpec(shape, lambda i: (0, 0))
    column = lambda height: pl.BlockSpec((height, tile), lambda i: (0, i))
    return pl.pallas_call(
        expert_kernel,
        grid=(steps,),
        in_specs=[whole((rows, payload))] * 2 + [column(width)] * 2 + [column(2 * rows)] * 2,
        out_specs=[column(2 * rows)] * 4 + [whole((rows, payload))] * 2,
        out_shape=[struct((2 * rows, hidden), BF16)] * 4
        + [struct((rows, payload), F32), struct((rows, payload), BF16)],
        scratch_shapes=[
            pltpu.VMEM((2 * rows, width), F32),
            pltpu.VMEM((2 * rows, GATE_LANES), F32),
        ],
        compiler_params=pltpu.CompilerParams(vmem_limit_bytes=VMEM_BYTES),
        cost_estimate=pl.CostEstimate(
            flops=8 * 2 * rows * width * hidden, bytes_accessed=16 << 20, transcendentals=0
        ),
        name="experts",
    )(own, mate, in_one, in_two, back_one, back_two)


def merge_kernel(keep_ref, mate_ref, out_ref):
    width = keep_ref.shape[1] - GATE_LANES
    out_ref[:, :width] = (keep_ref[:, :width] + mate_ref[:, :width].astype(F32)).astype(BF16)
    gate = keep_ref[:, width : width + 1] + lanes_sum(mate_ref[:, width:])
    out_ref[:, width:] = three_lanes(gate)


def combine_kernel(
    back_ref,
    slot_ref,
    gates_ref,
    mixed_ref,
    normed_ref,
    router_ref,
    routes_ref,
    grad_ref,
    gain_ref,
    mixed_grad_ref,
    low_ref,
    sums_ref,
):
    tokens, width = grad_ref.shape
    slots = back_ref.shape[0]
    experts = router_ref.shape[1]
    places = iota((tokens, slots), 1)
    slot = slot_ref[...]
    first = (slot[:, 0:1] == places).astype(F32).astype(BF16)
    second = (slot[:, 1:2] == places).astype(F32).astype(BF16)
    lanes = back_ref[:, width:]
    pull_one = jnp.sum(dot(first, lanes), axis=1, keepdims=True)
    pull_two = jnp.sum(dot(second, lanes), axis=1, keepdims=True)
    one, two = gates_ref[:, 0:1], gates_ref[:, 1:2]
    mean_pull = one * pull_one + two * pull_two
    delta_one = one * (pull_one - mean_pull)
    delta_two = two * (pull_two - mean_pull)
    routes = routes_ref[...]
    lane = iota((tokens, experts), 1)
    logit_grad = jnp.where(routes[:, 0:1] == lane, delta_one, 0.0) + jnp.where(
        routes[:, 1:2] == lane, delta_two, 0.0
    )
    high = logit_grad.astype(BF16)
    low = (logit_grad - high.astype(F32)).astype(BF16)
    normed = normed_ref[...]
    router = router_ref[...]
    normed_grad = dot(first + second, back_ref[:, :width]) + (
        dot(high, router, NT) + dot(low, router, NT)
    )
    mixed = mixed_ref[...]
    grad = grad_ref[...].astype(F32)
    scale = lax.rsqrt(jnp.mean(mixed * mixed, axis=1, keepdims=True) + 1e-6)
    scaled = normed_grad * gain_ref[...]
    cubed = scale * scale * scale
    mixed_grad = (
        grad
        + scale * scaled
        - mixed * cubed * jnp.mean(scaled * mixed, axis=1, keepdims=True)
    )
    mixed_grad_ref[...] = mixed_grad
    low_ref[...] = mixed_grad.astype(BF16)
    sums_ref[...] = jnp.zeros_like(sums_ref)
    sums_ref[:experts, :] = dot(high, normed, TN) + dot(low, normed, TN)
    sums_ref[experts : experts + 1, :] = jnp.sum(
        normed_grad * mixed * scale, axis=0, keepdims=True
    )


def result_kernel(back_ref, slot_ref, gates_ref, mixed_ref, out_ref):
    tokens = mixed_ref.shape[0]
    slots = back_ref.shape[0]
    places = iota((tokens, slots), 1)
    slot = slot_ref[...]
    first = (slot[:, 0:1] == places).astype(F32).astype(BF16)
    second = (slot[:, 1:2] == places).astype(F32).astype(BF16)
    back = back_ref[...]
    added = gates_ref[:, 0:1] * dot(first, back) + gates_ref[:, 1:2] * dot(second, back)
    out_ref[...] = (mixed_ref[...] + added).astype(BF16)


def backward_kernel(parts, pieces, heads, *refs):
    place_ref, start_ref, rel_ref = refs[:3]
    lows = refs[3 : 3 + pieces]
    weight_ref, row_ref, proj_ref, att_ref, lse_ref, gain_ref, doc_ref = refs[
        3 + pieces : 10 + pieces
    ]
    outs = refs[10 + pieces :]
    if parts > 1:
        grad_keep, grad_send, keep_out, send_out, sums_out, mixed, grad_proj, normed_grad, grads = outs
    else:
        grad_keep, keep_out, send_out, sums_out, mixed, grad_proj, normed_grad = outs
    piece = place_ref[1]
    cols = heads * HDIM
    for at in range(pieces):
        mixed[pl.ds(pl.multiple_of((piece ^ at) * ROWS, ROWS), ROWS), :] = lows[at][...]
    weight_last = weight_ref[:, 3 * cols :]
    att_grad = dot(mixed[...], weight_last).astype(BF16)
    grad_last = dot(mixed[...], att_ref[...], TN)
    tiles = bias_tiles(rel_ref, piece * heads, heads)
    proj = proj_ref[...]
    length = proj.shape[0]
    blocks = length // ROWS
    bucket_wide = bucket_of(jnp.maximum(ROWS + iota((ROWS, 256), 0) - iota((ROWS, 256), 1), 0))
    target = iota((8, HEADS * BUCKETS), 1)
    bias_row = jnp.zeros((8, HEADS * BUCKETS), F32)
    grads_q, grads_k, grads_v = [], [], []
    for head in range(heads):
        at = head * HDIM
        far = rel_ref[BUCKETS - 1, piece * heads + head]
        key_sum = [jnp.zeros((ROWS, HDIM), F32) for _ in range(blocks)]
        value_sum = [jnp.zeros((ROWS, HDIM), F32) for _ in range(blocks)]
        near_sum = jnp.zeros((ROWS, 256), F32)
        far_sum = jnp.zeros((ROWS, ROWS), F32)
        query_done = []
        for block in range(blocks):
            here = slice(block * ROWS, (block + 1) * ROWS)
            upto = slice(0, (block + 1) * ROWS)
            query = proj[here, at : at + HDIM]
            keys = proj[upto, cols + at : cols + at + HDIM]
            values = proj[upto, 2 * cols + at : 2 * cols + at + HDIM]
            out_grad = att_grad[here, at : at + HDIM]
            scores = masked_scores(query, keys, tiles[head], far, doc_ref[here, :], block)
            again = jnp.exp(scores - lse_ref[here, head : head + 1])
            prob_grad = dot(out_grad, values, NT)
            weighted = again * prob_grad
            score_grad = weighted - again * jnp.sum(weighted, axis=1, keepdims=True)
            score_low = score_grad.astype(BF16)
            value_add = dot(again.astype(BF16), out_grad, TN)
            key_add = dot(score_low, query, TN)
            for other in range(block + 1):
                there = slice(other * ROWS, (other + 1) * ROWS)
                key_sum[other] = key_sum[other] + key_add[there, :]
                value_sum[other] = value_sum[other] + value_add[there, :]
                if other < block - 1:
                    far_sum = far_sum + score_grad[:, there]
            if block == 0:
                near_sum = near_sum + jnp.concatenate(
                    [jnp.zeros((ROWS, ROWS), F32), score_grad], axis=1
                )
            else:
                near_sum = near_sum + score_grad[:, (block - 1) * ROWS :]
            query_done.append(dot(score_low, keys) * HDIM**-0.5)
        grads_q.append(jnp.concatenate(query_done, axis=0))
        grads_k.append(jnp.concatenate(key_sum, axis=0) * HDIM**-0.5)
        grads_v.append(jnp.concatenate(value_sum, axis=0))
        first_lane = (piece * heads + head) * BUCKETS
        for b in range(BUCKETS):
            amount = jnp.sum(jnp.where(bucket_wide == b, near_sum, 0.0))
            if b == BUCKETS - 1:
                amount = amount + jnp.sum(far_sum)
            bias_row = bias_row + jnp.where(target == first_lane + b, amount, 0.0)
    grad_proj[...] = jnp.concatenate(grads_q + grads_k + grads_v, axis=1).astype(BF16)
    x = row_ref[...].astype(F32)
    scale = lax.rsqrt(jnp.mean(x * x, axis=1, keepdims=True) + 1e-6)
    unit = x * scale
    normed = (unit * gain_ref[...]).astype(BF16)
    grad_first = dot(normed, grad_proj[...], TN)
    if parts > 1:
        depth = grad_first.shape[0] // parts
        grads[:, : 3 * cols] = grad_first
        grads[:, 3 * cols :] = grad_last
        for at in range(parts):
            piece_rows = grads[pl.ds(pl.multiple_of(start_ref[at], 16), depth), :]
            if at % 2 == 0:
                grad_keep[at // 2] = piece_rows
            else:
                grad_send[at // 2] = piece_rows.astype(BF16)
    else:
        grad_keep[:, : 3 * cols] = grad_first
        grad_keep[:, 3 * cols :] = grad_last
    normed_grad[...] = dot(grad_proj[...], weight_ref[:, : 3 * cols], NT)
    sums_out[...] = jnp.zeros_like(sums_out)
    sums_out[0:1, :] = jnp.sum(normed_grad[...] * unit, axis=0, keepdims=True)
    sums_out[1:2, : HEADS * BUCKETS] = bias_row[0:1, :]
    for at in range(pieces):
        mine = normed_grad[pl.ds(pl.multiple_of((piece ^ at) * ROWS, ROWS), ROWS), :]
        if at % 2 == 0:
            keep_out[at // 2] = mine
        else:
            send_out[at // 2] = mine.astype(BF16)


def input_kernel(own_ref, gain_ref, mixed_grad_ref, part_ref, near_ref, far_ref, out_ref):
    x = own_ref[...].astype(F32)
    scale = lax.rsqrt(jnp.mean(x * x, axis=1, keepdims=True) + 1e-6)
    scaled = (
        part_ref[...] + near_ref[...].astype(F32) + far_ref[...].astype(F32)
    ) * gain_ref[...]
    cubed = scale * scale * scale
    own = scale * scaled - x * cubed * jnp.mean(scaled * x, axis=1, keepdims=True)
    out_ref[...] = (mixed_grad_ref[...] + own).astype(BF16)


def swap(value, axis, size, mask):
    return lax.ppermute(value, axis, [(i, i ^ mask) for i in range(size)])


def gather_weights(shard, senders):
    mine = lax.axis_index("dp")
    depth = shard.shape[0]
    if senders != 8:
        return [lax.all_gather(shard, "dp", axis=0, tiled=True)], jnp.zeros((1,), jnp.int32)
    parts = {0: shard}
    parts[1] = swap(shard, "dp", senders, 1)
    for mask in (2, 4, 6):
        parts[mask] = swap(shard, "dp", senders, mask)
    for mask in (2, 4, 6):
        parts[mask + 1] = swap(parts[mask], "dp", senders, 1)
    starts = (mine ^ jnp.arange(senders, dtype=jnp.int32)) * depth
    return [parts[i] for i in range(senders)], starts


def scatter_grads(keep, send, senders):
    if senders != 8:
        return lax.psum_scatter(keep, "dp", scatter_dimension=0, tiled=True)
    halves = {}
    for at in (3, 2, 1, 0):
        near = swap(send[at], "dp", senders, 1)
        halves[at] = keep[at] + near.astype(F32)
    total = halves[0]
    arrived = [swap(halves[at].astype(BF16), "dp", senders, 2 * at) for at in (3, 2, 1)]
    for part in arrived:
        total = total + part.astype(F32)
    return total


def scatter_rows(keep, send, pieces):
    near = swap(send, "tensor", pieces, 1)
    other = (keep[1] + near[1].astype(F32)).astype(BF16)
    return keep[0], near[0], swap(other, "tensor", pieces, 2)


def gather_rows(rows, pieces):
    far = swap(rows, "tensor", pieces, 2)
    near = swap(rows, "tensor", pieces, 1)
    last = swap(far, "tensor", pieces, 1)
    return [rows, near, far, last]


def to_all(value, senders, pieces):
    if senders != 8:
        return lax.psum(value, ("dp", "tensor"))
    for axis, size in (("tensor", pieces), ("dp", senders)):
        mask = 1
        while mask < size:
            value = value + swap(value, axis, size, mask)
            mask *= 2
    return value


def exchange(blocks, senders, capacity):
    rows, width = blocks.shape
    return lax.all_to_all(
        blocks.reshape(senders, capacity, width), "dp", split_axis=0, concat_axis=0, tiled=True
    ).reshape(rows, width)


def body(
    tokens,
    doc_start,
    routes,
    gain_attn,
    w_qkv,
    w_out,
    rel_bias,
    gain_ffn,
    router,
    w_in,
    w_exp_out,
    out_grad,
):
    pieces = lax.axis_size("tensor")
    senders = lax.axis_size("dp")
    tok_dev, width = tokens.shape
    length = tok_dev * pieces
    experts = router.shape[1]
    capacity = max(2, 3 * tok_dev * routes.shape[1] // (2 * experts))
    slots = experts * capacity
    heads = w_out.shape[1] // HDIM
    cols = heads * HDIM
    place = jnp.stack([lax.axis_index("dp"), lax.axis_index("tensor")]).astype(jnp.int32)
    gain_one = gain_attn.reshape(1, width)
    gain_two = gain_ffn.reshape(1, width)
    doc_column = doc_start.reshape(length, 1)

    shard = jnp.concatenate([w_qkv.reshape(w_qkv.shape[0], 3 * cols), w_out], axis=1)
    weights, starts = gather_weights(shard, senders)
    rows = gather_rows(tokens, pieces)
    in_one, out_one = w_in[0], w_exp_out[0]
    in_two = swap(in_one, "tensor", pieces, 2)
    out_two = swap(out_one, "tensor", pieces, 2)

    slot, grad_out = call(
        functools.partial(slots_kernel, capacity),
        [struct((tok_dev, 128), jnp.int32), struct((slots, width), BF16)],
        [],
        [routes, out_grad],
        flops=2 * slots * tok_dev * width,
        name="slots",
    )

    whole_weight, whole_rows, projected, attended, lse, keep, send = call(
        functools.partial(forward_kernel, len(weights), pieces, heads),
        [
            struct((width, 4 * cols), BF16),
            struct((length, width), BF16),
            struct((length, 3 * cols), BF16),
            struct((length, cols), BF16),
            struct((length, 128), F32),
            struct((pieces // 2, tok_dev, width), F32),
            struct((pieces // 2, tok_dev, width), BF16),
        ],
        [],
        [place, starts, rel_bias] + weights + rows + [gain_one, doc_column],
        smem=3,
        flops=2 * length * width * 4 * cols + 4 * heads * length * length * HDIM,
        name="attend",
    )
    grad_rows = exchange(grad_out, senders, capacity)
    grad_both = jnp.concatenate([grad_rows, swap(grad_rows, "tensor", pieces, 1)], axis=0)
    back_one = dot(grad_both, out_one, NT)
    back_two = dot(grad_both, out_two, NT)

    part, near, far = scatter_rows(keep, send, pieces)
    mixed, normed_two, gates, outgoing = call(
        dispatch_kernel,
        [
            struct((tok_dev, width), F32),
            struct((tok_dev, width), BF16),
            struct((tok_dev, 128), F32),
            struct((slots, width + GATE_LANES), BF16),
        ],
        [],
        [tokens, part, near, far, gain_two, router, routes, slot],
        flops=2 * slots * tok_dev * width,
        name="dispatch",
    )
    slot_own = exchange(outgoing, senders, capacity)
    slot_mate = swap(slot_own, "tensor", pieces, 1)
    hidden_one, hidden_two, pre_one, pre_two, row_keep, row_send = run_experts(
        slot_own, slot_mate, in_one, in_two, back_one, back_two
    )
    row_mate = swap(row_send, "tensor", pieces, 1)
    (row_out,) = call(
        merge_kernel,
        [struct((slots, width + GATE_LANES), BF16)],
        [],
        [row_keep, row_mate],
        name="merge",
    )
    back = exchange(row_out, senders, capacity)

    slot_rows = jnp.concatenate([slot_own[:, :width], slot_mate[:, :width]], axis=0)
    gate_lanes = jnp.concatenate([slot_own[:, width:], slot_mate[:, width:]], axis=0)
    slot_gates = jnp.sum(gate_lanes.astype(F32), axis=1, keepdims=True)
    route_grad = (slot_gates * grad_both.astype(F32)).astype(BF16)
    partial_out = dot(hidden_one, out_one) + dot(hidden_two, out_two)
    out_mate = swap(partial_out[slots:].astype(BF16), "tensor", pieces, 1)
    expert_out = (partial_out[:slots] + out_mate.astype(F32)).astype(BF16)
    grad_out_two = swap(dot(hidden_two, route_grad, TN).astype(BF16), "tensor", pieces, 2)
    grad_in_two = swap(dot(slot_rows, pre_two, TN).astype(BF16), "tensor", pieces, 2)
    grad_out_sum = dot(hidden_one, route_grad, TN) + grad_out_two.astype(F32)
    grad_in_sum = dot(slot_rows, pre_one, TN) + grad_in_two.astype(F32)

    sum_rows = -(-(experts + 1) // 8) * 8
    mixed_grad, mixed_low, sums_two = call(
        combine_kernel,
        [
            struct((tok_dev, width), F32),
            struct((tok_dev, width), BF16),
            struct((sum_rows, width), F32),
        ],
        [],
        [back, slot, gates, mixed, normed_two, router, routes, out_grad, gain_two],
        flops=2 * slots * tok_dev * width,
        name="combine",
    )
    returned = exchange(expert_out, senders, capacity)
    (result,) = call(
        result_kernel,
        [struct((tok_dev, width), BF16)],
        [],
        [returned, slot, gates, mixed],
        flops=4 * slots * tok_dev * width,
        name="result",
    )

    lows = gather_rows(mixed_low, pieces)
    parts = len(weights)
    if parts > 1:
        grad_outs = [
            struct((parts // 2, width // parts, 4 * cols), F32),
            struct((parts // 2, width // parts, 4 * cols), BF16),
        ]
        grad_scratch = [pltpu.VMEM((width, 4 * cols), F32)]
    else:
        grad_outs = [struct((width, 4 * cols), F32)]
        grad_scratch = []
    *weight_grads, keep, send, sums_one = call(
        functools.partial(backward_kernel, parts, pieces, heads),
        grad_outs
        + [
            struct((pieces // 2, tok_dev, width), F32),
            struct((pieces // 2, tok_dev, width), BF16),
            struct((8, width), F32),
        ],
        [
            pltpu.VMEM((length, width), BF16),
            pltpu.VMEM((length, 3 * cols), BF16),
            pltpu.VMEM((length, width), F32),
        ]
        + grad_scratch,
        [place, starts, rel_bias]
        + lows
        + [whole_weight, whole_rows, projected, attended, lse, gain_one, doc_column],
        smem=3,
        flops=6 * length * width * 4 * cols + 10 * heads * length * length * HDIM,
        name="attend_back",
    )
    weight_sum = scatter_grads(weight_grads[0], weight_grads[-1], senders)
    part, near, far = scatter_rows(keep, send, pieces)
    (input_grad,) = call(
        input_kernel,
        [struct((tok_dev, width), BF16)],
        [],
        [tokens, gain_one, mixed_grad, part, near, far],
        name="input_grad",
    )
    summed = to_all(jnp.concatenate([sums_one, sums_two], axis=0), senders, pieces)
    bias_grad = summed[1, : HEADS * BUCKETS].reshape(HEADS, BUCKETS).T
    return (
        result,
        input_grad,
        summed[0],
        weight_sum[:, : 3 * cols].reshape(-1, 3, cols),
        weight_sum[:, 3 * cols :],
        bias_grad,
        summed[8 + experts],
        summed[8 : 8 + experts].T,
        grad_in_sum[None],
        grad_out_sum[None],
    )


def solution(mesh):
    in_specs = (
        P(("dp", "tensor"), None),
        P("dp"),
        P(("dp", "tensor"), None),
        P(),
        P("dp", None, "tensor"),
        P("dp", "tensor"),
        P(),
        P(),
        P(),
        P("dp", None, "tensor"),
        P("dp", "tensor", None),
        P(("dp", "tensor"), None),
    )
    out_specs = (
        P(("dp", "tensor"), None),
        P(("dp", "tensor"), None),
        P(),
        P("dp", None, "tensor"),
        P("dp", "tensor"),
        P(),
        P(),
        P(),
        P("dp", None, "tensor"),
        P("dp", "tensor", None),
    )
    return jax.shard_map(body, mesh=mesh, in_specs=in_specs, out_specs=out_specs, check_vma=False)
```

```python
import functools

import jax
import jax.numpy as jnp
import numpy as np
from jax import lax
from jax.experimental import pallas as pl
from jax.experimental.pallas import tpu as pltpu
from jax.sharding import PartitionSpec as P

HEADS = 12
HDIM = 64
BUCKETS = 32
ROWS = 128
GATE_LANES = 128

LIMITS = np.array([19, 21, 24, 27, 31, 35, 40, 46, 52, 59, 67, 77, 87, 99, 113], np.int32)
HIGHEST = lax.Precision.HIGHEST
F32 = jnp.float32
BF16 = jnp.bfloat16
MIB = 1024 * 1024

NN = (((1,), (0,)), ((), ()))
NT = (((1,), (1,)), ((), ()))
TN = (((0,), (0,)), ((), ()))


def dot(left, right, dims=NN, precision=None):
    return lax.dot_general(left, right, dims, preferred_element_type=F32, precision=precision)


def iota(shape, axis):
    return lax.broadcasted_iota(jnp.int32, shape, axis)


def bucket_of(distance):
    bucket = jnp.minimum(distance, 16)
    for limit in LIMITS:
        bucket = bucket + (distance >= int(limit)).astype(jnp.int32)
    return bucket


def in_three(value):
    high = value.astype(BF16)
    rest = value - high.astype(F32)
    middle = rest.astype(BF16)
    low = (rest - middle.astype(F32)).astype(BF16)
    return high, middle, low


def three_lanes(value):
    high, middle, low = in_three(value)
    lane = iota((value.shape[0], GATE_LANES), 1)
    zero = jnp.zeros((value.shape[0], GATE_LANES), F32)
    spread = jnp.where(
        lane == 0,
        high.astype(F32),
        jnp.where(lane == 1, middle.astype(F32), jnp.where(lane == 2, low.astype(F32), zero)),
    )
    return spread.astype(BF16)


def lanes_sum(lanes):
    return jnp.sum(lanes.astype(F32), axis=1, keepdims=True)


def pick(columns, at):
    return columns[:, at : at + 1]


def call(
    kernel,
    outs,
    scratch,
    args,
    smem=0,
    flops=0,
    name=None,
    after=(),
    vmem=6,
    held=(),
    kept=(),
    passed=(),
    prompt=False,
):
    n_in, n_after, n_out = len(args), len(after), len(outs)
    n_pass = len(passed)

    def run(*refs):
        ins, rest = refs[:n_in], refs[n_in + n_after + n_pass :]
        kernel(*ins, *rest[:n_out], *rest[n_out + n_pass :])

    def whole(a):
        return pl.BlockSpec(a.shape, lambda i: (0,) * len(a.shape))

    moved = sum(a.size * a.dtype.itemsize for a in list(args) + list(outs))
    args = [
        pltpu.with_memory_space_constraint(a, pltpu.HBM) if at in held else a
        for at, a in enumerate(args)
    ]
    after = [
        pltpu.with_memory_space_constraint(a, pltpu.HBM) if a.size > 1 << 18 else a for a in after
    ]
    out_shape = [
        pltpu.HBM(o.shape, o.dtype) if at in kept else jax.ShapeDtypeStruct(o.shape, o.dtype)
        for at, o in enumerate(outs)
    ]
    return pl.pallas_call(
        run,
        grid=(1,),
        out_shape=out_shape + [jax.ShapeDtypeStruct(o.shape, o.dtype) for o in passed],
        in_specs=[pl.BlockSpec(memory_space=pltpu.SMEM)] * smem
        + [whole(a) for a in args[smem:]]
        + [pl.BlockSpec(memory_space=pl.ANY)] * (n_after + n_pass),
        out_specs=[whole(o) for o in outs] + [pl.BlockSpec(memory_space=pl.ANY)] * n_pass,
        scratch_shapes=scratch,
        input_output_aliases={n_in + n_after + at: n_out + at for at in range(n_pass)},
        compiler_params=pltpu.CompilerParams(vmem_limit_bytes=vmem * MIB),
        cost_estimate=pl.CostEstimate(
            flops=1 if prompt else flops,
            bytes_accessed=1 if prompt else moved,
            transcendentals=0,
        ),
        name=name,
    )(*args, *after, *passed)


def columns_of(turned):
    filled = jnp.concatenate(
        [turned.astype(F32), jnp.zeros((8 - turned.shape[0], turned.shape[1]), F32)], axis=0
    )
    return filled.T.astype(jnp.int32)


def pack_kernel(first_ref, last_ref, out_ref):
    cols = last_ref.shape[1]
    for at in range(3):
        out_ref[:, at * cols : (at + 1) * cols] = first_ref[at]
    out_ref[:, 3 * cols :] = last_ref[...]


def struct(shape, dtype):
    return jax.ShapeDtypeStruct(shape, dtype)


def slots_kernel(capacity, routes_ref, grad_ref, slot_ref, out_ref):
    tokens = routes_ref.shape[1]
    slots = out_ref.shape[0]
    experts = slots // capacity
    routes = columns_of(routes_ref[...])
    first, second = routes[:, 0:1], routes[:, 1:2]
    lane = iota((tokens, experts), 1)
    one_first = (first == lane).astype(F32)
    one_second = (second == lane).astype(F32)
    member = (one_first + one_second).astype(BF16)
    below = (iota((tokens, tokens), 1) < iota((tokens, tokens), 0)).astype(F32).astype(BF16)
    earlier = dot(below, member)
    slot_first = first * capacity + jnp.sum(one_first * earlier, axis=1, keepdims=True).astype(
        jnp.int32
    )
    slot_second = second * capacity + jnp.sum(one_second * earlier, axis=1, keepdims=True).astype(
        jnp.int32
    )
    wide = iota((tokens, 128), 1)
    slot_ref[...] = jnp.where(wide == 0, slot_first, slot_second)
    places = iota((tokens, slots), 1)
    chosen = ((slot_first == places) | (slot_second == places)).astype(F32).astype(BF16)
    out_ref[...] = dot(chosen, grad_ref[...], TN).astype(BF16)


def bias_tiles(rel_ref, first_head, heads):
    column = iota((8, 256), 1)
    distance = (ROWS - column) & 255
    bucket = bucket_of(distance)
    tiles = []
    for head in range(heads):
        line = jnp.zeros((8, 256), F32)
        for b in range(BUCKETS):
            line = jnp.where(bucket == b, rel_ref[first_head + head, b], line)
        wide = jnp.broadcast_to(line[0:1, :], (ROWS, 256))
        tiles.append(pltpu.roll(wide, 0, 1, stride=1, stride_axis=0))
    return tiles


def masked_scores(query, keys, tile, far, second, block):
    width = (block + 1) * ROWS
    raw = dot(query, keys, NT) * HDIM**-0.5
    if block == 0:
        bias = tile[:, ROWS:]
    elif block == 1:
        bias = tile
    else:
        bias = jnp.concatenate([jnp.full((ROWS, width - 2 * ROWS), far, F32), tile], axis=1)
    column = iota((ROWS, width), 1)
    row = iota((ROWS, width), 0) + block * ROWS
    starts = jnp.where(row >= second, second, 0)
    allowed = (column <= row) & (column >= starts)
    return jnp.where(allowed, raw + bias, -1e9)


def forward_kernel(parts, pieces, heads, *refs):
    doc_ref, rel_ref = refs[:2]
    weights = refs[2 : 2 + parts]
    rows = refs[2 + parts : 2 + parts + pieces]
    gain_ref = refs[2 + parts + pieces]
    weight_out, row_out, proj_out, att_out, lse_out, keep_a, keep_b, send_out = refs[
        3 + parts + pieces :
    ]
    keep_out = (keep_a, keep_b)
    piece, mine_dp = lax.axis_index("tensor"), lax.axis_index("dp")
    second = doc_ref[doc_ref.shape[0] - 1]
    cols = heads * HDIM
    for at in range(parts):
        depth = weights[at].shape[0]
        start = (mine_dp ^ at) * depth if parts > 1 else 0
        weight_out[pl.ds(pl.multiple_of(start, 16), depth), :] = weights[at][...]
    for at in range(pieces):
        row_out[pl.ds(pl.multiple_of((piece ^ at) * ROWS, ROWS), ROWS), :] = rows[at][...]
    x = row_out[...].astype(F32)
    scale = lax.rsqrt(jnp.mean(x * x, axis=1, keepdims=True) + 1e-6)
    normed = (x * scale * gain_ref[...]).astype(BF16)
    proj_out[...] = dot(normed, weight_out[:, : 3 * cols]).astype(BF16)
    tiles = bias_tiles(rel_ref, piece * heads, heads)
    blocks = x.shape[0] // ROWS
    proj = proj_out[...]
    wide = iota((ROWS, 128), 1)
    for block in range(blocks):
        here = slice(block * ROWS, (block + 1) * ROWS)
        upto = slice(0, (block + 1) * ROWS)
        done = []
        kept = jnp.zeros((ROWS, 128), F32)
        for head in range(heads):
            at = head * HDIM
            query = proj[here, at : at + HDIM]
            keys = proj[upto, cols + at : cols + at + HDIM]
            values = proj[upto, 2 * cols + at : 2 * cols + at + HDIM]
            far = rel_ref[piece * heads + head, BUCKETS - 1]
            scores = masked_scores(query, keys, tiles[head], far, second, block)
            peak = jnp.max(scores, axis=1, keepdims=True)
            shifted = jnp.exp(scores - peak)
            total = jnp.sum(shifted, axis=1, keepdims=True)
            attention = (shifted * (1.0 / total)).astype(BF16)
            done.append(dot(attention, values).astype(BF16))
            kept = jnp.where(wide == head, peak + jnp.log(total), kept)
        att_out[here, :] = jnp.concatenate(done, axis=1)
        lse_out[here, :] = kept
    weight_last = weight_out[:, 3 * cols :]
    for at in range(pieces):
        mine = att_out[pl.ds(pl.multiple_of((piece ^ at) * ROWS, ROWS), ROWS), :]
        product = dot(mine, weight_last, NT)
        if at % 2 == 0:
            keep_out[at // 2][...] = product
        else:
            send_out[at // 2] = product.astype(BF16)


def dispatch_kernel(
    own_ref,
    part_ref,
    near_ref,
    far_ref,
    gain_ref,
    router_ref,
    routes_ref,
    slot_ref,
    mixed_ref,
    normed_ref,
    gates_ref,
    out_ref,
):
    width = own_ref.shape[1]
    tokens = own_ref.shape[0]
    slots = out_ref.shape[0]
    mixed = own_ref[...].astype(F32) + (
        part_ref[...] + near_ref[0].astype(F32) + far_ref[...].astype(F32)
    )
    mixed_ref[...] = mixed
    scale = lax.rsqrt(jnp.mean(mixed * mixed, axis=1, keepdims=True) + 1e-6)
    normed = (mixed * scale * gain_ref[...]).astype(BF16)
    normed_ref[...] = normed
    logits = dot(normed, router_ref[...], NT)
    routes = columns_of(routes_ref[...])
    lane = iota(logits.shape, 1)
    one = jnp.sum(jnp.where(routes[:, 0:1] == lane, logits, 0.0), axis=1, keepdims=True)
    two = jnp.sum(jnp.where(routes[:, 1:2] == lane, logits, 0.0), axis=1, keepdims=True)
    peak = jnp.maximum(one, two)
    one, two = jnp.exp(one - peak), jnp.exp(two - peak)
    total = one + two
    one, two = one / total, two / total
    wide = iota((tokens, 128), 1)
    gates_ref[...] = jnp.where(wide == 0, one, two)
    places = iota((tokens, slots), 1)
    slot = slot_ref[...]
    first = (slot[:, 0:1] == places).astype(F32).astype(BF16)
    second = (slot[:, 1:2] == places).astype(F32).astype(BF16)
    out_ref[:, :width] = dot(first + second, normed, TN).astype(BF16)
    gate_slots = dot(first, three_lanes(one), TN) + dot(second, three_lanes(two), TN)
    out_ref[:, width:] = gate_slots.astype(BF16)


def gelu_and_slope(x):
    inner = 0.7978845608028654 * (x + 0.044715 * (x * x * x))
    bend = jnp.tanh(inner)
    half = 0.5 * (1.0 + bend)
    slope = half + 0.5 * x * (1.0 - bend * bend) * (
        0.7978845608028654 * (1.0 + 3 * 0.044715 * (x * x))
    )
    return x * half, slope


def expert_side(source, pull, in_ref, out_ref, here, hidden_out, pre_out, total, fresh):
    width, hidden_units = in_ref.shape
    tile = 256
    slot_rows = source[:, :width]
    gate = lanes_sum(source[:, width:])
    pulls = pull[...]
    gate_sum = jnp.zeros((source.shape[0], 1), F32)
    for at in range(0, hidden_units, tile):
        there = slice(at, at + tile)
        weight = in_ref[:, there]
        pulled = dot(pulls, out_ref[there, :], NT)
        hidden, slope = gelu_and_slope(dot(slot_rows, weight))
        hidden = hidden.astype(BF16)
        pre_grad = (pulled * gate * slope).astype(BF16)
        hidden_out[here, there] = hidden
        if pre_out is not None:
            pre_out[here, there] = pre_grad
        product = dot(pre_grad, weight, NT)
        if fresh and at == 0:
            total[here, :] = product
        else:
            total[here, :] += product
        gate_sum += jnp.sum(hidden.astype(F32) * pulled, axis=1, keepdims=True)
    return gate_sum


def own_slice_kernel(
    own_ref, mate_ref, pull_own, pull_mate, in_ref, out_ref, hidden_ref, pre_ref, total_ref, sum_ref
):
    rows = own_ref.shape[0]
    for side, (source, pull) in enumerate(((own_ref, pull_own), (mate_ref, pull_mate))):
        here = slice(side * rows, (side + 1) * rows)
        gate_sum = expert_side(
            source, pull, in_ref, out_ref, here, hidden_ref, pre_ref, total_ref, True
        )
        sum_ref[here, :] = jnp.broadcast_to(gate_sum, (rows, GATE_LANES))


def far_slice_kernel(
    own_ref,
    mate_ref,
    pull_own,
    pull_mate,
    in_a_ref,
    in_b_ref,
    out_ref,
    total_ref,
    sum_ref,
    hidden_ref,
    keep_ref,
    send_ref,
    total,
    in_ref,
):
    rows = own_ref.shape[0]
    width, split = in_ref.shape[0], in_a_ref.shape[0]
    in_ref[:split, :] = in_a_ref[...]
    in_ref[split:, :] = in_b_ref[...]
    total[...] = total_ref[...]
    for side, (source, pull) in enumerate(((mate_ref, pull_mate), (own_ref, pull_own))):
        here = slice((1 - side) * rows, (2 - side) * rows)
        gate_sum = sum_ref[here, 0:1] + expert_side(
            source, pull, in_ref, out_ref, here, hidden_ref, None, total, False
        )
        if side == 0:
            send_ref[:, :width] = total[here, :].astype(BF16)
            send_ref[:, width:] = three_lanes(gate_sum)
        else:
            keep_ref[:, :width] = total[here, :]
            keep_ref[:, width:] = jnp.broadcast_to(gate_sum, (rows, GATE_LANES))


def weight_grad_kernel(
    own_ref,
    mate_ref,
    pull_own,
    pull_mate,
    far_ref,
    far_mate_ref,
    far_pull_own,
    far_pull_mate,
    in_one,
    out_one,
    hidden_one,
    pre_one,
    grad_in,
    grad_out,
    token_ref,
    rows_turned,
    pulls_all,
    hidden_far,
    pre_far,
):
    rows = own_ref.shape[0]
    width, hidden_units = in_one.shape
    tile = 256
    token_ref[...] = jnp.zeros_like(token_ref)
    for at, (source, pull) in enumerate(
        (
            (own_ref, pull_own),
            (mate_ref, pull_mate),
            (far_ref, far_pull_own),
            (far_mate_ref, far_pull_mate),
        )
    ):
        here = slice(at * rows, (at + 1) * rows)
        slot_rows = source[:, :width]
        rows_turned[:, here] = slot_rows.T
        gate = lanes_sum(source[:, width:])
        pulls_all[here, :] = (gate * pull[...].astype(F32)).astype(BF16)
        if at >= 2:
            back = slice((at - 2) * rows, (at - 1) * rows)
            for unit in range(0, hidden_units, tile):
                there = slice(unit, unit + tile)
                hidden, slope = gelu_and_slope(dot(slot_rows, in_one[:, there]))
                pulled = dot(pulls_all[here, :], out_one[there, :], NT)
                hidden_far[back, there] = hidden.astype(BF16)
                pre_far[back, there] = (pulled * slope).astype(BF16)
    for unit in range(0, hidden_units, tile):
        there = slice(unit, unit + tile)
        grad_in[:, there] = dot(rows_turned[:, : 2 * rows], pre_one[:, there]) + dot(
            rows_turned[:, 2 * rows :], pre_far[:, there]
        )
        grad_out[there, :] = dot(hidden_one[:, there], pulls_all[: 2 * rows, :], TN) + dot(
            hidden_far[:, there], pulls_all[2 * rows :, :], TN
        )


def expert_out_kernel(hidden_one, hidden_two, out_one, out_two, keep_ref, send_ref):
    rows = keep_ref.shape[0]
    product = dot(hidden_one[...], out_one[...]) + dot(hidden_two[...], out_two[...])
    keep_ref[...] = product[:rows]
    send_ref[...] = product[rows:].astype(BF16)


def merge_kernel(keep_ref, mate_ref, out_ref):
    width = keep_ref.shape[1] - GATE_LANES
    out_ref[:, :width] = (keep_ref[:, :width] + mate_ref[:, :width].astype(F32)).astype(BF16)
    gate = keep_ref[:, width : width + 1] + lanes_sum(mate_ref[:, width:])
    out_ref[:, width:] = three_lanes(gate)


def combine_kernel(
    back_ref,
    slot_ref,
    gates_ref,
    mixed_ref,
    normed_ref,
    router_ref,
    routes_ref,
    grad_ref,
    gain_ref,
    mixed_grad_ref,
    low_ref,
    sums_ref,
):
    tokens, width = grad_ref.shape
    slots = back_ref.shape[0]
    experts = router_ref.shape[0]
    places = iota((tokens, slots), 1)
    slot = slot_ref[...]
    first = (slot[:, 0:1] == places).astype(F32).astype(BF16)
    second = (slot[:, 1:2] == places).astype(F32).astype(BF16)
    lanes = back_ref[:, width:]
    pull_one = jnp.sum(dot(first, lanes), axis=1, keepdims=True)
    pull_two = jnp.sum(dot(second, lanes), axis=1, keepdims=True)
    one, two = gates_ref[:, 0:1], gates_ref[:, 1:2]
    mean_pull = one * pull_one + two * pull_two
    delta_one = one * (pull_one - mean_pull)
    delta_two = two * (pull_two - mean_pull)
    routes = columns_of(routes_ref[...])
    lane = iota((tokens, experts), 1)
    logit_grad = jnp.where(routes[:, 0:1] == lane, delta_one, 0.0) + jnp.where(
        routes[:, 1:2] == lane, delta_two, 0.0
    )
    high = logit_grad.astype(BF16)
    low = (logit_grad - high.astype(F32)).astype(BF16)
    normed = normed_ref[...]
    router = router_ref[...]
    normed_grad = dot(first + second, back_ref[:, :width]) + (
        dot(high, router) + dot(low, router)
    )
    mixed = mixed_ref[...]
    grad = grad_ref[...].astype(F32)
    scale = lax.rsqrt(jnp.mean(mixed * mixed, axis=1, keepdims=True) + 1e-6)
    scaled = normed_grad * gain_ref[...]
    cubed = scale * scale * scale
    mixed_grad = (
        grad
        + scale * scaled
        - mixed * cubed * jnp.mean(scaled * mixed, axis=1, keepdims=True)
    )
    mixed_grad_ref[...] = mixed_grad
    low_ref[...] = mixed_grad.astype(BF16)
    sums_ref[...] = jnp.zeros_like(sums_ref)
    sums_ref[:experts, :] = dot(high, normed, TN) + dot(low, normed, TN)
    sums_ref[experts : experts + 1, :] = jnp.sum(
        normed_grad * mixed * scale, axis=0, keepdims=True
    )


def result_kernel(back_ref, slot_ref, gates_ref, mixed_ref, out_ref):
    tokens = mixed_ref.shape[0]
    slots = back_ref.shape[0]
    places = iota((tokens, slots), 1)
    slot = slot_ref[...]
    first = (slot[:, 0:1] == places).astype(F32).astype(BF16)
    second = (slot[:, 1:2] == places).astype(F32).astype(BF16)
    back = back_ref[...]
    added = gates_ref[:, 0:1] * dot(first, back) + gates_ref[:, 1:2] * dot(second, back)
    out_ref[...] = (mixed_ref[...] + added).astype(BF16)


def backward_kernel(parts, pieces, heads, experts, *refs):
    doc_ref, rel_ref = refs[:2]
    lows = refs[2 : 2 + pieces]
    weight_ref, row_ref, proj_ref, att_ref, lse_ref, gain_ref, sums_ref = refs[
        2 + pieces : 9 + pieces
    ]
    outs = refs[9 + pieces :]
    n_grads = parts // 2 + 2 if parts > 1 else 1
    grad_outs = outs[:n_grads]
    keep_a, keep_b, send_out, sums_out, mixed, grad_proj, normed_grad = outs[n_grads : n_grads + 7]
    keep_out = (keep_a, keep_b)
    piece, mine_dp = lax.axis_index("tensor"), lax.axis_index("dp")
    second = doc_ref[doc_ref.shape[0] - 1]
    cols = heads * HDIM
    for at in range(pieces):
        mixed[pl.ds(pl.multiple_of((piece ^ at) * ROWS, ROWS), ROWS), :] = lows[at][...]
    weight_last = weight_ref[:, 3 * cols :]
    att_grad = dot(mixed[...], weight_last).astype(BF16)
    grad_last = dot(mixed[...], att_ref[...], TN)
    tiles = bias_tiles(rel_ref, piece * heads, heads)
    proj = proj_ref[...]
    length = proj.shape[0]
    blocks = length // ROWS
    flipped = (iota((ROWS, ROWS), 0) + iota((ROWS, ROWS), 1) == ROWS - 1).astype(F32).astype(BF16)
    line_bucket = bucket_of((ROWS - iota((256, HEADS * BUCKETS), 0)) & 255)
    target = iota((256, HEADS * BUCKETS), 1)
    target_row = iota((8, HEADS * BUCKETS), 1)
    bias_row = jnp.zeros((8, HEADS * BUCKETS), F32)
    grads_q, grads_k, grads_v = [], [], []
    for head in range(heads):
        at = head * HDIM
        far = rel_ref[piece * heads + head, BUCKETS - 1]
        key_sum = [jnp.zeros((ROWS, HDIM), F32) for _ in range(blocks)]
        value_sum = [jnp.zeros((ROWS, HDIM), F32) for _ in range(blocks)]
        near_sum = jnp.zeros((ROWS, 256), F32)
        far_sum = jnp.zeros((ROWS, ROWS), F32)
        query_done = []
        for block in range(blocks):
            here = slice(block * ROWS, (block + 1) * ROWS)
            upto = slice(0, (block + 1) * ROWS)
            query = proj[here, at : at + HDIM]
            keys = proj[upto, cols + at : cols + at + HDIM]
            values = proj[upto, 2 * cols + at : 2 * cols + at + HDIM]
            out_grad = att_grad[here, at : at + HDIM]
            scores = masked_scores(query, keys, tiles[head], far, second, block)
            again = jnp.exp(scores - lse_ref[here, head : head + 1])
            prob_grad = dot(out_grad, values, NT)
            weighted = again * prob_grad
            score_grad = weighted - again * jnp.sum(weighted, axis=1, keepdims=True)
            score_low = score_grad.astype(BF16)
            value_add = dot(again.astype(BF16), out_grad, TN)
            key_add = dot(score_low, query, TN)
            for other in range(block + 1):
                there = slice(other * ROWS, (other + 1) * ROWS)
                key_sum[other] = key_sum[other] + key_add[there, :]
                value_sum[other] = value_sum[other] + value_add[there, :]
                if other < block - 1:
                    far_sum = far_sum + score_grad[:, there]
            if block == 0:
                near_sum = near_sum + jnp.concatenate(
                    [jnp.zeros((ROWS, ROWS), F32), score_grad], axis=1
                )
            else:
                near_sum = near_sum + score_grad[:, (block - 1) * ROWS :]
            query_done.append(dot(score_low, keys) * HDIM**-0.5)
        grads_q.append(jnp.concatenate(query_done, axis=0))
        grads_k.append(jnp.concatenate(key_sum, axis=0) * HDIM**-0.5)
        grads_v.append(jnp.concatenate(value_sum, axis=0))
        first_lane = (piece * heads + head) * BUCKETS
        near_high = near_sum.astype(BF16)
        near_low = (near_sum - near_high.astype(F32)).astype(BF16)
        turned = dot(flipped, near_high) + dot(flipped, near_low)
        turned = pltpu.roll(turned, ROWS + 1, 1, stride=1, stride_axis=0)
        line = jnp.broadcast_to(jnp.sum(turned, axis=0, keepdims=True), (8, 256))
        spread = (line_bucket + first_lane == target).astype(F32)
        bias_row = bias_row + dot(line, spread, precision=HIGHEST)
        far_total = jnp.sum(jnp.sum(far_sum, axis=0, keepdims=True), axis=1, keepdims=True)
        bias_row = bias_row + jnp.where(
            target_row == first_lane + BUCKETS - 1, far_total, 0.0
        )
    grad_proj[...] = jnp.concatenate(grads_q + grads_k + grads_v, axis=1).astype(BF16)
    x = row_ref[...].astype(F32)
    scale = lax.rsqrt(jnp.mean(x * x, axis=1, keepdims=True) + 1e-6)
    unit = x * scale
    normed = (unit * gain_ref[...]).astype(BF16)
    grad_first = dot(normed, grad_proj[...], TN)
    if parts > 1:
        grads = outs[n_grads + 7]
        depth = grad_first.shape[0] // parts
        grads[:, : 3 * cols] = grad_first
        grads[:, 3 * cols :] = grad_last
        for at in range(parts):
            piece_rows = grads[pl.ds(pl.multiple_of((mine_dp ^ at) * depth, 16), depth), :]
            if at % 2 == 0:
                grad_outs[at // 2][...] = piece_rows
            else:
                at_send = parts // 2 + (0 if at > 4 else 1)
                grad_outs[at_send][0 if at % 4 == 3 else 1] = piece_rows.astype(BF16)
    else:
        grad_outs[0][:, : 3 * cols] = grad_first
        grad_outs[0][:, 3 * cols :] = grad_last
    normed_grad[...] = dot(grad_proj[...], weight_ref[:, : 3 * cols], NT)
    sums_out[...] = sums_ref[...]
    sums_out[experts + 1 : experts + 2, :] = jnp.sum(
        normed_grad[...] * unit, axis=0, keepdims=True
    )
    sums_out[experts + 2 : experts + 3, : HEADS * BUCKETS] = bias_row[0:1, :]
    for at in range(pieces):
        mine = normed_grad[pl.ds(pl.multiple_of((piece ^ at) * ROWS, ROWS), ROWS), :]
        if at % 2 == 0:
            keep_out[at // 2][...] = mine
        else:
            send_out[at // 2] = mine.astype(BF16)


def input_kernel(own_ref, gain_ref, mixed_grad_ref, part_ref, near_ref, far_ref, out_ref):
    x = own_ref[...].astype(F32)
    scale = lax.rsqrt(jnp.mean(x * x, axis=1, keepdims=True) + 1e-6)
    scaled = (
        part_ref[...] + near_ref[0].astype(F32) + far_ref[...].astype(F32)
    ) * gain_ref[...]
    cubed = scale * scale * scale
    own = scale * scaled - x * cubed * jnp.mean(scaled * x, axis=1, keepdims=True)
    out_ref[...] = (mixed_grad_ref[...] + own).astype(BF16)


def swap(value, axis, size, mask):
    return lax.ppermute(value, axis, [(i, i ^ mask) for i in range(size)])


def gather_weights(shard, senders):
    if senders != 8:
        return [lax.all_gather(shard, "dp", axis=0, tiled=True)]
    parts = {0: shard}
    parts[1] = swap(shard, "dp", senders, 1)
    for mask in (2, 4, 6):
        parts[mask] = swap(shard, "dp", senders, mask)
    for mask in (2, 4, 6):
        parts[mask + 1] = swap(parts[mask], "dp", senders, 1)
    return [parts[i] for i in range(senders)]


def fold_kernel(keep_ref, near_ref, out_ref):
    out_ref[...] = (keep_ref[...] + near_ref[...].astype(F32)).astype(BF16)


def fold(keep, near, name, after=()):
    return call(fold_kernel, [struct(near.shape, BF16)], [], [keep, near], name=name, after=after)[0]


def finish_kernel(cols, keep_ref, near_ref, one_ref, two_ref, three_ref, first_ref, last_ref):
    total = keep_ref[...] + near_ref[...].astype(F32)
    for part in (one_ref, two_ref, three_ref):
        total = total + part[...].astype(F32)
    for at in range(3):
        first_ref[at] = total[:, at * cols : (at + 1) * cols]
    last_ref[...] = total[:, 3 * cols :]


def fold_two_kernel(one_ref, two_ref, near_ref, one_out, two_out):
    one_out[...] = (one_ref[...] + near_ref[0].astype(F32)).astype(BF16)
    two_out[...] = (two_ref[...] + near_ref[1].astype(F32)).astype(BF16)


def finish_kernel(cols, keep_ref, near_ref, one_ref, two_ref, three_ref, first_ref, last_ref):
    total = keep_ref[...] + near_ref[1].astype(F32)
    for part in (one_ref, two_ref, three_ref):
        total = total + part[...].astype(F32)
    for at in range(3):
        first_ref[at] = total[:, at * cols : (at + 1) * cols]
    last_ref[...] = total[:, 3 * cols :]


def add_kernel(one_ref, two_ref, out_ref):
    out_ref[...] = one_ref[...] + two_ref[...]


def sums_kernel(experts, *refs):
    *parts, gains_ref, bias_ref, router_ref = refs
    total = parts[0][...]
    for part in parts[1:]:
        total = total + part[...]
    router_ref[...] = total[:experts]
    gains_ref[0:2, :] = total[experts : experts + 2]
    for head in range(HEADS):
        bias_ref[head : head + 1, :] = total[
            experts + 2 : experts + 3, head * BUCKETS : (head + 1) * BUCKETS
        ]


def add(one, two, after):
    return call(
        add_kernel, [struct(one.shape, F32)], [], [one, two], name="add_sums", after=after
    )[0]


def last_sums(grads, keep_a, keep_b, near, sums, senders, pieces, cols, experts):
    if senders != 8:
        part, near, far, _ = scatter_rows(keep_a, keep_b, near, pieces)
        total = lax.psum_scatter(grads[0], "dp", scatter_dimension=0, tiled=True)
        first = jnp.stack([total[:, at * cols : (at + 1) * cols] for at in range(3)])
        weight_sums = (first, total[:, 3 * cols :])
        sums = [lax.psum(sums, ("dp", "tensor"))]
    else:
        near_two = swap(grads[4], "dp", senders, 1)
        near_one = swap(grads[5], "dp", senders, 1)
        sums = add(sums, swap(sums, "tensor", pieces, 1), [near])
        got = swap(sums, "tensor", pieces, 2)
        other = call(
            lambda keep, got, out: fold_kernel(keep, got.at[1], out),
            [struct(keep_b.shape, BF16)],
            [],
            [keep_b, near],
            name="fold_rows",
            after=[sums],
        )[0]
        part, far = keep_a, swap(other, "tensor", pieces, 2)
        sums = add(sums, got, [other])
        got = swap(sums, "dp", senders, 1)
        six, four = call(
            fold_two_kernel,
            [struct(keep.shape, BF16) for keep in (grads[3], grads[2])],
            [],
            [grads[3], grads[2], near_two],
            name="fold_weights",
            after=[sums],
        )
        arrived = [swap(six, "dp", senders, 6), swap(four, "dp", senders, 4)]
        sums = add(sums, got, [six])
        two = call(
            lambda keep, got, out: fold_kernel(keep, got.at[0], out),
            [struct(grads[1].shape, BF16)],
            [],
            [grads[1], near_one],
            name="fold_weights",
            after=[sums],
        )[0]
        arrived.append(swap(two, "dp", senders, 2))
        sums = [sums] + [swap(sums, "dp", senders, mask) for mask in (6, 4, 2)]
        depth = grads[0].shape[0]
        weight_sums = call(
            functools.partial(finish_kernel, cols),
            [struct((3, depth, cols), F32), struct((depth, cols), F32)],
            [],
            [grads[0], near_one] + arrived,
            name="finish",
        )
    width = sums[0].shape[1]
    small = call(
        functools.partial(sums_kernel, experts),
        [
            struct((8, width), F32),
            struct((HEADS, BUCKETS), F32),
            struct((experts, width), F32),
        ],
        [],
        sums,
        name="sums",
    )
    return weight_sums, (part, near, far), small


def scatter_rows(keep_a, keep_b, near, pieces, after=()):
    other = call(
        lambda keep, got, out: fold_kernel(keep, got.at[1], out),
        [struct(keep_b.shape, BF16)],
        [],
        [keep_b, near],
        name="fold_rows",
        after=after,
    )[0]
    return keep_a, near, swap(other, "tensor", pieces, 2), other


def gather_rows(rows, pieces):
    far = swap(rows, "tensor", pieces, 2)
    near = swap(rows, "tensor", pieces, 1)
    last = swap(far, "tensor", pieces, 1)
    return [rows, near, far, last]


def exchange(blocks, senders, capacity):
    rows, width = blocks.shape
    return lax.all_to_all(
        blocks.reshape(senders, capacity, width), "dp", split_axis=0, concat_axis=0, tiled=True
    ).reshape(rows, width)


def body(
    tokens,
    doc_start,
    routes,
    gain_attn,
    w_qkv,
    w_out,
    rel_bias,
    gain_ffn,
    router,
    w_in,
    w_exp_out,
    out_grad,
):
    pieces = lax.axis_size("tensor")
    senders = lax.axis_size("dp")
    tok_dev, width = tokens.shape
    routes, rel_bias, router = routes.T, rel_bias.T, router.T
    length = tok_dev * pieces
    experts = router.shape[0]
    capacity = max(2, 3 * tok_dev * routes.shape[0] // (2 * experts))
    slots = experts * capacity
    heads = w_out.shape[1] // HDIM
    cols = heads * HDIM
    gain_one = gain_attn.reshape(1, width)
    gain_two = gain_ffn.reshape(1, width)

    (shard,) = call(
        pack_kernel,
        [struct((w_out.shape[0], 4 * cols), BF16)],
        [],
        [w_qkv.transpose(1, 0, 2), w_out],
        name="pack",
        held=(0, 1),
    )
    weights = gather_weights(shard, senders)
    rows = gather_rows(tokens, pieces)
    in_one, out_one = w_in[0], w_exp_out[0]
    out_two = swap(out_one, "tensor", pieces, 2)
    split = width // 3
    in_two_a = swap(in_one[:split], "tensor", pieces, 2)
    in_two_b = swap(in_one[split:], "tensor", pieces, 2)

    slot, grad_out = call(
        functools.partial(slots_kernel, capacity),
        [struct((tok_dev, 128), jnp.int32), struct((slots, width), BF16)],
        [],
        [routes, out_grad],
        flops=2 * slots * tok_dev * width,
        name="slots",
        kept=(0, 1),
    )

    (grad_out,) = call(
        lambda: None,
        [],
        [],
        [],
        name="gathered",
        after=weights[1::2],
        passed=[grad_out],
    )
    whole_weight, whole_rows, projected, attended, lse, keep_a, keep_b, send = call(
        functools.partial(forward_kernel, len(weights), pieces, heads),
        [
            struct((width, 4 * cols), BF16),
            struct((length, width), BF16),
            struct((length, 3 * cols), BF16),
            struct((length, cols), BF16),
            struct((length, 128), F32),
            struct((tok_dev, width), F32),
            struct((tok_dev, width), F32),
            struct((pieces // 2, tok_dev, width), BF16),
        ],
        [],
        [doc_start, rel_bias] + weights + rows + [gain_one],
        smem=2,
        flops=2 * length * width * 4 * cols + 4 * heads * length * length * HDIM,
        name="attend",
        held=tuple(range(2, 2 + len(weights))),
        kept=(0, 1, 2, 3, 4),
        vmem=12,
    )
    pull_own = exchange(grad_out, senders, capacity)
    pull_mate = swap(pull_own, "tensor", pieces, 1)
    far_pull_own = swap(pull_own, "tensor", pieces, 2)
    far_pull_mate = swap(far_pull_own, "tensor", pieces, 1)

    near = swap(send, "tensor", pieces, 1)
    part, near, far, _ = scatter_rows(keep_a, keep_b, near, pieces, [out_two, in_two_a])
    mixed, normed_two, gates, outgoing = call(
        dispatch_kernel,
        [
            struct((tok_dev, width), F32),
            struct((tok_dev, width), BF16),
            struct((tok_dev, 128), F32),
            struct((slots, width + GATE_LANES), BF16),
        ],
        [],
        [tokens, part, near, far, gain_two, router, routes, slot],
        flops=2 * slots * tok_dev * width,
        name="dispatch",
        after=[pull_own],
        kept=(0, 1, 2),
    )
    slot_own = exchange(outgoing, senders, capacity)
    slot_mate = swap(slot_own, "tensor", pieces, 1)
    payload = width + GATE_LANES
    units = in_one.shape[1]
    expert_flops = 12 * slots * width * units
    hidden_one, pre_one, row_total, gate_total = call(
        own_slice_kernel,
        [struct((2 * slots, units), BF16)] * 2
        + [struct((2 * slots, width), F32), struct((2 * slots, GATE_LANES), F32)],
        [],
        [slot_own, slot_mate, pull_own, pull_mate, in_one, out_one],
        flops=expert_flops,
        name="own_slice",
        prompt=True,
        held=(4, 5),
        kept=(0, 1),
        vmem=14,
    )
    hidden_two, row_keep, row_send = call(
        far_slice_kernel,
        [
            struct((2 * slots, units), BF16),
            struct((slots, payload), F32),
            struct((slots, payload), BF16),
        ],
        [pltpu.VMEM((2 * slots, width), F32), pltpu.VMEM((width, units), BF16)],
        [slot_own, slot_mate, pull_own, pull_mate, in_two_a, in_two_b, out_two, row_total, gate_total],
        flops=expert_flops,
        name="far_slice",
        prompt=True,
        after=[far_pull_own],
        held=(4, 5, 6),
        kept=(0,),
        vmem=14,
    )
    row_mate = swap(row_send, "tensor", pieces, 1)
    far_own = swap(slot_own, "tensor", pieces, 2)
    (row_out,) = call(
        merge_kernel,
        [struct((slots, payload), BF16)],
        [],
        [row_keep, row_mate],
        name="merge",
    )
    back = exchange(row_out, senders, capacity)

    far_mate = swap(far_own, "tensor", pieces, 1)
    out_keep, out_send = call(
        expert_out_kernel,
        [struct((slots, width), F32), struct((slots, width), BF16)],
        [],
        [hidden_one, hidden_two, out_one, out_two],
        flops=4 * 2 * slots * width * in_one.shape[1],
        name="expert_out",
        held=(0, 1, 2, 3),
        after=[far_own],
        vmem=10,
    )
    grad_in, grad_out_sum, graded = call(
        weight_grad_kernel,
        [struct(in_one.shape, F32), struct(out_one.shape, F32), struct((8, 128), F32)],
        [
            pltpu.VMEM((width, 4 * slots), BF16),
            pltpu.VMEM((4 * slots, width), BF16),
            pltpu.VMEM((2 * slots, in_one.shape[1]), BF16),
            pltpu.VMEM((2 * slots, in_one.shape[1]), BF16),
        ],
        [
            slot_own,
            slot_mate,
            pull_own,
            pull_mate,
            far_own,
            far_mate,
            far_pull_own,
            far_pull_mate,
            in_one,
            out_one,
            hidden_one,
            pre_one,
        ],
        flops=24 * slots * width * in_one.shape[1],
        name="weight_grads",
        held=tuple(range(12)),
        after=[out_send],
        vmem=26,
    )

    sum_rows = -(-(experts + 3) // 8) * 8
    mixed_grad, mixed_low, sums_two = call(
        combine_kernel,
        [
            struct((tok_dev, width), F32),
            struct((tok_dev, width), BF16),
            struct((sum_rows, width), F32),
        ],
        [],
        [back, slot, gates, mixed, normed_two, router, routes, out_grad, gain_two],
        flops=2 * slots * tok_dev * width,
        name="combine",
        after=[graded],
        held=(1, 2, 3, 4, 7),
    )
    expert_out = fold(out_keep, swap(out_send, "tensor", pieces, 1), "fold_out", [mixed_low])
    returned = exchange(expert_out, senders, capacity)
    (result,) = call(
        result_kernel,
        [struct((tok_dev, width), BF16)],
        [],
        [returned, slot, gates, mixed],
        flops=4 * slots * tok_dev * width,
        name="result",
        held=(1, 2, 3),
    )

    lows = gather_rows(mixed_low, pieces)
    parts = len(weights)
    if parts > 1:
        depth = width // parts
        grad_shapes = [struct((depth, 4 * cols), F32)] * (parts // 2)
        grad_shapes += [struct((2, depth, 4 * cols), BF16)] * 2
        grad_scratch = [pltpu.VMEM((width, 4 * cols), F32)]
    else:
        grad_shapes = [struct((width, 4 * cols), F32)]
        grad_scratch = []
    *weight_grads, keep_a, keep_b, send, sums = call(
        functools.partial(backward_kernel, parts, pieces, heads, experts),
        grad_shapes
        + [
            struct((tok_dev, width), F32),
            struct((tok_dev, width), F32),
            struct((pieces // 2, tok_dev, width), BF16),
            struct((sum_rows, width), F32),
        ],
        [
            pltpu.VMEM((length, width), BF16),
            pltpu.VMEM((length, 3 * cols), BF16),
            pltpu.VMEM((length, width), F32),
        ]
        + grad_scratch,
        [doc_start, rel_bias]
        + lows
        + [whole_weight, whole_rows, projected, attended, lse, gain_one, sums_two],
        smem=2,
        name="attend_back",
        prompt=True,
        held=tuple(range(2 + pieces, 7 + pieces)),
        vmem=16,
    )
    near = swap(send, "tensor", pieces, 1)
    (first_sum, last_sum), (part, near, far), (gains, bias_grad, router_grad) = last_sums(
        weight_grads, keep_a, keep_b, near, sums, senders, pieces, cols, experts
    )
    (input_grad,) = call(
        input_kernel,
        [struct((tok_dev, width), BF16)],
        [],
        [tokens, gain_one, mixed_grad, part, near, far],
        name="input_grad",
        held=(0, 2),
    )
    return (
        result,
        input_grad,
        gains[1],
        first_sum.transpose(1, 0, 2),
        last_sum,
        bias_grad.T,
        gains[0],
        router_grad.T,
        grad_in[None],
        grad_out_sum[None],
    )


def solution(mesh):
    in_specs = (
        P(("dp", "tensor"), None),
        P("dp"),
        P(("dp", "tensor"), None),
        P(),
        P("dp", None, "tensor"),
        P("dp", "tensor"),
        P(),
        P(),
        P(),
        P("dp", None, "tensor"),
        P("dp", "tensor", None),
        P(("dp", "tensor"), None),
    )
    out_specs = (
        P(("dp", "tensor"), None),
        P(("dp", "tensor"), None),
        P(),
        P("dp", None, "tensor"),
        P("dp", "tensor"),
        P(),
        P(),
        P(),
        P("dp", None, "tensor"),
        P("dp", "tensor", None),
    )
    return jax.shard_map(body, mesh=mesh, in_specs=in_specs, out_specs=out_specs, check_vma=False)
```

```python
import functools

import jax
import jax.numpy as jnp
import numpy as np
from jax import lax
from jax.experimental import pallas as pl
from jax.experimental.pallas import tpu as pltpu
from jax.sharding import PartitionSpec as P

HEADS = 12
HDIM = 64
BUCKETS = 32
ROWS = 128
BLOCK = 256
GATE_LANES = 128

LIMITS = np.array([19, 21, 24, 27, 31, 35, 40, 46, 52, 59, 67, 77, 87, 99, 113], np.int32)
HIGHEST = lax.Precision.HIGHEST
F32 = jnp.float32
BF16 = jnp.bfloat16
MIB = 1024 * 1024

NN = (((1,), (0,)), ((), ()))
NT = (((1,), (1,)), ((), ()))
TN = (((0,), (0,)), ((), ()))


def dot(left, right, dims=NN, precision=None):
    return lax.dot_general(left, right, dims, preferred_element_type=F32, precision=precision)


def iota(shape, axis):
    return lax.broadcasted_iota(jnp.int32, shape, axis)


def bucket_of(distance):
    bucket = jnp.minimum(distance, 16)
    for limit in LIMITS:
        bucket = bucket + (distance >= int(limit)).astype(jnp.int32)
    return bucket


def in_three(value):
    high = value.astype(BF16)
    rest = value - high.astype(F32)
    middle = rest.astype(BF16)
    low = (rest - middle.astype(F32)).astype(BF16)
    return high, middle, low


def three_lanes(value):
    high, middle, low = in_three(value)
    lane = iota((value.shape[0], GATE_LANES), 1)
    zero = jnp.zeros((value.shape[0], GATE_LANES), F32)
    spread = jnp.where(
        lane == 0,
        high.astype(F32),
        jnp.where(lane == 1, middle.astype(F32), jnp.where(lane == 2, low.astype(F32), zero)),
    )
    return spread.astype(BF16)


def lanes_sum(lanes):
    return jnp.sum(lanes.astype(F32), axis=1, keepdims=True)


def pick(columns, at):
    return columns[:, at : at + 1]


def call(
    kernel,
    outs,
    scratch,
    args,
    smem=0,
    flops=0,
    name=None,
    after=(),
    vmem=6,
    held=(),
    kept=(),
    passed=(),
    prompt=False,
    parts={},
):
    n_in, n_after, n_out = len(args), len(after), len(outs)
    n_pass = len(passed)

    def run(*refs):
        ins, rest = refs[:n_in], refs[n_in + n_after + n_pass :]
        kernel(*ins, *rest[:n_out], *rest[n_out + n_pass :])

    def whole(a):
        shape = getattr(a, "shape", a)
        return pl.BlockSpec(shape, lambda i: (0,) * len(shape))

    moved = sum(a.size * a.dtype.itemsize for a in list(args) + list(outs))
    args = [
        pltpu.with_memory_space_constraint(a, pltpu.HBM) if at in held else a
        for at, a in enumerate(args)
    ]
    after = [
        pltpu.with_memory_space_constraint(a, pltpu.HBM) if a.size > 1 << 18 else a for a in after
    ]
    out_shape = [
        pltpu.HBM(o.shape, o.dtype) if at in kept else jax.ShapeDtypeStruct(o.shape, o.dtype)
        for at, o in enumerate(outs)
    ]
    return pl.pallas_call(
        run,
        grid=(1,),
        out_shape=out_shape + [jax.ShapeDtypeStruct(o.shape, o.dtype) for o in passed],
        in_specs=[pl.BlockSpec(memory_space=pltpu.SMEM)] * smem
        + [whole(parts.get(smem + at, a)) for at, a in enumerate(args[smem:])]
        + [pl.BlockSpec(memory_space=pl.ANY)] * (n_after + n_pass),
        out_specs=[whole(o) for o in outs] + [pl.BlockSpec(memory_space=pl.ANY)] * n_pass,
        scratch_shapes=scratch,
        input_output_aliases={n_in + n_after + at: n_out + at for at in range(n_pass)},
        compiler_params=pltpu.CompilerParams(vmem_limit_bytes=vmem * MIB),
        cost_estimate=pl.CostEstimate(
            flops=1 if prompt else flops,
            bytes_accessed=1 if prompt else moved,
            transcendentals=0,
        ),
        name=name,
    )(*args, *after, *passed)


def once(value, after, name):
    return call(lambda: None, [], [], [], name=name, after=after, passed=[value])[0]


def columns_of(turned):
    filled = jnp.concatenate(
        [turned.astype(F32), jnp.zeros((8 - turned.shape[0], turned.shape[1]), F32)], axis=0
    )
    return filled.T.astype(jnp.int32)


def pack_kernel(first_ref, last_ref, in_ref, out_ref, head_ref):
    head_ref[...] = in_ref[...]
    cols = last_ref.shape[1]
    for at in range(3):
        out_ref[:, at * cols : (at + 1) * cols] = first_ref[at]
    out_ref[:, 3 * cols :] = last_ref[...]


def struct(shape, dtype):
    return jax.ShapeDtypeStruct(shape, dtype)


def slots_kernel(capacity, routes_ref, grad_ref, slot_ref, out_ref):
    tokens = routes_ref.shape[1]
    slots = out_ref.shape[0]
    experts = slots // capacity
    routes = columns_of(routes_ref[...])
    first, second = routes[:, 0:1], routes[:, 1:2]
    lane = iota((tokens, experts), 1)
    one_first = (first == lane).astype(F32)
    one_second = (second == lane).astype(F32)
    member = (one_first + one_second).astype(BF16)
    below = (iota((tokens, tokens), 1) < iota((tokens, tokens), 0)).astype(F32).astype(BF16)
    earlier = dot(below, member)
    slot_first = first * capacity + jnp.sum(one_first * earlier, axis=1, keepdims=True).astype(
        jnp.int32
    )
    slot_second = second * capacity + jnp.sum(one_second * earlier, axis=1, keepdims=True).astype(
        jnp.int32
    )
    wide = iota((tokens, 128), 1)
    slot_ref[...] = jnp.where(wide == 0, slot_first, slot_second)
    places = iota((tokens, slots), 1)
    chosen = ((slot_first == places) | (slot_second == places)).astype(F32).astype(BF16)
    out_ref[...] = dot(chosen, grad_ref[...], TN).astype(BF16)


def bias_tiles(rel_ref, first_head, heads):
    wide = 2 * BLOCK
    distance = (BLOCK - iota((8, wide), 1)) & (wide - 1)
    bucket = bucket_of(distance)
    tiles = []
    for head in range(heads):
        line = jnp.zeros((8, wide), F32)
        for b in range(BUCKETS):
            line = jnp.where(bucket == b, rel_ref[first_head + head, b], line)
        grid = jnp.broadcast_to(line[0:1, :], (BLOCK, wide))
        tiles.append(pltpu.roll(grid, 0, 1, stride=1, stride_axis=0))
    return tiles


def masked_scores(query, keys, tile, second, block):
    width = (block + 1) * BLOCK
    raw = dot(query, keys, NT) * HDIM**-0.5
    bias = tile[:, 2 * BLOCK - width :]
    column = iota((BLOCK, width), 1)
    row = iota((BLOCK, width), 0) + block * BLOCK
    starts = jnp.where(row >= second, second, 0)
    allowed = (column <= row) & (column >= starts)
    return jnp.where(allowed, raw + bias, -1e9)


def forward_kernel(parts, pieces, heads, *refs):
    doc_ref, rel_ref = refs[:2]
    weights = refs[2 : 2 + parts]
    rows = refs[2 + parts : 2 + parts + pieces]
    gain_ref = refs[2 + parts + pieces]
    weight_out, row_out, proj_out, att_out, lse_out, keep_a, keep_b, send_out = refs[
        3 + parts + pieces :
    ]
    keep_out = (keep_a, keep_b)
    piece, mine_dp = lax.axis_index("tensor"), lax.axis_index("dp")
    second = doc_ref[doc_ref.shape[0] - 1]
    cols = heads * HDIM
    for at in range(parts):
        depth = weights[at].shape[0]
        start = (mine_dp ^ at) * depth if parts > 1 else 0
        weight_out[pl.ds(pl.multiple_of(start, 16), depth), :] = weights[at][...]
    for at in range(pieces):
        row_out[pl.ds(pl.multiple_of((piece ^ at) * ROWS, ROWS), ROWS), :] = rows[at][...]
    x = row_out[...].astype(F32)
    scale = lax.rsqrt(jnp.mean(x * x, axis=1, keepdims=True) + 1e-6)
    normed = (x * scale * gain_ref[...]).astype(BF16)
    proj_out[...] = dot(normed, weight_out[:, : 3 * cols]).astype(BF16)
    tiles = bias_tiles(rel_ref, piece * heads, heads)
    blocks = x.shape[0] // BLOCK
    proj = proj_out[...]
    wide = iota((BLOCK, 128), 1)
    for block in range(blocks):
        here = slice(block * BLOCK, (block + 1) * BLOCK)
        upto = slice(0, (block + 1) * BLOCK)
        done = []
        kept = jnp.zeros((BLOCK, 128), F32)
        for head in range(heads):
            at = head * HDIM
            query = proj[here, at : at + HDIM]
            keys = proj[upto, cols + at : cols + at + HDIM]
            values = proj[upto, 2 * cols + at : 2 * cols + at + HDIM]
            scores = masked_scores(query, keys, tiles[head], second, block)
            peak = jnp.max(scores, axis=1, keepdims=True)
            shifted = jnp.exp(scores - peak)
            total = jnp.sum(shifted, axis=1, keepdims=True)
            attention = (shifted * (1.0 / total)).astype(BF16)
            done.append(dot(attention, values).astype(BF16))
            kept = jnp.where(wide == head, peak + jnp.log(total), kept)
        att_out[here, :] = jnp.concatenate(done, axis=1)
        lse_out[here, :] = kept
    weight_last = weight_out[:, 3 * cols :]
    for at in range(pieces):
        mine = att_out[pl.ds(pl.multiple_of((piece ^ at) * ROWS, ROWS), ROWS), :]
        product = dot(mine, weight_last, NT)
        if at % 2 == 0:
            keep_out[at // 2][...] = product
        else:
            send_out[at // 2] = product.astype(BF16)


def dispatch_kernel(
    own_ref,
    part_ref,
    near_ref,
    far_ref,
    gain_ref,
    router_ref,
    routes_ref,
    slot_ref,
    mixed_ref,
    normed_ref,
    gates_ref,
    out_ref,
):
    width = own_ref.shape[1]
    tokens = own_ref.shape[0]
    slots = out_ref.shape[0]
    mixed = own_ref[...].astype(F32) + (
        part_ref[...] + near_ref[0].astype(F32) + far_ref[...].astype(F32)
    )
    mixed_ref[...] = mixed
    scale = lax.rsqrt(jnp.mean(mixed * mixed, axis=1, keepdims=True) + 1e-6)
    normed = (mixed * scale * gain_ref[...]).astype(BF16)
    normed_ref[...] = normed
    logits = dot(normed, router_ref[...], NT)
    routes = columns_of(routes_ref[...])
    lane = iota(logits.shape, 1)
    one = jnp.sum(jnp.where(routes[:, 0:1] == lane, logits, 0.0), axis=1, keepdims=True)
    two = jnp.sum(jnp.where(routes[:, 1:2] == lane, logits, 0.0), axis=1, keepdims=True)
    peak = jnp.maximum(one, two)
    one, two = jnp.exp(one - peak), jnp.exp(two - peak)
    total = one + two
    one, two = one / total, two / total
    wide = iota((tokens, 128), 1)
    gates_ref[...] = jnp.where(wide == 0, one, two)
    places = iota((tokens, slots), 1)
    slot = slot_ref[...]
    first = (slot[:, 0:1] == places).astype(F32).astype(BF16)
    second = (slot[:, 1:2] == places).astype(F32).astype(BF16)
    out_ref[:, :width] = dot(first + second, normed, TN).astype(BF16)
    gate_slots = dot(first, three_lanes(one), TN) + dot(second, three_lanes(two), TN)
    out_ref[:, width:] = gate_slots.astype(BF16)


def gelu_and_slope(x):
    inner = 0.7978845608028654 * (x + 0.044715 * (x * x * x))
    bend = jnp.tanh(inner)
    half = 0.5 * (1.0 + bend)
    slope = half + 0.5 * x * (1.0 - bend * bend) * (
        0.7978845608028654 * (1.0 + 3 * 0.044715 * (x * x))
    )
    return x * half, slope


def gather_sides(sources, pulls, rows_all, pulls_all):
    rows, width = pulls[0].shape
    gates = []
    for at, (source, pull) in enumerate(zip(sources, pulls)):
        here = slice(at * rows, (at + 1) * rows)
        rows_all[here, :] = source[:, :width]
        pulls_all[here, :] = pull[...]
        gates.append(lanes_sum(source[:, width:]))
    return jnp.concatenate(gates, axis=0)


def through_slice(rows_all, pulls_all, gate, in_ref, out_ref, hidden_out, pre_out):
    hidden_units = in_ref.shape[1]
    tile = 256
    gate_wide = jnp.zeros((rows_all.shape[0], tile), F32)
    for at in range(0, hidden_units, tile):
        there = slice(at, at + tile)
        pulled = dot(pulls_all[...], out_ref[there, :], NT)
        hidden, slope = gelu_and_slope(dot(rows_all[...], in_ref[:, there]))
        hidden = hidden.astype(BF16)
        hidden_out[:, there] = hidden
        pre_out[:, there] = (pulled * gate * slope).astype(BF16)
        gate_wide = gate_wide + hidden.astype(F32) * pulled
    return jnp.sum(gate_wide, axis=1, keepdims=True)


def own_slice_kernel(
    own_ref,
    mate_ref,
    pull_own,
    pull_mate,
    in_ref,
    out_ref,
    hidden_ref,
    pre_ref,
    total_ref,
    sum_ref,
    rows_all,
    pulls_all,
):
    gate = gather_sides((own_ref, mate_ref), (pull_own, pull_mate), rows_all, pulls_all)
    gate_sum = through_slice(rows_all, pulls_all, gate, in_ref, out_ref, hidden_ref, pre_ref)
    sum_ref[...] = jnp.broadcast_to(gate_sum, sum_ref.shape)
    total_ref[...] = dot(pre_ref[...], in_ref[...], NT)


def far_slice_kernel(
    own_ref,
    mate_ref,
    pull_own,
    pull_mate,
    in_a_ref,
    in_b_ref,
    out_ref,
    total_ref,
    sum_ref,
    hidden_ref,
    keep_ref,
    send_ref,
    in_ref,
    pre_ref,
    rows_all,
    pulls_all,
):
    rows, width = pull_own.shape
    split = in_a_ref.shape[0]
    in_ref[:split, :] = in_a_ref[...]
    in_ref[split:, :] = in_b_ref[...]
    gate = gather_sides((own_ref, mate_ref), (pull_own, pull_mate), rows_all, pulls_all)
    gate_sum = sum_ref[:, 0:1] + through_slice(
        rows_all, pulls_all, gate, in_ref, out_ref, hidden_ref, pre_ref
    )
    total = total_ref[...] + dot(pre_ref[...], in_ref[...], NT)
    keep_ref[:, :width] = total[:rows, :]
    keep_ref[:, width:] = jnp.broadcast_to(gate_sum[:rows], (rows, GATE_LANES))
    send_ref[:, :width] = total[rows:, :].astype(BF16)
    send_ref[:, width:] = three_lanes(gate_sum[rows:])


def weight_grad_kernel(
    own_ref,
    mate_ref,
    pull_own,
    pull_mate,
    far_ref,
    far_mate_ref,
    far_pull_own,
    far_pull_mate,
    in_one,
    out_one,
    hidden_one,
    pre_one,
    grad_in,
    grad_out,
    token_ref,
    rows_turned,
    pulls_all,
    hidden_far,
    pre_far,
):
    rows = own_ref.shape[0]
    width, hidden_units = in_one.shape
    tile = 256
    token_ref[...] = jnp.zeros_like(token_ref)
    for at, (source, pull) in enumerate(
        (
            (own_ref, pull_own),
            (mate_ref, pull_mate),
            (far_ref, far_pull_own),
            (far_mate_ref, far_pull_mate),
        )
    ):
        here = slice(at * rows, (at + 1) * rows)
        slot_rows = source[:, :width]
        rows_turned[:, here] = slot_rows.T
        gate = lanes_sum(source[:, width:])
        pulls_all[here, :] = (gate * pull[...].astype(F32)).astype(BF16)
        if at >= 2:
            back = slice((at - 2) * rows, (at - 1) * rows)
            for unit in range(0, hidden_units, tile):
                there = slice(unit, unit + tile)
                hidden, slope = gelu_and_slope(dot(slot_rows, in_one[:, there]))
                pulled = dot(pulls_all[here, :], out_one[there, :], NT)
                hidden_far[back, there] = hidden.astype(BF16)
                pre_far[back, there] = (pulled * slope).astype(BF16)
    for unit in range(0, hidden_units, tile):
        there = slice(unit, unit + tile)
        grad_in[:, there] = dot(rows_turned[:, : 2 * rows], pre_one[:, there]) + dot(
            rows_turned[:, 2 * rows :], pre_far[:, there]
        )
        grad_out[there, :] = dot(hidden_one[:, there], pulls_all[: 2 * rows, :], TN) + dot(
            hidden_far[:, there], pulls_all[2 * rows :, :], TN
        )


def expert_out_kernel(hidden_one, hidden_two, out_one, out_two, keep_ref, send_ref):
    rows = keep_ref.shape[0]
    product = dot(hidden_one[...], out_one[...]) + dot(hidden_two[...], out_two[...])
    keep_ref[...] = product[:rows]
    send_ref[...] = product[rows:].astype(BF16)


def merge_kernel(keep_ref, mate_ref, out_ref):
    width = keep_ref.shape[1] - GATE_LANES
    out_ref[:, :width] = (keep_ref[:, :width] + mate_ref[:, :width].astype(F32)).astype(BF16)
    gate = keep_ref[:, width : width + 1] + lanes_sum(mate_ref[:, width:])
    out_ref[:, width:] = three_lanes(gate)


def combine_kernel(
    back_ref,
    slot_ref,
    gates_ref,
    mixed_ref,
    normed_ref,
    router_ref,
    routes_ref,
    grad_ref,
    gain_ref,
    mixed_grad_ref,
    low_ref,
    sums_ref,
):
    tokens, width = grad_ref.shape
    slots = back_ref.shape[0]
    experts = router_ref.shape[0]
    places = iota((tokens, slots), 1)
    slot = slot_ref[...]
    first = (slot[:, 0:1] == places).astype(F32).astype(BF16)
    second = (slot[:, 1:2] == places).astype(F32).astype(BF16)
    lanes = back_ref[:, width:]
    pull_one = jnp.sum(dot(first, lanes), axis=1, keepdims=True)
    pull_two = jnp.sum(dot(second, lanes), axis=1, keepdims=True)
    one, two = gates_ref[:, 0:1], gates_ref[:, 1:2]
    mean_pull = one * pull_one + two * pull_two
    delta_one = one * (pull_one - mean_pull)
    delta_two = two * (pull_two - mean_pull)
    routes = columns_of(routes_ref[...])
    lane = iota((tokens, experts), 1)
    logit_grad = jnp.where(routes[:, 0:1] == lane, delta_one, 0.0) + jnp.where(
        routes[:, 1:2] == lane, delta_two, 0.0
    )
    high = logit_grad.astype(BF16)
    low = (logit_grad - high.astype(F32)).astype(BF16)
    normed = normed_ref[...]
    router = router_ref[...]
    normed_grad = dot(first + second, back_ref[:, :width]) + (
        dot(high, router) + dot(low, router)
    )
    mixed = mixed_ref[...]
    grad = grad_ref[...].astype(F32)
    scale = lax.rsqrt(jnp.mean(mixed * mixed, axis=1, keepdims=True) + 1e-6)
    scaled = normed_grad * gain_ref[...]
    cubed = scale * scale * scale
    mixed_grad = (
        grad
        + scale * scaled
        - mixed * cubed * jnp.mean(scaled * mixed, axis=1, keepdims=True)
    )
    mixed_grad_ref[...] = mixed_grad
    low_ref[...] = mixed_grad.astype(BF16)
    sums_ref[...] = jnp.zeros_like(sums_ref)
    sums_ref[:experts, :] = dot(high, normed, TN) + dot(low, normed, TN)
    sums_ref[experts : experts + 1, :] = jnp.sum(
        normed_grad * mixed * scale, axis=0, keepdims=True
    )


def result_kernel(back_ref, slot_ref, gates_ref, mixed_ref, out_ref):
    tokens = mixed_ref.shape[0]
    slots = back_ref.shape[0]
    places = iota((tokens, slots), 1)
    slot = slot_ref[...]
    first = (slot[:, 0:1] == places).astype(F32).astype(BF16)
    second = (slot[:, 1:2] == places).astype(F32).astype(BF16)
    back = back_ref[...]
    added = gates_ref[:, 0:1] * dot(first, back) + gates_ref[:, 1:2] * dot(second, back)
    out_ref[...] = (mixed_ref[...] + added).astype(BF16)


def backward_kernel(parts, pieces, heads, experts, *refs):
    doc_ref, rel_ref = refs[:2]
    lows = refs[2 : 2 + pieces]
    weight_ref, row_ref, proj_ref, att_ref, lse_ref, gain_ref, sums_ref = refs[
        2 + pieces : 9 + pieces
    ]
    outs = refs[9 + pieces :]
    n_grads = parts // 2 + 2 if parts > 1 else 1
    grad_outs = outs[:n_grads]
    keep_a, keep_b, send_out, sums_out, mixed, grad_proj, normed_grad = outs[n_grads : n_grads + 7]
    keep_out = (keep_a, keep_b)
    piece, mine_dp = lax.axis_index("tensor"), lax.axis_index("dp")
    second = doc_ref[doc_ref.shape[0] - 1]
    cols = heads * HDIM
    for at in range(pieces):
        mixed[pl.ds(pl.multiple_of((piece ^ at) * ROWS, ROWS), ROWS), :] = lows[at][...]
    weight_last = weight_ref[:, 3 * cols :]
    att_grad = dot(mixed[...], weight_last).astype(BF16)
    grad_last = dot(mixed[...], att_ref[...], TN)
    tiles = bias_tiles(rel_ref, piece * heads, heads)
    proj = proj_ref[...]
    length = proj.shape[0]
    blocks = length // BLOCK
    flipped = iota((BLOCK, BLOCK), 0) + iota((BLOCK, BLOCK), 1) == BLOCK - 1
    flipped = flipped.astype(F32).astype(BF16)
    wide = 2 * BLOCK
    lines = []
    grads_q, grads_k, grads_v = [], [], []
    for head in range(heads):
        at = head * HDIM
        key_sum = [jnp.zeros((BLOCK, HDIM), F32) for _ in range(blocks)]
        value_sum = [jnp.zeros((BLOCK, HDIM), F32) for _ in range(blocks)]
        near_sum = None
        query_done = []
        for block in reversed(range(blocks)):
            here = slice(block * BLOCK, (block + 1) * BLOCK)
            upto = slice(0, (block + 1) * BLOCK)
            query = proj[here, at : at + HDIM]
            keys = proj[upto, cols + at : cols + at + HDIM]
            values = proj[upto, 2 * cols + at : 2 * cols + at + HDIM]
            out_grad = att_grad[here, at : at + HDIM]
            scores = masked_scores(query, keys, tiles[head], second, block)
            again = jnp.exp(scores - lse_ref[here, head : head + 1])
            prob_grad = dot(out_grad, values, NT)
            weighted = again * prob_grad
            score_grad = weighted - again * jnp.sum(weighted, axis=1, keepdims=True)
            score_low = score_grad.astype(BF16)
            value_add = dot(again.astype(BF16), out_grad, TN)
            key_add = dot(score_low, query, TN)
            for other in range(block + 1):
                there = slice(other * BLOCK, (other + 1) * BLOCK)
                key_sum[other] = key_sum[other] + key_add[there, :]
                value_sum[other] = value_sum[other] + value_add[there, :]
            if block == 1:
                near_sum = score_grad
            else:
                near_sum = jnp.concatenate(
                    [near_sum[:, :BLOCK], near_sum[:, BLOCK:] + score_grad], axis=1
                )
            query_done.insert(0, dot(score_low, keys) * HDIM**-0.5)
        grads_q.append(jnp.concatenate(query_done, axis=0))
        grads_k.append(jnp.concatenate(key_sum, axis=0) * HDIM**-0.5)
        grads_v.append(jnp.concatenate(value_sum, axis=0))
        near_high = near_sum.astype(BF16)
        near_low = (near_sum - near_high.astype(F32)).astype(BF16)
        turned = dot(flipped, near_high) + dot(flipped, near_low)
        turned = pltpu.roll(turned, BLOCK + 1, 1, stride=1, stride_axis=0)
        lines.append(jnp.sum(turned, axis=0, keepdims=True))
    lines = jnp.concatenate(lines + [jnp.zeros((8 - heads, wide), F32)], axis=0)
    line_bucket = bucket_of((BLOCK - iota((wide, 128), 0)) & (wide - 1))
    spread = (line_bucket == iota((wide, 128), 1)).astype(F32)
    by_bucket = jnp.concatenate(
        [dot(lines, spread, precision=HIGHEST), jnp.zeros((8, HEADS * BUCKETS - 128), F32)], axis=1
    )
    bias_row = jnp.zeros((1, HEADS * BUCKETS), F32)
    for head in range(heads):
        placed = pltpu.roll(by_bucket, (piece * heads + head) * BUCKETS, 1)
        bias_row = bias_row + placed[head : head + 1, :]
    grad_proj[...] = jnp.concatenate(grads_q + grads_k + grads_v, axis=1).astype(BF16)
    x = row_ref[...].astype(F32)
    scale = lax.rsqrt(jnp.mean(x * x, axis=1, keepdims=True) + 1e-6)
    unit = x * scale
    normed = (unit * gain_ref[...]).astype(BF16)
    grad_first = dot(normed, grad_proj[...], TN)
    if parts > 1:
        grads = outs[n_grads + 7]
        depth = grad_first.shape[0] // parts
        grads[:, : 3 * cols] = grad_first
        grads[:, 3 * cols :] = grad_last
        for at in range(parts):
            piece_rows = grads[pl.ds(pl.multiple_of((mine_dp ^ at) * depth, 16), depth), :]
            if at % 2 == 0:
                grad_outs[at // 2][...] = piece_rows
            else:
                at_send = parts // 2 + (0 if at > 4 else 1)
                grad_outs[at_send][0 if at % 4 == 3 else 1] = piece_rows.astype(BF16)
    else:
        grad_outs[0][:, : 3 * cols] = grad_first
        grad_outs[0][:, 3 * cols :] = grad_last
    normed_grad[...] = dot(grad_proj[...], weight_ref[:, : 3 * cols], NT)
    sums_out[...] = sums_ref[...]
    sums_out[experts + 1 : experts + 2, :] = jnp.sum(
        normed_grad[...] * unit, axis=0, keepdims=True
    )
    sums_out[experts + 2 : experts + 3, : HEADS * BUCKETS] = bias_row
    for at in range(pieces):
        mine = normed_grad[pl.ds(pl.multiple_of((piece ^ at) * ROWS, ROWS), ROWS), :]
        if at % 2 == 0:
            keep_out[at // 2][...] = mine
        else:
            send_out[at // 2] = mine.astype(BF16)


def input_kernel(own_ref, gain_ref, mixed_grad_ref, part_ref, near_ref, far_ref, out_ref):
    x = own_ref[...].astype(F32)
    scale = lax.rsqrt(jnp.mean(x * x, axis=1, keepdims=True) + 1e-6)
    scaled = (
        part_ref[...] + near_ref[0].astype(F32) + far_ref[...].astype(F32)
    ) * gain_ref[...]
    cubed = scale * scale * scale
    own = scale * scaled - x * cubed * jnp.mean(scaled * x, axis=1, keepdims=True)
    out_ref[...] = (mixed_grad_ref[...] + own).astype(BF16)


def swap(value, axis, size, mask):
    return lax.ppermute(value, axis, [(i, i ^ mask) for i in range(size)])


def gather_weights(shard, senders):
    if senders != 8:
        return [lax.all_gather(shard, "dp", axis=0, tiled=True)]
    parts = {0: shard}
    parts[1] = swap(shard, "dp", senders, 1)
    for mask in (2, 4, 6):
        parts[mask] = swap(shard, "dp", senders, mask)
    for mask in (2, 4, 6):
        parts[mask + 1] = swap(parts[mask], "dp", senders, 1)
    return [parts[i] for i in range(senders)]


def fold_kernel(keep_ref, near_ref, out_ref):
    out_ref[...] = (keep_ref[...] + near_ref[...].astype(F32)).astype(BF16)


def fold(keep, near, name, after=()):
    return call(fold_kernel, [struct(near.shape, BF16)], [], [keep, near], name=name, after=after)[0]


def finish_kernel(cols, keep_ref, near_ref, one_ref, two_ref, three_ref, first_ref, last_ref):
    total = keep_ref[...] + near_ref[...].astype(F32)
    for part in (one_ref, two_ref, three_ref):
        total = total + part[...].astype(F32)
    for at in range(3):
        first_ref[at] = total[:, at * cols : (at + 1) * cols]
    last_ref[...] = total[:, 3 * cols :]


def fold_two_kernel(one_ref, two_ref, near_ref, one_out, two_out):
    one_out[...] = (one_ref[...] + near_ref[0].astype(F32)).astype(BF16)
    two_out[...] = (two_ref[...] + near_ref[1].astype(F32)).astype(BF16)


def finish_kernel(cols, keep_ref, near_ref, one_ref, two_ref, three_ref, first_ref, last_ref):
    total = keep_ref[...] + near_ref[1].astype(F32)
    for part in (one_ref, two_ref, three_ref):
        total = total + part[...].astype(F32)
    for at in range(3):
        first_ref[at] = total[:, at * cols : (at + 1) * cols]
    last_ref[...] = total[:, 3 * cols :]


def add_kernel(one_ref, two_ref, out_ref):
    out_ref[...] = one_ref[...] + two_ref[...]


def sums_kernel(experts, *refs):
    *parts, gains_ref, bias_ref, router_ref = refs
    total = parts[0][...]
    for part in parts[1:]:
        total = total + part[...]
    router_ref[...] = total[:experts]
    gains_ref[0:2, :] = total[experts : experts + 2]
    for head in range(HEADS):
        bias_ref[head : head + 1, :] = total[
            experts + 2 : experts + 3, head * BUCKETS : (head + 1) * BUCKETS
        ]


def add(one, two, after):
    return call(
        add_kernel, [struct(one.shape, F32)], [], [one, two], name="add_sums", prompt=True, after=after
    )[0]


def last_sums(grads, keep_a, keep_b, near, sums, senders, pieces, cols, experts):
    if senders != 8:
        part, near, far, _ = scatter_rows(keep_a, keep_b, near, pieces)
        total = lax.psum_scatter(grads[0], "dp", scatter_dimension=0, tiled=True)
        first = jnp.stack([total[:, at * cols : (at + 1) * cols] for at in range(3)])
        weight_sums = (first, total[:, 3 * cols :])
        sums = [lax.psum(sums, ("dp", "tensor"))]
    else:
        near_two = swap(grads[4], "dp", senders, 1)
        near_one = swap(grads[5], "dp", senders, 1)
        sums = add(sums, swap(sums, "tensor", pieces, 1), [near])
        got = swap(sums, "tensor", pieces, 2)
        other = call(
            lambda keep, got, out: fold_kernel(keep, got.at[1], out),
            [struct(keep_b.shape, BF16)],
            [],
            [keep_b, near],
            name="fold_rows", prompt=True,
            after=[sums],
        )[0]
        part, far = keep_a, swap(other, "tensor", pieces, 2)
        sums = add(sums, got, [other])
        got = swap(sums, "dp", senders, 1)
        six, four = call(
            fold_two_kernel,
            [struct(keep.shape, BF16) for keep in (grads[3], grads[2])],
            [],
            [grads[3], grads[2], near_two],
            name="fold_weights", prompt=True,
            after=[sums],
        )
        arrived = [swap(six, "dp", senders, 6), swap(four, "dp", senders, 4)]
        sums = add(sums, got, [six])
        two = call(
            lambda keep, got, out: fold_kernel(keep, got.at[0], out),
            [struct(grads[1].shape, BF16)],
            [],
            [grads[1], near_one],
            name="fold_weights", prompt=True,
            after=[sums],
        )[0]
        arrived.append(swap(two, "dp", senders, 2))
        sums = [sums] + [swap(sums, "dp", senders, mask) for mask in (6, 4, 2)]
        depth = grads[0].shape[0]
        weight_sums = call(
            functools.partial(finish_kernel, cols),
            [struct((3, depth, cols), F32), struct((depth, cols), F32)],
            [],
            [grads[0], near_one] + arrived,
            name="finish", prompt=True,
        )
    width = sums[0].shape[1]
    small = call(
        functools.partial(sums_kernel, experts),
        [
            struct((8, width), F32),
            struct((HEADS, BUCKETS), F32),
            struct((experts, width), F32),
        ],
        [],
        sums,
        name="sums", prompt=True,
    )
    return weight_sums, (part, near, far), small


def scatter_rows(keep_a, keep_b, near, pieces, after=()):
    other = call(
        lambda keep, got, out: fold_kernel(keep, got.at[1], out),
        [struct(keep_b.shape, BF16)],
        [],
        [keep_b, near],
        name="fold_rows", prompt=True,
        after=after,
    )[0]
    return keep_a, near, swap(other, "tensor", pieces, 2), other


def gather_rows(rows, pieces):
    far = swap(rows, "tensor", pieces, 2)
    near = swap(rows, "tensor", pieces, 1)
    last = swap(far, "tensor", pieces, 1)
    return [rows, near, far, last]


def exchange(blocks, senders, capacity):
    rows, width = blocks.shape
    return lax.all_to_all(
        blocks.reshape(senders, capacity, width), "dp", split_axis=0, concat_axis=0, tiled=True
    ).reshape(rows, width)


def body(
    tokens,
    doc_start,
    routes,
    gain_attn,
    w_qkv,
    w_out,
    rel_bias,
    gain_ffn,
    router,
    w_in,
    w_exp_out,
    out_grad,
):
    pieces = lax.axis_size("tensor")
    senders = lax.axis_size("dp")
    tok_dev, width = tokens.shape
    routes, rel_bias, router = routes.T, rel_bias.T, router.T
    length = tok_dev * pieces
    experts = router.shape[0]
    capacity = max(2, 3 * tok_dev * routes.shape[0] // (2 * experts))
    slots = experts * capacity
    heads = w_out.shape[1] // HDIM
    cols = heads * HDIM
    gain_one = gain_attn.reshape(1, width)
    gain_two = gain_ffn.reshape(1, width)

    shard, in_head = call(
        pack_kernel,
        [
            struct((w_out.shape[0], 4 * cols), BF16),
            struct((width // 3, w_in.shape[2]), BF16),
        ],
        [],
        [w_qkv.transpose(1, 0, 2), w_out, w_in[0]],
        name="pack",
        held=(0, 1, 2),
        parts={2: (width // 3, w_in.shape[2])},
    )
    weights = gather_weights(shard, senders)
    rows = gather_rows(tokens, pieces)
    out_one = w_exp_out[0]
    in_one = w_in[0]
    out_two = swap(out_one, "tensor", pieces, 2)
    in_two_a = swap(in_head, "tensor", pieces, 2)
    in_two_b = swap(in_one[in_head.shape[0] :], "tensor", pieces, 2)

    slot, grad_out = call(
        functools.partial(slots_kernel, capacity),
        [struct((tok_dev, 128), jnp.int32), struct((slots, width), BF16)],
        [],
        [routes, out_grad],
        flops=2 * slots * tok_dev * width,
        name="slots",
        held=(1,),
        kept=(0, 1),
    )

    grad_out = once(grad_out, weights[1::2], "gathered")
    whole_weight, whole_rows, projected, attended, lse, keep_a, keep_b, send = call(
        functools.partial(forward_kernel, len(weights), pieces, heads),
        [
            struct((width, 4 * cols), BF16),
            struct((length, width), BF16),
            struct((length, 3 * cols), BF16),
            struct((length, cols), BF16),
            struct((length, 128), F32),
            struct((tok_dev, width), F32),
            struct((tok_dev, width), F32),
            struct((pieces // 2, tok_dev, width), BF16),
        ],
        [],
        [doc_start, rel_bias] + weights + rows + [gain_one],
        smem=2,
        flops=2 * length * width * 4 * cols + 4 * heads * length * length * HDIM,
        name="attend",
        held=tuple(range(2, 2 + len(weights))),
        kept=(0, 1, 2, 3, 4),
        vmem=12,
    )
    pull_own = exchange(grad_out, senders, capacity)
    pull_mate = swap(pull_own, "tensor", pieces, 1)
    far_pull_own = swap(pull_own, "tensor", pieces, 2)

    near = swap(send, "tensor", pieces, 1)
    part, near, far, _ = scatter_rows(keep_a, keep_b, near, pieces, [out_two, in_two_a])
    mixed, normed_two, gates, outgoing = call(
        dispatch_kernel,
        [
            struct((tok_dev, width), F32),
            struct((tok_dev, width), BF16),
            struct((tok_dev, 128), F32),
            struct((slots, width + GATE_LANES), BF16),
        ],
        [],
        [tokens, part, near, far, gain_two, router, routes, slot],
        flops=2 * slots * tok_dev * width,
        name="dispatch",
        after=[pull_own],
        kept=(0, 1, 2),
    )
    slot_own = exchange(outgoing, senders, capacity)
    slot_mate = swap(slot_own, "tensor", pieces, 1)
    payload = width + GATE_LANES
    units = in_one.shape[1]
    expert_flops = 12 * slots * width * units
    hidden_one, pre_one, row_total, gate_total = call(
        own_slice_kernel,
        [struct((2 * slots, units), BF16)] * 2
        + [struct((2 * slots, width), F32), struct((2 * slots, GATE_LANES), F32)],
        [pltpu.VMEM((2 * slots, width), BF16)] * 2,
        [slot_own, slot_mate, pull_own, pull_mate, in_one, out_one],
        flops=expert_flops,
        name="own_slice",
        prompt=True,
        held=(4, 5),
        kept=(0, 1),
        vmem=18,
    )
    hidden_two, row_keep, row_send = call(
        far_slice_kernel,
        [
            struct((2 * slots, units), BF16),
            struct((slots, payload), F32),
            struct((slots, payload), BF16),
        ],
        [pltpu.VMEM((width, units), BF16), pltpu.VMEM((2 * slots, units), BF16)]
        + [pltpu.VMEM((2 * slots, width), BF16)] * 2,
        [slot_own, slot_mate, pull_own, pull_mate, in_two_a, in_two_b, out_two, row_total, gate_total],
        flops=expert_flops,
        name="far_slice",
        prompt=True,
        held=(4, 5, 6),
        kept=(0,),
        vmem=20,
    )
    row_mate = swap(row_send, "tensor", pieces, 1)
    far_own = swap(slot_own, "tensor", pieces, 2)
    (row_out,) = call(
        merge_kernel,
        [struct((slots, payload), BF16)],
        [],
        [row_keep, row_mate],
        name="merge",
    )
    back = exchange(row_out, senders, capacity)

    far_mate = swap(far_own, "tensor", pieces, 1)
    out_keep, out_send = call(
        expert_out_kernel,
        [struct((slots, width), F32), struct((slots, width), BF16)],
        [],
        [hidden_one, hidden_two, out_one, out_two],
        flops=4 * 2 * slots * width * in_one.shape[1],
        name="expert_out",
        held=(0, 1, 2, 3),
        after=[far_own],
        vmem=10,
    )
    far_pull_own = once(far_pull_own, [out_send], "pulled")
    far_pull_mate = swap(far_pull_own, "tensor", pieces, 1)
    grad_in, grad_out_sum, graded = call(
        weight_grad_kernel,
        [struct(in_one.shape, F32), struct(out_one.shape, F32), struct((8, 128), F32)],
        [
            pltpu.VMEM((width, 4 * slots), BF16),
            pltpu.VMEM((4 * slots, width), BF16),
            pltpu.VMEM((2 * slots, in_one.shape[1]), BF16),
            pltpu.VMEM((2 * slots, in_one.shape[1]), BF16),
        ],
        [
            slot_own,
            slot_mate,
            pull_own,
            pull_mate,
            far_own,
            far_mate,
            far_pull_own,
            far_pull_mate,
            in_one,
            out_one,
            hidden_one,
            pre_one,
        ],
        flops=24 * slots * width * in_one.shape[1],
        name="weight_grads",
        held=tuple(range(12)),
        after=[out_send],
        vmem=26,
    )

    sum_rows = -(-(experts + 3) // 8) * 8
    mixed_grad, mixed_low, sums_two = call(
        combine_kernel,
        [
            struct((tok_dev, width), F32),
            struct((tok_dev, width), BF16),
            struct((sum_rows, width), F32),
        ],
        [],
        [back, slot, gates, mixed, normed_two, router, routes, out_grad, gain_two],
        flops=2 * slots * tok_dev * width,
        name="combine",
        after=[graded],
        held=(1, 2, 3, 4, 7),
    )
    expert_out = fold(out_keep, swap(out_send, "tensor", pieces, 1), "fold_out", [mixed_low])
    returned = exchange(expert_out, senders, capacity)
    (result,) = call(
        result_kernel,
        [struct((tok_dev, width), BF16)],
        [],
        [returned, slot, gates, mixed],
        flops=4 * slots * tok_dev * width,
        name="result", prompt=True,
        held=(1, 2, 3),
    )

    lows = gather_rows(mixed_low, pieces)
    parts = len(weights)
    if parts > 1:
        depth = width // parts
        grad_shapes = [struct((depth, 4 * cols), F32)] * (parts // 2)
        grad_shapes += [struct((2, depth, 4 * cols), BF16)] * 2
        grad_scratch = [pltpu.VMEM((width, 4 * cols), F32)]
    else:
        grad_shapes = [struct((width, 4 * cols), F32)]
        grad_scratch = []
    *weight_grads, keep_a, keep_b, send, sums = call(
        functools.partial(backward_kernel, parts, pieces, heads, experts),
        grad_shapes
        + [
            struct((tok_dev, width), F32),
            struct((tok_dev, width), F32),
            struct((pieces // 2, tok_dev, width), BF16),
            struct((sum_rows, width), F32),
        ],
        [
            pltpu.VMEM((length, width), BF16),
            pltpu.VMEM((length, 3 * cols), BF16),
            pltpu.VMEM((length, width), F32),
        ]
        + grad_scratch,
        [doc_start, rel_bias]
        + lows
        + [whole_weight, whole_rows, projected, attended, lse, gain_one, sums_two],
        smem=2,
        name="attend_back",
        prompt=True,
        held=tuple(range(2 + pieces, 7 + pieces)),
        vmem=16,
    )
    near = swap(send, "tensor", pieces, 1)
    (first_sum, last_sum), (part, near, far), (gains, bias_grad, router_grad) = last_sums(
        weight_grads, keep_a, keep_b, near, sums, senders, pieces, cols, experts
    )
    (input_grad,) = call(
        input_kernel,
        [struct((tok_dev, width), BF16)],
        [],
        [tokens, gain_one, mixed_grad, part, near, far],
        name="input_grad", prompt=True,
        held=(0, 2),
    )
    return (
        result,
        input_grad,
        gains[1],
        first_sum.transpose(1, 0, 2),
        last_sum,
        bias_grad.T,
        gains[0],
        router_grad.T,
        grad_in[None],
        grad_out_sum[None],
    )


def solution(mesh):
    in_specs = (
        P(("dp", "tensor"), None),
        P("dp"),
        P(("dp", "tensor"), None),
        P(),
        P("dp", None, "tensor"),
        P("dp", "tensor"),
        P(),
        P(),
        P(),
        P("dp", None, "tensor"),
        P("dp", "tensor", None),
        P(("dp", "tensor"), None),
    )
    out_specs = (
        P(("dp", "tensor"), None),
        P(("dp", "tensor"), None),
        P(),
        P("dp", None, "tensor"),
        P("dp", "tensor"),
        P(),
        P(),
        P(),
        P("dp", None, "tensor"),
        P("dp", "tensor", None),
    )
    return jax.shard_map(body, mesh=mesh, in_specs=in_specs, out_specs=out_specs, check_vma=False)
```

```python
import functools

import jax
import jax.numpy as jnp
import numpy as np
from jax import lax
from jax.experimental import pallas as pl
from jax.experimental.pallas import tpu as pltpu
from jax.sharding import PartitionSpec as P

HEADS = 12
HDIM = 64
BUCKETS = 32
ROWS = 128
BLOCK = 256
GATE_LANES = 128

LIMITS = np.array([19, 21, 24, 27, 31, 35, 40, 46, 52, 59, 67, 77, 87, 99, 113], np.int32)
HIGHEST = lax.Precision.HIGHEST
F32 = jnp.float32
BF16 = jnp.bfloat16
MIB = 1024 * 1024

NN = (((1,), (0,)), ((), ()))
NT = (((1,), (1,)), ((), ()))
TN = (((0,), (0,)), ((), ()))


def dot(left, right, dims=NN, precision=None):
    return lax.dot_general(left, right, dims, preferred_element_type=F32, precision=precision)


def iota(shape, axis):
    return lax.broadcasted_iota(jnp.int32, shape, axis)


def bucket_of(distance):
    bucket = jnp.minimum(distance, 16)
    for limit in LIMITS:
        bucket = bucket + (distance >= int(limit)).astype(jnp.int32)
    return bucket


def in_three(value):
    high = value.astype(BF16)
    rest = value - high.astype(F32)
    middle = rest.astype(BF16)
    low = (rest - middle.astype(F32)).astype(BF16)
    return high, middle, low


def three_lanes(value):
    high, middle, low = in_three(value)
    lane = iota((value.shape[0], GATE_LANES), 1)
    zero = jnp.zeros((value.shape[0], GATE_LANES), F32)
    spread = jnp.where(
        lane == 0,
        high.astype(F32),
        jnp.where(lane == 1, middle.astype(F32), jnp.where(lane == 2, low.astype(F32), zero)),
    )
    return spread.astype(BF16)


def lanes_sum(lanes):
    return jnp.sum(lanes.astype(F32), axis=1, keepdims=True)


def pick(columns, at):
    return columns[:, at : at + 1]


def call(
    kernel,
    outs,
    scratch,
    args,
    smem=0,
    flops=0,
    name=None,
    after=(),
    vmem=6,
    held=(),
    kept=(),
    passed=(),
    prompt=False,
    parts={},
):
    n_in, n_after, n_out = len(args), len(after), len(outs)
    n_pass = len(passed)

    def run(*refs):
        ins, rest = refs[:n_in], refs[n_in + n_after + n_pass :]
        kernel(*ins, *rest[:n_out], *rest[n_out + n_pass :])

    def whole(a):
        shape = getattr(a, "shape", a)
        return pl.BlockSpec(shape, lambda i: (0,) * len(shape))

    moved = sum(a.size * a.dtype.itemsize for a in list(args) + list(outs))
    args = [
        pltpu.with_memory_space_constraint(a, pltpu.HBM) if at in held else a
        for at, a in enumerate(args)
    ]
    after = [
        pltpu.with_memory_space_constraint(a, pltpu.HBM) if a.size > 1 << 18 else a for a in after
    ]
    out_shape = [
        pltpu.HBM(o.shape, o.dtype) if at in kept else jax.ShapeDtypeStruct(o.shape, o.dtype)
        for at, o in enumerate(outs)
    ]
    return pl.pallas_call(
        run,
        grid=(1,),
        out_shape=out_shape + [jax.ShapeDtypeStruct(o.shape, o.dtype) for o in passed],
        in_specs=[pl.BlockSpec(memory_space=pltpu.SMEM)] * smem
        + [whole(parts.get(smem + at, a)) for at, a in enumerate(args[smem:])]
        + [pl.BlockSpec(memory_space=pl.ANY)] * (n_after + n_pass),
        out_specs=[whole(o) for o in outs] + [pl.BlockSpec(memory_space=pl.ANY)] * n_pass,
        scratch_shapes=scratch,
        input_output_aliases={n_in + n_after + at: n_out + at for at in range(n_pass)},
        compiler_params=pltpu.CompilerParams(vmem_limit_bytes=vmem * MIB),
        cost_estimate=pl.CostEstimate(
            flops=1 if prompt else flops,
            bytes_accessed=1 if prompt else moved,
            transcendentals=0,
        ),
        name=name,
    )(*args, *after, *passed)


def once(value, after, name):
    return call(lambda: None, [], [], [], name=name, after=after, passed=[value])[0]


def columns_of(turned):
    filled = jnp.concatenate(
        [turned.astype(F32), jnp.zeros((8 - turned.shape[0], turned.shape[1]), F32)], axis=0
    )
    return filled.T.astype(jnp.int32)


def pack_kernel(first_ref, last_ref, in_ref, out_ref, head_ref):
    head_ref[...] = in_ref[...]
    cols = last_ref.shape[1]
    for at in range(3):
        out_ref[:, at * cols : (at + 1) * cols] = first_ref[at]
    out_ref[:, 3 * cols :] = last_ref[...]


def struct(shape, dtype):
    return jax.ShapeDtypeStruct(shape, dtype)


def slots_kernel(capacity, routes_ref, grad_ref, slot_ref, out_ref):
    tokens = routes_ref.shape[1]
    slots = out_ref.shape[0]
    experts = slots // capacity
    routes = columns_of(routes_ref[...])
    first, second = routes[:, 0:1], routes[:, 1:2]
    lane = iota((tokens, experts), 1)
    one_first = (first == lane).astype(F32)
    one_second = (second == lane).astype(F32)
    member = (one_first + one_second).astype(BF16)
    below = (iota((tokens, tokens), 1) < iota((tokens, tokens), 0)).astype(F32).astype(BF16)
    earlier = dot(below, member)
    slot_first = first * capacity + jnp.sum(one_first * earlier, axis=1, keepdims=True).astype(
        jnp.int32
    )
    slot_second = second * capacity + jnp.sum(one_second * earlier, axis=1, keepdims=True).astype(
        jnp.int32
    )
    wide = iota((tokens, 128), 1)
    slot_ref[...] = jnp.where(wide == 0, slot_first, slot_second)
    places = iota((tokens, slots), 1)
    chosen = ((slot_first == places) | (slot_second == places)).astype(F32).astype(BF16)
    out_ref[...] = dot(chosen, grad_ref[...], TN).astype(BF16)


def bias_tiles(rel_ref, first_head, heads):
    wide = 2 * BLOCK
    distance = (BLOCK - iota((8, wide), 1)) & (wide - 1)
    bucket = bucket_of(distance)
    tiles = []
    for head in range(heads):
        line = jnp.zeros((8, wide), F32)
        for b in range(BUCKETS):
            line = jnp.where(bucket == b, rel_ref[first_head + head, b], line)
        grid = jnp.broadcast_to(line[0:1, :], (BLOCK, wide))
        tiles.append(pltpu.roll(grid, 0, 1, stride=1, stride_axis=0))
    return tiles


def masked_scores(query, keys, tile, second, block):
    width = (block + 1) * BLOCK
    raw = dot(query, keys, NT) * HDIM**-0.5
    bias = tile[:, 2 * BLOCK - width :]
    column = iota((BLOCK, width), 1)
    row = iota((BLOCK, width), 0) + block * BLOCK
    starts = jnp.where(row >= second, second, 0)
    allowed = (column <= row) & (column >= starts)
    return jnp.where(allowed, raw + bias, -1e9)


def forward_kernel(parts, pieces, heads, *refs):
    doc_ref, rel_ref = refs[:2]
    weights = refs[2 : 2 + parts]
    rows = refs[2 + parts : 2 + parts + pieces]
    gain_ref = refs[2 + parts + pieces]
    weight_out, row_out, proj_out, att_out, lse_out, keep_a, keep_b, send_out = refs[
        3 + parts + pieces :
    ]
    keep_out = (keep_a, keep_b)
    piece, mine_dp = lax.axis_index("tensor"), lax.axis_index("dp")
    second = doc_ref[doc_ref.shape[0] - 1]
    cols = heads * HDIM
    for at in range(parts):
        depth = weights[at].shape[0]
        start = (mine_dp ^ at) * depth if parts > 1 else 0
        weight_out[pl.ds(pl.multiple_of(start, 16), depth), :] = weights[at][...]
    for at in range(pieces):
        row_out[pl.ds(pl.multiple_of((piece ^ at) * ROWS, ROWS), ROWS), :] = rows[at][...]
    x = row_out[...].astype(F32)
    scale = lax.rsqrt(jnp.mean(x * x, axis=1, keepdims=True) + 1e-6)
    normed = (x * scale * gain_ref[...]).astype(BF16)
    proj_out[...] = dot(normed, weight_out[:, : 3 * cols]).astype(BF16)
    tiles = bias_tiles(rel_ref, piece * heads, heads)
    blocks = x.shape[0] // BLOCK
    proj = proj_out[...]
    wide = iota((BLOCK, 128), 1)
    for block in range(blocks):
        here = slice(block * BLOCK, (block + 1) * BLOCK)
        upto = slice(0, (block + 1) * BLOCK)
        done = []
        kept = jnp.zeros((BLOCK, 128), F32)
        for head in range(heads):
            at = head * HDIM
            query = proj[here, at : at + HDIM]
            keys = proj[upto, cols + at : cols + at + HDIM]
            values = proj[upto, 2 * cols + at : 2 * cols + at + HDIM]
            scores = masked_scores(query, keys, tiles[head], second, block)
            peak = jnp.max(scores, axis=1, keepdims=True)
            shifted = jnp.exp(scores - peak)
            total = jnp.sum(shifted, axis=1, keepdims=True)
            attention = (shifted * (1.0 / total)).astype(BF16)
            done.append(dot(attention, values).astype(BF16))
            kept = jnp.where(wide == head, peak + jnp.log(total), kept)
        att_out[here, :] = jnp.concatenate(done, axis=1)
        lse_out[here, :] = kept
    weight_last = weight_out[:, 3 * cols :]
    for at in range(pieces):
        mine = att_out[pl.ds(pl.multiple_of((piece ^ at) * ROWS, ROWS), ROWS), :]
        product = dot(mine, weight_last, NT)
        if at % 2 == 0:
            keep_out[at // 2][...] = product
        else:
            send_out[at // 2] = product.astype(BF16)


def dispatch_kernel(
    own_ref,
    part_ref,
    near_ref,
    far_ref,
    gain_ref,
    router_ref,
    routes_ref,
    slot_ref,
    mixed_ref,
    normed_ref,
    gates_ref,
    out_ref,
):
    width = own_ref.shape[1]
    tokens = own_ref.shape[0]
    slots = out_ref.shape[0]
    mixed = own_ref[...].astype(F32) + (
        part_ref[...] + near_ref[0].astype(F32) + far_ref[...].astype(F32)
    )
    mixed_ref[...] = mixed
    scale = lax.rsqrt(jnp.mean(mixed * mixed, axis=1, keepdims=True) + 1e-6)
    normed = (mixed * scale * gain_ref[...]).astype(BF16)
    normed_ref[...] = normed
    logits = dot(normed, router_ref[...], NT)
    routes = columns_of(routes_ref[...])
    lane = iota(logits.shape, 1)
    one = jnp.sum(jnp.where(routes[:, 0:1] == lane, logits, 0.0), axis=1, keepdims=True)
    two = jnp.sum(jnp.where(routes[:, 1:2] == lane, logits, 0.0), axis=1, keepdims=True)
    peak = jnp.maximum(one, two)
    one, two = jnp.exp(one - peak), jnp.exp(two - peak)
    total = one + two
    one, two = one / total, two / total
    wide = iota((tokens, 128), 1)
    gates_ref[...] = jnp.where(wide == 0, one, two)
    places = iota((tokens, slots), 1)
    slot = slot_ref[...]
    first = (slot[:, 0:1] == places).astype(F32).astype(BF16)
    second = (slot[:, 1:2] == places).astype(F32).astype(BF16)
    out_ref[:, :width] = dot(first + second, normed, TN).astype(BF16)
    gate_slots = dot(first, three_lanes(one), TN) + dot(second, three_lanes(two), TN)
    out_ref[:, width:] = gate_slots.astype(BF16)


def gelu_and_slope(x):
    inner = 0.7978845608028654 * (x + 0.044715 * (x * x * x))
    bend = jnp.tanh(inner)
    half = 0.5 * (1.0 + bend)
    slope = half + 0.5 * x * (1.0 - bend * bend) * (
        0.7978845608028654 * (1.0 + 3 * 0.044715 * (x * x))
    )
    return x * half, slope


def gather_sides(sources, pulls, rows_all, pulls_all):
    rows, width = pulls[0].shape
    gates = []
    for at, (source, pull) in enumerate(zip(sources, pulls)):
        here = slice(at * rows, (at + 1) * rows)
        rows_all[here, :] = source[:, :width]
        pulls_all[here, :] = pull[...]
        gates.append(lanes_sum(source[:, width:]))
    return jnp.concatenate(gates, axis=0)


def through_slice(rows_all, pulls_all, gate, in_ref, out_ref, hidden_out, pre_out):
    hidden_units = in_ref.shape[1]
    tile = 256
    gate_wide = jnp.zeros((rows_all.shape[0], tile), F32)
    for at in range(0, hidden_units, tile):
        there = slice(at, at + tile)
        pulled = dot(pulls_all[...], out_ref[there, :], NT)
        hidden, slope = gelu_and_slope(dot(rows_all[...], in_ref[:, there]))
        hidden = hidden.astype(BF16)
        hidden_out[:, there] = hidden
        pre_out[:, there] = (pulled * gate * slope).astype(BF16)
        gate_wide = gate_wide + hidden.astype(F32) * pulled
    return jnp.sum(gate_wide, axis=1, keepdims=True)


def own_slice_kernel(
    own_ref,
    mate_ref,
    pull_own,
    pull_mate,
    in_ref,
    out_ref,
    hidden_ref,
    pre_ref,
    total_ref,
    sum_ref,
    rows_all,
    pulls_all,
):
    gate = gather_sides((own_ref, mate_ref), (pull_own, pull_mate), rows_all, pulls_all)
    gate_sum = through_slice(rows_all, pulls_all, gate, in_ref, out_ref, hidden_ref, pre_ref)
    sum_ref[...] = jnp.broadcast_to(gate_sum, sum_ref.shape)
    total_ref[...] = dot(pre_ref[...], in_ref[...], NT)


def far_slice_kernel(
    own_ref,
    mate_ref,
    pull_own,
    pull_mate,
    in_a_ref,
    in_b_ref,
    out_ref,
    total_ref,
    sum_ref,
    hidden_ref,
    keep_ref,
    send_ref,
    in_ref,
    pre_ref,
    rows_all,
    pulls_all,
):
    rows, width = pull_own.shape
    split = in_a_ref.shape[0]
    in_ref[:split, :] = in_a_ref[...]
    in_ref[split:, :] = in_b_ref[...]
    gate = gather_sides((own_ref, mate_ref), (pull_own, pull_mate), rows_all, pulls_all)
    gate_sum = sum_ref[:, 0:1] + through_slice(
        rows_all, pulls_all, gate, in_ref, out_ref, hidden_ref, pre_ref
    )
    total = total_ref[...] + dot(pre_ref[...], in_ref[...], NT)
    keep_ref[:, :width] = total[:rows, :]
    keep_ref[:, width:] = jnp.broadcast_to(gate_sum[:rows], (rows, GATE_LANES))
    send_ref[:, :width] = total[rows:, :].astype(BF16)
    send_ref[:, width:] = three_lanes(gate_sum[rows:])


def turn_slots(sources, pulls, rows_turned, pulls_all, rows_all=None):
    rows, width = pulls[0].shape
    for at, (source, pull) in enumerate(zip(sources, pulls)):
        here = slice(at * rows, (at + 1) * rows)
        rows_turned[:, here] = source[:, :width].T
        gate = lanes_sum(source[:, width:])
        pulls_all[here, :] = (gate * pull[...].astype(F32)).astype(BF16)
        if rows_all is not None:
            rows_all[here, :] = source[:, :width]


def own_grads_kernel(
    own_ref,
    mate_ref,
    pull_own,
    pull_mate,
    hidden_ref,
    pre_ref,
    grad_in,
    grad_out,
    token_ref,
    rows_turned,
    pulls_all,
):
    token_ref[...] = jnp.zeros_like(token_ref)
    turn_slots((own_ref, mate_ref), (pull_own, pull_mate), rows_turned, pulls_all)
    tile = 256
    for unit in range(0, hidden_ref.shape[1], tile):
        there = slice(unit, unit + tile)
        grad_in[:, there] = dot(rows_turned[...], pre_ref[:, there])
        grad_out[there, :] = dot(hidden_ref[:, there], pulls_all[...], TN)


def far_grads_kernel(
    own_ref,
    mate_ref,
    pull_own,
    pull_mate,
    in_ref,
    out_ref,
    own_in,
    own_out,
    grad_in,
    grad_out,
    token_ref,
    rows_turned,
    pulls_all,
    rows_all,
):
    token_ref[...] = jnp.zeros_like(token_ref)
    turn_slots((own_ref, mate_ref), (pull_own, pull_mate), rows_turned, pulls_all, rows_all)
    tile = 256
    for unit in range(0, in_ref.shape[1], tile):
        there = slice(unit, unit + tile)
        hidden, slope = gelu_and_slope(dot(rows_all[...], in_ref[:, there]))
        pulled = dot(pulls_all[...], out_ref[there, :], NT)
        pre_grad = (pulled * slope).astype(BF16)
        grad_in[:, there] = own_in[:, there] + dot(rows_turned[...], pre_grad)
        grad_out[there, :] = own_out[there, :] + dot(hidden.astype(BF16), pulls_all[...], TN)


def expert_out_kernel(hidden_one, hidden_two, out_one, out_two, keep_ref, send_ref):
    rows = keep_ref.shape[0]
    product = dot(hidden_one[...], out_one[...]) + dot(hidden_two[...], out_two[...])
    keep_ref[...] = product[:rows]
    send_ref[...] = product[rows:].astype(BF16)


def merge_kernel(keep_ref, mate_ref, out_ref):
    width = keep_ref.shape[1] - GATE_LANES
    out_ref[:, :width] = (keep_ref[:, :width] + mate_ref[:, :width].astype(F32)).astype(BF16)
    gate = keep_ref[:, width : width + 1] + lanes_sum(mate_ref[:, width:])
    out_ref[:, width:] = three_lanes(gate)


def combine_kernel(
    back_ref,
    slot_ref,
    gates_ref,
    mixed_ref,
    normed_ref,
    router_ref,
    routes_ref,
    grad_ref,
    gain_ref,
    mixed_grad_ref,
    low_ref,
    sums_ref,
):
    tokens, width = grad_ref.shape
    slots = back_ref.shape[0]
    experts = router_ref.shape[0]
    places = iota((tokens, slots), 1)
    slot = slot_ref[...]
    first = (slot[:, 0:1] == places).astype(F32).astype(BF16)
    second = (slot[:, 1:2] == places).astype(F32).astype(BF16)
    lanes = back_ref[:, width:]
    pull_one = jnp.sum(dot(first, lanes), axis=1, keepdims=True)
    pull_two = jnp.sum(dot(second, lanes), axis=1, keepdims=True)
    one, two = gates_ref[:, 0:1], gates_ref[:, 1:2]
    mean_pull = one * pull_one + two * pull_two
    delta_one = one * (pull_one - mean_pull)
    delta_two = two * (pull_two - mean_pull)
    routes = columns_of(routes_ref[...])
    lane = iota((tokens, experts), 1)
    logit_grad = jnp.where(routes[:, 0:1] == lane, delta_one, 0.0) + jnp.where(
        routes[:, 1:2] == lane, delta_two, 0.0
    )
    high = logit_grad.astype(BF16)
    low = (logit_grad - high.astype(F32)).astype(BF16)
    normed = normed_ref[...]
    router = router_ref[...]
    normed_grad = dot(first + second, back_ref[:, :width]) + (
        dot(high, router) + dot(low, router)
    )
    mixed = mixed_ref[...]
    grad = grad_ref[...].astype(F32)
    scale = lax.rsqrt(jnp.mean(mixed * mixed, axis=1, keepdims=True) + 1e-6)
    scaled = normed_grad * gain_ref[...]
    cubed = scale * scale * scale
    mixed_grad = (
        grad
        + scale * scaled
        - mixed * cubed * jnp.mean(scaled * mixed, axis=1, keepdims=True)
    )
    mixed_grad_ref[...] = mixed_grad
    low_ref[...] = mixed_grad.astype(BF16)
    sums_ref[...] = jnp.zeros_like(sums_ref)
    sums_ref[:experts, :] = dot(high, normed, TN) + dot(low, normed, TN)
    sums_ref[experts : experts + 1, :] = jnp.sum(
        normed_grad * mixed * scale, axis=0, keepdims=True
    )


def result_kernel(back_ref, slot_ref, gates_ref, mixed_ref, out_ref):
    tokens = mixed_ref.shape[0]
    slots = back_ref.shape[0]
    places = iota((tokens, slots), 1)
    slot = slot_ref[...]
    first = (slot[:, 0:1] == places).astype(F32).astype(BF16)
    second = (slot[:, 1:2] == places).astype(F32).astype(BF16)
    back = back_ref[...]
    added = gates_ref[:, 0:1] * dot(first, back) + gates_ref[:, 1:2] * dot(second, back)
    out_ref[...] = (mixed_ref[...] + added).astype(BF16)


def backward_kernel(parts, pieces, heads, experts, *refs):
    doc_ref, rel_ref = refs[:2]
    lows = refs[2 : 2 + pieces]
    weight_ref, row_ref, proj_ref, att_ref, lse_ref, gain_ref, sums_ref = refs[
        2 + pieces : 9 + pieces
    ]
    outs = refs[9 + pieces :]
    n_grads = parts // 2 + 2 if parts > 1 else 1
    grad_outs = outs[:n_grads]
    keep_a, keep_b, send_out, sums_out, mixed, grad_proj, normed_grad = outs[n_grads : n_grads + 7]
    keep_out = (keep_a, keep_b)
    piece, mine_dp = lax.axis_index("tensor"), lax.axis_index("dp")
    second = doc_ref[doc_ref.shape[0] - 1]
    cols = heads * HDIM
    for at in range(pieces):
        mixed[pl.ds(pl.multiple_of((piece ^ at) * ROWS, ROWS), ROWS), :] = lows[at][...]
    weight_last = weight_ref[:, 3 * cols :]
    att_grad = dot(mixed[...], weight_last).astype(BF16)
    grad_last = dot(mixed[...], att_ref[...], TN)
    tiles = bias_tiles(rel_ref, piece * heads, heads)
    proj = proj_ref[...]
    length = proj.shape[0]
    blocks = length // BLOCK
    flipped = iota((BLOCK, BLOCK), 0) + iota((BLOCK, BLOCK), 1) == BLOCK - 1
    flipped = flipped.astype(F32).astype(BF16)
    wide = 2 * BLOCK
    lines = []
    grads_q, grads_k, grads_v = [], [], []
    for head in range(heads):
        at = head * HDIM
        key_sum = [jnp.zeros((BLOCK, HDIM), F32) for _ in range(blocks)]
        value_sum = [jnp.zeros((BLOCK, HDIM), F32) for _ in range(blocks)]
        near_sum = None
        query_done = []
        for block in reversed(range(blocks)):
            here = slice(block * BLOCK, (block + 1) * BLOCK)
            upto = slice(0, (block + 1) * BLOCK)
            query = proj[here, at : at + HDIM]
            keys = proj[upto, cols + at : cols + at + HDIM]
            values = proj[upto, 2 * cols + at : 2 * cols + at + HDIM]
            out_grad = att_grad[here, at : at + HDIM]
            scores = masked_scores(query, keys, tiles[head], second, block)
            again = jnp.exp(scores - lse_ref[here, head : head + 1])
            prob_grad = dot(out_grad, values, NT)
            weighted = again * prob_grad
            score_grad = weighted - again * jnp.sum(weighted, axis=1, keepdims=True)
            score_low = score_grad.astype(BF16)
            value_add = dot(again.astype(BF16), out_grad, TN)
            key_add = dot(score_low, query, TN)
            for other in range(block + 1):
                there = slice(other * BLOCK, (other + 1) * BLOCK)
                key_sum[other] = key_sum[other] + key_add[there, :]
                value_sum[other] = value_sum[other] + value_add[there, :]
            if block == 1:
                near_sum = score_grad
            else:
                near_sum = jnp.concatenate(
                    [near_sum[:, :BLOCK], near_sum[:, BLOCK:] + score_grad], axis=1
                )
            query_done.insert(0, dot(score_low, keys) * HDIM**-0.5)
        grads_q.append(jnp.concatenate(query_done, axis=0))
        grads_k.append(jnp.concatenate(key_sum, axis=0) * HDIM**-0.5)
        grads_v.append(jnp.concatenate(value_sum, axis=0))
        near_high = near_sum.astype(BF16)
        near_low = (near_sum - near_high.astype(F32)).astype(BF16)
        turned = dot(flipped, near_high) + dot(flipped, near_low)
        turned = pltpu.roll(turned, BLOCK + 1, 1, stride=1, stride_axis=0)
        lines.append(jnp.sum(turned, axis=0, keepdims=True))
    lines = jnp.concatenate(lines + [jnp.zeros((8 - heads, wide), F32)], axis=0)
    line_bucket = bucket_of((BLOCK - iota((wide, 128), 0)) & (wide - 1))
    spread = (line_bucket == iota((wide, 128), 1)).astype(F32)
    by_bucket = jnp.concatenate(
        [dot(lines, spread, precision=HIGHEST), jnp.zeros((8, HEADS * BUCKETS - 128), F32)], axis=1
    )
    bias_row = jnp.zeros((1, HEADS * BUCKETS), F32)
    for head in range(heads):
        placed = pltpu.roll(by_bucket, (piece * heads + head) * BUCKETS, 1)
        bias_row = bias_row + placed[head : head + 1, :]
    grad_proj[...] = jnp.concatenate(grads_q + grads_k + grads_v, axis=1).astype(BF16)
    x = row_ref[...].astype(F32)
    scale = lax.rsqrt(jnp.mean(x * x, axis=1, keepdims=True) + 1e-6)
    unit = x * scale
    normed = (unit * gain_ref[...]).astype(BF16)
    grad_first = dot(normed, grad_proj[...], TN)
    if parts > 1:
        grads = outs[n_grads + 7]
        depth = grad_first.shape[0] // parts
        grads[:, : 3 * cols] = grad_first
        grads[:, 3 * cols :] = grad_last
        for at in range(parts):
            piece_rows = grads[pl.ds(pl.multiple_of((mine_dp ^ at) * depth, 16), depth), :]
            if at % 2 == 0:
                grad_outs[at // 2][...] = piece_rows
            else:
                grad_outs[parts // 2 + (at == 1)][max(at // 2 - 1, 0)] = piece_rows.astype(BF16)
    else:
        grad_outs[0][:, : 3 * cols] = grad_first
        grad_outs[0][:, 3 * cols :] = grad_last
    normed_grad[...] = dot(grad_proj[...], weight_ref[:, : 3 * cols], NT)
    sums_out[...] = sums_ref[...]
    sums_out[experts + 1 : experts + 2, :] = jnp.sum(
        normed_grad[...] * unit, axis=0, keepdims=True
    )
    sums_out[experts + 2 : experts + 3, : HEADS * BUCKETS] = bias_row
    for at in range(pieces):
        mine = normed_grad[pl.ds(pl.multiple_of((piece ^ at) * ROWS, ROWS), ROWS), :]
        if at % 2 == 0:
            keep_out[at // 2][...] = mine
        else:
            send_out[at // 2 * ROWS : (at // 2 + 1) * ROWS, :] = mine.astype(BF16)
    put_sums(send_out, pieces // 2 * ROWS, sums_out[...])


def put_sums(out, start, sums):
    count = sums.shape[0]
    high = sums.astype(BF16)
    out[start : start + count, :] = high
    out[start + count : start + 2 * count, :] = (sums - high.astype(F32)).astype(BF16)


def get_sums(rows, start, count):
    return rows[start : start + count, :].astype(F32) + rows[
        start + count : start + 2 * count, :
    ].astype(F32)


def fold_back_kernel(keep_ref, near_ref, sums_ref, out_ref, sums_out):
    count = sums_ref.shape[0]
    out_ref[:ROWS, :] = (keep_ref[...] + near_ref[ROWS : 2 * ROWS, :].astype(F32)).astype(BF16)
    sums = sums_ref[...] + get_sums(near_ref, 2 * ROWS, count)
    sums_out[...] = sums
    put_sums(out_ref, ROWS, sums)


def join_kernel(sums_ref, far_ref, out_ref):
    out_ref[...] = sums_ref[...] + get_sums(far_ref, ROWS, sums_ref.shape[0])


def input_kernel(own_ref, gain_ref, mixed_grad_ref, part_ref, near_ref, far_ref, out_ref):
    x = own_ref[...].astype(F32)
    scale = lax.rsqrt(jnp.mean(x * x, axis=1, keepdims=True) + 1e-6)
    scaled = (
        part_ref[...] + near_ref[:ROWS, :].astype(F32) + far_ref[:ROWS, :].astype(F32)
    ) * gain_ref[...]
    cubed = scale * scale * scale
    own = scale * scaled - x * cubed * jnp.mean(scaled * x, axis=1, keepdims=True)
    out_ref[...] = (mixed_grad_ref[...] + own).astype(BF16)


def swap(value, axis, size, mask):
    return lax.ppermute(value, axis, [(i, i ^ mask) for i in range(size)])


def gather_weights(shard, senders):
    if senders != 8:
        return [lax.all_gather(shard, "dp", axis=0, tiled=True)]
    parts = {0: shard}
    parts[1] = swap(shard, "dp", senders, 1)
    for mask in (2, 4, 6):
        parts[mask] = swap(shard, "dp", senders, mask)
    for mask in (2, 4, 6):
        parts[mask + 1] = swap(parts[mask], "dp", senders, 1)
    return [parts[i] for i in range(senders)]


def fold_kernel(keep_ref, near_ref, out_ref):
    out_ref[...] = (keep_ref[...] + near_ref[...].astype(F32)).astype(BF16)


def fold(keep, near, name, after=()):
    return call(fold_kernel, [struct(near.shape, BF16)], [], [keep, near], name=name, after=after)[0]


def finish_kernel(cols, keep_ref, near_ref, one_ref, two_ref, three_ref, first_ref, last_ref):
    total = keep_ref[...] + near_ref[...].astype(F32)
    for part in (one_ref, two_ref, three_ref):
        total = total + part[...].astype(F32)
    for at in range(3):
        first_ref[at] = total[:, at * cols : (at + 1) * cols]
    last_ref[...] = total[:, 3 * cols :]


def fold_three_kernel(one_ref, two_ref, three_ref, near_ref, *outs):
    for at, (keep, out) in enumerate(zip((one_ref, two_ref, three_ref), outs)):
        out[...] = (keep[...] + near_ref[at].astype(F32)).astype(BF16)


def finish_kernel(cols, keep_ref, near_ref, one_ref, two_ref, three_ref, first_ref, last_ref):
    total = keep_ref[...] + near_ref[...].astype(F32)
    for part in (one_ref, two_ref, three_ref):
        total = total + part[...].astype(F32)
    for at in range(3):
        first_ref[at] = total[:, at * cols : (at + 1) * cols]
    last_ref[...] = total[:, 3 * cols :]


def fold_two_kernel(one_ref, two_ref, near_ref, one_out, two_out):
    one_out[...] = (one_ref[...] + near_ref[0].astype(F32)).astype(BF16)
    two_out[...] = (two_ref[...] + near_ref[1].astype(F32)).astype(BF16)


def finish_kernel(cols, keep_ref, near_ref, one_ref, two_ref, three_ref, first_ref, last_ref):
    total = keep_ref[...] + near_ref[0].astype(F32)
    for part in (one_ref, two_ref, three_ref):
        total = total + part[...].astype(F32)
    for at in range(3):
        first_ref[at] = total[:, at * cols : (at + 1) * cols]
    last_ref[...] = total[:, 3 * cols :]


def add_kernel(one_ref, two_ref, out_ref, low_ref):
    total = one_ref[...] + two_ref[...]
    out_ref[...] = total
    low_ref[...] = total.astype(BF16)


def sums_kernel(experts, *refs):
    *parts, gains_ref, bias_ref, router_ref = refs
    total = parts[0][...]
    for part in parts[1:]:
        total = total + part[...].astype(F32)
    router_ref[...] = total[:experts]
    gains_ref[0:2, :] = total[experts : experts + 2]
    for head in range(HEADS):
        bias_ref[head : head + 1, :] = total[
            experts + 2 : experts + 3, head * BUCKETS : (head + 1) * BUCKETS
        ]


def add(one, two, after):
    return call(
        add_kernel,
        [struct(one.shape, F32), struct(one.shape, BF16)],
        [],
        [one, two],
        name="add_sums",
        prompt=True,
        after=after,
    )


def last_sums(grads, keep_a, keep_b, near, sums, senders, pieces, cols, experts):
    count, width = sums.shape
    if senders == 8:
        near_grads = swap(grads[4], "dp", senders, 1)
        near_last = swap(grads[5], "dp", senders, 1)
    other, sums = call(
        fold_back_kernel,
        [struct((ROWS + 2 * count, width), BF16), struct((count, width), F32)],
        [],
        [keep_b, near, sums],
        name="fold_rows",
        prompt=True,
    )
    far = swap(other, "tensor", pieces, 2)
    (sums,) = call(
        join_kernel, [struct((count, width), F32)], [], [sums, far], name="join", prompt=True
    )
    if senders != 8:
        total = lax.psum_scatter(grads[0], "dp", scatter_dimension=0, tiled=True)
        first = jnp.stack([total[:, at * cols : (at + 1) * cols] for at in range(3)])
        weight_sums = (first, total[:, 3 * cols :])
        sums = [lax.psum(sums, "dp")]
    else:
        got = swap(sums, "dp", senders, 1)
        folded = call(
            fold_three_kernel,
            [struct(grads[0].shape, BF16)] * 3,
            [],
            [grads[1], grads[2], grads[3], near_grads],
            name="fold_weights",
            prompt=True,
            after=[sums],
        )
        arrived = [swap(folded[at], "dp", senders, 2 * at + 2) for at in (2, 1, 0)]
        sums, low = add(sums, got, [folded[0]])
        sums = [sums] + [swap(low, "dp", senders, mask) for mask in (6, 4, 2)]
        depth = grads[0].shape[0]
        weight_sums = call(
            functools.partial(finish_kernel, cols),
            [struct((3, depth, cols), F32), struct((depth, cols), F32)],
            [],
            [grads[0], near_last] + arrived,
            name="finish",
            prompt=True,
        )
    width = sums[0].shape[1]
    small = call(
        functools.partial(sums_kernel, experts),
        [
            struct((8, width), F32),
            struct((HEADS, BUCKETS), F32),
            struct((experts, width), F32),
        ],
        [],
        sums,
        name="sums", prompt=True,
    )
    return weight_sums, (keep_a, near, far), small


def scatter_rows(keep_a, keep_b, near, pieces, after=()):
    other = call(
        lambda keep, got, out: fold_kernel(keep, got.at[1], out),
        [struct(keep_b.shape, BF16)],
        [],
        [keep_b, near],
        name="fold_rows", prompt=True,
        after=after,
    )[0]
    return keep_a, near, swap(other, "tensor", pieces, 2), other


def gather_rows(rows, pieces):
    far = swap(rows, "tensor", pieces, 2)
    near = swap(rows, "tensor", pieces, 1)
    last = swap(far, "tensor", pieces, 1)
    return [rows, near, far, last]


def exchange(blocks, senders, capacity):
    rows, width = blocks.shape
    return lax.all_to_all(
        blocks.reshape(senders, capacity, width), "dp", split_axis=0, concat_axis=0, tiled=True
    ).reshape(rows, width)


def body(
    tokens,
    doc_start,
    routes,
    gain_attn,
    w_qkv,
    w_out,
    rel_bias,
    gain_ffn,
    router,
    w_in,
    w_exp_out,
    out_grad,
):
    pieces = lax.axis_size("tensor")
    senders = lax.axis_size("dp")
    tok_dev, width = tokens.shape
    routes, rel_bias, router = routes.T, rel_bias.T, router.T
    length = tok_dev * pieces
    experts = router.shape[0]
    capacity = max(2, 3 * tok_dev * routes.shape[0] // (2 * experts))
    slots = experts * capacity
    heads = w_out.shape[1] // HDIM
    cols = heads * HDIM
    gain_one = gain_attn.reshape(1, width)
    gain_two = gain_ffn.reshape(1, width)

    shard, in_head = call(
        pack_kernel,
        [
            struct((w_out.shape[0], 4 * cols), BF16),
            struct((width // 3, w_in.shape[2]), BF16),
        ],
        [],
        [w_qkv.transpose(1, 0, 2), w_out, w_in[0]],
        name="pack",
        held=(0, 1, 2),
        parts={2: (width // 3, w_in.shape[2])},
    )
    weights = gather_weights(shard, senders)
    rows = gather_rows(tokens, pieces)
    out_one = w_exp_out[0]
    in_one = w_in[0]
    out_two = swap(out_one, "tensor", pieces, 2)
    in_two_a = swap(in_head, "tensor", pieces, 2)
    in_two_b = swap(in_one[in_head.shape[0] :], "tensor", pieces, 2)

    slot, grad_out = call(
        functools.partial(slots_kernel, capacity),
        [struct((tok_dev, 128), jnp.int32), struct((slots, width), BF16)],
        [],
        [routes, out_grad],
        flops=2 * slots * tok_dev * width,
        name="slots",
        held=(1,),
        kept=(0, 1),
    )

    grad_out = once(grad_out, weights[1::2], "gathered")
    whole_weight, whole_rows, projected, attended, lse, keep_a, keep_b, send = call(
        functools.partial(forward_kernel, len(weights), pieces, heads),
        [
            struct((width, 4 * cols), BF16),
            struct((length, width), BF16),
            struct((length, 3 * cols), BF16),
            struct((length, cols), BF16),
            struct((length, 128), F32),
            struct((tok_dev, width), F32),
            struct((tok_dev, width), F32),
            struct((pieces // 2, tok_dev, width), BF16),
        ],
        [],
        [doc_start, rel_bias] + weights + rows + [gain_one],
        smem=2,
        flops=2 * length * width * 4 * cols + 4 * heads * length * length * HDIM,
        name="attend",
        held=tuple(range(2, 2 + len(weights))),
        kept=(0, 1, 2, 3, 4),
        vmem=12,
    )
    pull_own = exchange(grad_out, senders, capacity)
    pull_mate = swap(pull_own, "tensor", pieces, 1)
    far_pull_own = swap(pull_own, "tensor", pieces, 2)

    near = swap(send, "tensor", pieces, 1)
    part, near, far, _ = scatter_rows(keep_a, keep_b, near, pieces, [out_two, in_two_a])
    mixed, normed_two, gates, outgoing = call(
        dispatch_kernel,
        [
            struct((tok_dev, width), F32),
            struct((tok_dev, width), BF16),
            struct((tok_dev, 128), F32),
            struct((slots, width + GATE_LANES), BF16),
        ],
        [],
        [tokens, part, near, far, gain_two, router, routes, slot],
        flops=2 * slots * tok_dev * width,
        name="dispatch",
        after=[pull_own],
        kept=(0, 1, 2),
    )
    slot_own = exchange(outgoing, senders, capacity)
    slot_mate = swap(slot_own, "tensor", pieces, 1)
    payload = width + GATE_LANES
    units = in_one.shape[1]
    expert_flops = 12 * slots * width * units
    hidden_one, pre_one, row_total, gate_total = call(
        own_slice_kernel,
        [struct((2 * slots, units), BF16)] * 2
        + [struct((2 * slots, width), F32), struct((2 * slots, GATE_LANES), F32)],
        [pltpu.VMEM((2 * slots, width), BF16)] * 2,
        [slot_own, slot_mate, pull_own, pull_mate, in_one, out_one],
        flops=expert_flops,
        name="own_slice",
        prompt=True,
        held=(4, 5),
        kept=(0, 1),
        vmem=18,
    )
    hidden_two, row_keep, row_send = call(
        far_slice_kernel,
        [
            struct((2 * slots, units), BF16),
            struct((slots, payload), F32),
            struct((slots, payload), BF16),
        ],
        [pltpu.VMEM((width, units), BF16), pltpu.VMEM((2 * slots, units), BF16)]
        + [pltpu.VMEM((2 * slots, width), BF16)] * 2,
        [slot_own, slot_mate, pull_own, pull_mate, in_two_a, in_two_b, out_two, row_total, gate_total],
        flops=expert_flops,
        name="far_slice",
        prompt=True,
        held=(4, 5, 6),
        kept=(0,),
        vmem=20,
    )
    row_mate = swap(row_send, "tensor", pieces, 1)
    far_own = swap(slot_own, "tensor", pieces, 2)
    (row_out,) = call(
        merge_kernel,
        [struct((slots, payload), BF16)],
        [],
        [row_keep, row_mate],
        name="merge",
    )
    back = exchange(row_out, senders, capacity)

    far_mate = swap(far_own, "tensor", pieces, 1)
    out_keep, out_send = call(
        expert_out_kernel,
        [struct((slots, width), F32), struct((slots, width), BF16)],
        [],
        [hidden_one, hidden_two, out_one, out_two],
        flops=4 * 2 * slots * width * in_one.shape[1],
        name="expert_out",
        held=(0, 1, 2, 3),
        after=[far_own],
        vmem=10,
    )
    turned = [pltpu.VMEM((width, 2 * slots), BF16), pltpu.VMEM((2 * slots, width), BF16)]
    grads_both = [struct(in_one.shape, F32), struct(out_one.shape, F32), struct((8, 128), F32)]
    own_in, own_out, own_graded = call(
        own_grads_kernel,
        grads_both,
        turned,
        [slot_own, slot_mate, pull_own, pull_mate, hidden_one, pre_one],
        flops=8 * slots * width * units,
        name="own_grads",
        after=[out_send],
        held=(0, 1, 2, 3, 4, 5),
        vmem=24,
    )
    far_pull_own = once(far_pull_own, [own_graded], "pulled")
    far_pull_mate = swap(far_pull_own, "tensor", pieces, 1)
    grad_in, grad_out_sum, graded = call(
        far_grads_kernel,
        grads_both,
        turned + [pltpu.VMEM((2 * slots, width), BF16)],
        [far_own, far_mate, far_pull_own, far_pull_mate, in_one, out_one, own_in, own_out],
        flops=16 * slots * width * units,
        name="far_grads",
        held=(4, 5),
        vmem=30,
    )

    sum_rows = -(-(experts + 3) // 8) * 8
    mixed_grad, mixed_low, sums_two = call(
        combine_kernel,
        [
            struct((tok_dev, width), F32),
            struct((tok_dev, width), BF16),
            struct((sum_rows, width), F32),
        ],
        [],
        [back, slot, gates, mixed, normed_two, router, routes, out_grad, gain_two],
        flops=2 * slots * tok_dev * width,
        name="combine",
        after=[graded],
        held=(1, 2, 3, 4, 7),
    )
    expert_out = fold(out_keep, swap(out_send, "tensor", pieces, 1), "fold_out", [mixed_low])
    returned = exchange(expert_out, senders, capacity)
    (result,) = call(
        result_kernel,
        [struct((tok_dev, width), BF16)],
        [],
        [returned, slot, gates, mixed],
        flops=4 * slots * tok_dev * width,
        name="result", prompt=True,
        held=(1, 2, 3),
    )

    lows = gather_rows(mixed_low, pieces)
    parts = len(weights)
    if parts > 1:
        depth = width // parts
        grad_shapes = [struct((depth, 4 * cols), F32)] * (parts // 2)
        grad_shapes += [struct((n, depth, 4 * cols), BF16) for n in (parts // 2 - 1, 1)]
        grad_scratch = [pltpu.VMEM((width, 4 * cols), F32)]
    else:
        grad_shapes = [struct((width, 4 * cols), F32)]
        grad_scratch = []
    *weight_grads, keep_a, keep_b, send, sums = call(
        functools.partial(backward_kernel, parts, pieces, heads, experts),
        grad_shapes
        + [
            struct((tok_dev, width), F32),
            struct((tok_dev, width), F32),
            struct((pieces // 2 * tok_dev + 2 * sum_rows, width), BF16),
            struct((sum_rows, width), F32),
        ],
        [
            pltpu.VMEM((length, width), BF16),
            pltpu.VMEM((length, 3 * cols), BF16),
            pltpu.VMEM((length, width), F32),
        ]
        + grad_scratch,
        [doc_start, rel_bias]
        + lows
        + [whole_weight, whole_rows, projected, attended, lse, gain_one, sums_two],
        smem=2,
        name="attend_back",
        prompt=True,
        held=tuple(range(2 + pieces, 7 + pieces)),
        vmem=16,
    )
    near = swap(send, "tensor", pieces, 1)
    (first_sum, last_sum), (part, near, far), (gains, bias_grad, router_grad) = last_sums(
        weight_grads, keep_a, keep_b, near, sums, senders, pieces, cols, experts
    )
    (input_grad,) = call(
        input_kernel,
        [struct((tok_dev, width), BF16)],
        [],
        [tokens, gain_one, mixed_grad, part, near, far],
        name="input_grad", prompt=True,
        held=(0, 2),
    )
    return (
        result,
        input_grad,
        gains[1],
        first_sum.transpose(1, 0, 2),
        last_sum,
        bias_grad.T,
        gains[0],
        router_grad.T,
        grad_in[None],
        grad_out_sum[None],
    )


def solution(mesh):
    in_specs = (
        P(("dp", "tensor"), None),
        P("dp"),
        P(("dp", "tensor"), None),
        P(),
        P("dp", None, "tensor"),
        P("dp", "tensor"),
        P(),
        P(),
        P(),
        P("dp", None, "tensor"),
        P("dp", "tensor", None),
        P(("dp", "tensor"), None),
    )
    out_specs = (
        P(("dp", "tensor"), None),
        P(("dp", "tensor"), None),
        P(),
        P("dp", None, "tensor"),
        P("dp", "tensor"),
        P(),
        P(),
        P(),
        P("dp", None, "tensor"),
        P("dp", "tensor", None),
    )
    return jax.shard_map(body, mesh=mesh, in_specs=in_specs, out_specs=out_specs, check_vma=False)
```

```python
import functools

import jax
import jax.numpy as jnp
import numpy as np
from jax import lax
from jax.experimental import pallas as pl
from jax.experimental.pallas import tpu as pltpu
from jax.sharding import PartitionSpec as P

HEADS = 12
HDIM = 64
BUCKETS = 32
ROWS = 128
BLOCK = 256
GATE_LANES = 128

LIMITS = np.array([19, 21, 24, 27, 31, 35, 40, 46, 52, 59, 67, 77, 87, 99, 113], np.int32)
HIGHEST = lax.Precision.HIGHEST
F32 = jnp.float32
BF16 = jnp.bfloat16
MIB = 1024 * 1024

NN = (((1,), (0,)), ((), ()))
NT = (((1,), (1,)), ((), ()))
TN = (((0,), (0,)), ((), ()))


def dot(left, right, dims=NN, precision=None):
    return lax.dot_general(left, right, dims, preferred_element_type=F32, precision=precision)


def iota(shape, axis):
    return lax.broadcasted_iota(jnp.int32, shape, axis)


def bucket_of(distance):
    bucket = jnp.minimum(distance, 16)
    for limit in LIMITS:
        bucket = bucket + (distance >= int(limit)).astype(jnp.int32)
    return bucket


def in_three(value):
    high = value.astype(BF16)
    rest = value - high.astype(F32)
    middle = rest.astype(BF16)
    low = (rest - middle.astype(F32)).astype(BF16)
    return high, middle, low


def three_lanes(value):
    high, middle, low = in_three(value)
    lane = iota((value.shape[0], GATE_LANES), 1)
    zero = jnp.zeros((value.shape[0], GATE_LANES), F32)
    spread = jnp.where(
        lane == 0,
        high.astype(F32),
        jnp.where(lane == 1, middle.astype(F32), jnp.where(lane == 2, low.astype(F32), zero)),
    )
    return spread.astype(BF16)


def lanes_sum(lanes):
    return jnp.sum(lanes.astype(F32), axis=1, keepdims=True)


def pick(columns, at):
    return columns[:, at : at + 1]


def call(
    kernel,
    outs,
    scratch,
    args,
    smem=0,
    flops=0,
    name=None,
    after=(),
    vmem=6,
    held=(),
    kept=(),
    passed=(),
    prompt=False,
    parts={},
):
    n_in, n_after, n_out = len(args), len(after), len(outs)
    n_pass = len(passed)

    def run(*refs):
        ins, rest = refs[:n_in], refs[n_in + n_after + n_pass :]
        kernel(*ins, *rest[:n_out], *rest[n_out + n_pass :])

    def whole(a):
        shape = getattr(a, "shape", a)
        return pl.BlockSpec(shape, lambda i: (0,) * len(shape))

    moved = sum(a.size * a.dtype.itemsize for a in list(args) + list(outs))
    args = [
        pltpu.with_memory_space_constraint(a, pltpu.HBM) if at in held else a
        for at, a in enumerate(args)
    ]
    after = [
        pltpu.with_memory_space_constraint(a, pltpu.HBM) if a.size > 1 << 18 else a for a in after
    ]
    out_shape = [
        pltpu.HBM(o.shape, o.dtype) if at in kept else jax.ShapeDtypeStruct(o.shape, o.dtype)
        for at, o in enumerate(outs)
    ]
    return pl.pallas_call(
        run,
        grid=(1,),
        out_shape=out_shape + [jax.ShapeDtypeStruct(o.shape, o.dtype) for o in passed],
        in_specs=[pl.BlockSpec(memory_space=pltpu.SMEM)] * smem
        + [whole(parts.get(smem + at, a)) for at, a in enumerate(args[smem:])]
        + [pl.BlockSpec(memory_space=pl.ANY)] * (n_after + n_pass),
        out_specs=[whole(o) for o in outs] + [pl.BlockSpec(memory_space=pl.ANY)] * n_pass,
        scratch_shapes=scratch,
        input_output_aliases={n_in + n_after + at: n_out + at for at in range(n_pass)},
        compiler_params=pltpu.CompilerParams(vmem_limit_bytes=vmem * MIB),
        cost_estimate=pl.CostEstimate(
            flops=1 if prompt else flops,
            bytes_accessed=1 if prompt else moved,
            transcendentals=0,
        ),
        name=name,
    )(*args, *after, *passed)


def once(value, after, name):
    return call(lambda: None, [], [], [], name=name, after=after, passed=[value])[0]


def columns_of(turned):
    filled = jnp.concatenate(
        [turned.astype(F32), jnp.zeros((8 - turned.shape[0], turned.shape[1]), F32)], axis=0
    )
    return filled.T.astype(jnp.int32)


def pack_kernel(first_ref, last_ref, in_ref, out_ref, head_ref):
    head_ref[...] = in_ref[...]
    cols = last_ref.shape[1]
    for at in range(3):
        out_ref[:, at * cols : (at + 1) * cols] = first_ref[at]
    out_ref[:, 3 * cols :] = last_ref[...]


def struct(shape, dtype):
    return jax.ShapeDtypeStruct(shape, dtype)


def slots_kernel(capacity, routes_ref, grad_ref, slot_ref, out_ref):
    tokens = routes_ref.shape[1]
    slots = out_ref.shape[0]
    experts = slots // capacity
    routes = columns_of(routes_ref[...])
    first, second = routes[:, 0:1], routes[:, 1:2]
    lane = iota((tokens, experts), 1)
    one_first = (first == lane).astype(F32)
    one_second = (second == lane).astype(F32)
    member = (one_first + one_second).astype(BF16)
    below = (iota((tokens, tokens), 1) < iota((tokens, tokens), 0)).astype(F32).astype(BF16)
    earlier = dot(below, member)
    slot_first = first * capacity + jnp.sum(one_first * earlier, axis=1, keepdims=True).astype(
        jnp.int32
    )
    slot_second = second * capacity + jnp.sum(one_second * earlier, axis=1, keepdims=True).astype(
        jnp.int32
    )
    wide = iota((tokens, 128), 1)
    slot_ref[...] = jnp.where(wide == 0, slot_first, slot_second)
    places = iota((tokens, slots), 1)
    chosen = ((slot_first == places) | (slot_second == places)).astype(F32).astype(BF16)
    out_ref[...] = dot(chosen, grad_ref[...], TN).astype(BF16)


def bias_tiles(rel_ref, first_head, heads):
    wide = 2 * BLOCK
    distance = (BLOCK - iota((8, wide), 1)) & (wide - 1)
    bucket = bucket_of(distance)
    tiles = []
    for head in range(heads):
        line = jnp.zeros((8, wide), F32)
        for b in range(BUCKETS):
            line = jnp.where(bucket == b, rel_ref[first_head + head, b], line)
        grid = jnp.broadcast_to(line[0:1, :], (BLOCK, wide))
        tiles.append(pltpu.roll(grid, 0, 1, stride=1, stride_axis=0))
    return tiles


def masked_scores(query, keys, tile, second, block):
    width = (block + 1) * BLOCK
    raw = dot(query, keys, NT) * HDIM**-0.5
    bias = tile[:, 2 * BLOCK - width :]
    column = iota((BLOCK, width), 1)
    row = iota((BLOCK, width), 0) + block * BLOCK
    starts = jnp.where(row >= second, second, 0)
    allowed = (column <= row) & (column >= starts)
    return jnp.where(allowed, raw + bias, -1e9)


def forward_kernel(parts, pieces, heads, *refs):
    doc_ref, rel_ref = refs[:2]
    weights = refs[2 : 2 + parts]
    rows = refs[2 + parts : 2 + parts + pieces]
    gain_ref = refs[2 + parts + pieces]
    weight_out, row_out, proj_out, att_out, lse_out, keep_a, keep_b, send_out = refs[
        3 + parts + pieces :
    ]
    keep_out = (keep_a, keep_b)
    piece, mine_dp = lax.axis_index("tensor"), lax.axis_index("dp")
    second = doc_ref[doc_ref.shape[0] - 1]
    cols = heads * HDIM
    for at in range(parts):
        depth = weights[at].shape[0]
        start = (mine_dp ^ at) * depth if parts > 1 else 0
        weight_out[pl.ds(pl.multiple_of(start, 16), depth), :] = weights[at][...]
    for at in range(pieces):
        row_out[pl.ds(pl.multiple_of((piece ^ at) * ROWS, ROWS), ROWS), :] = rows[at][...]
    x = row_out[...].astype(F32)
    scale = lax.rsqrt(jnp.mean(x * x, axis=1, keepdims=True) + 1e-6)
    normed = (x * scale * gain_ref[...]).astype(BF16)
    proj_out[...] = dot(normed, weight_out[:, : 3 * cols]).astype(BF16)
    tiles = bias_tiles(rel_ref, piece * heads, heads)
    blocks = x.shape[0] // BLOCK
    proj = proj_out[...]
    wide = iota((BLOCK, 128), 1)
    for block in range(blocks):
        here = slice(block * BLOCK, (block + 1) * BLOCK)
        upto = slice(0, (block + 1) * BLOCK)
        done = []
        kept = jnp.zeros((BLOCK, 128), F32)
        for head in range(heads):
            at = head * HDIM
            query = proj[here, at : at + HDIM]
            keys = proj[upto, cols + at : cols + at + HDIM]
            values = proj[upto, 2 * cols + at : 2 * cols + at + HDIM]
            scores = masked_scores(query, keys, tiles[head], second, block)
            peak = jnp.max(scores, axis=1, keepdims=True)
            shifted = jnp.exp(scores - peak)
            total = jnp.sum(shifted, axis=1, keepdims=True)
            attention = (shifted * (1.0 / total)).astype(BF16)
            done.append(dot(attention, values).astype(BF16))
            kept = jnp.where(wide == head, peak + jnp.log(total), kept)
        att_out[here, :] = jnp.concatenate(done, axis=1)
        lse_out[here, :] = kept
    weight_last = weight_out[:, 3 * cols :]
    for at in range(pieces):
        mine = att_out[pl.ds(pl.multiple_of((piece ^ at) * ROWS, ROWS), ROWS), :]
        product = dot(mine, weight_last, NT)
        if at % 2 == 0:
            keep_out[at // 2][...] = product
        else:
            send_out[at // 2] = product.astype(BF16)


def dispatch_kernel(
    own_ref,
    part_ref,
    near_ref,
    far_ref,
    gain_ref,
    router_ref,
    routes_ref,
    slot_ref,
    mixed_ref,
    normed_ref,
    gates_ref,
    out_ref,
):
    width = own_ref.shape[1]
    tokens = own_ref.shape[0]
    slots = out_ref.shape[0]
    mixed = own_ref[...].astype(F32) + (
        part_ref[...] + near_ref[0].astype(F32) + far_ref[...].astype(F32)
    )
    mixed_ref[...] = mixed
    scale = lax.rsqrt(jnp.mean(mixed * mixed, axis=1, keepdims=True) + 1e-6)
    normed = (mixed * scale * gain_ref[...]).astype(BF16)
    normed_ref[...] = normed
    logits = dot(normed, router_ref[...], NT)
    routes = columns_of(routes_ref[...])
    lane = iota(logits.shape, 1)
    one = jnp.sum(jnp.where(routes[:, 0:1] == lane, logits, 0.0), axis=1, keepdims=True)
    two = jnp.sum(jnp.where(routes[:, 1:2] == lane, logits, 0.0), axis=1, keepdims=True)
    peak = jnp.maximum(one, two)
    one, two = jnp.exp(one - peak), jnp.exp(two - peak)
    total = one + two
    one, two = one / total, two / total
    wide = iota((tokens, 128), 1)
    gates_ref[...] = jnp.where(wide == 0, one, two)
    places = iota((tokens, slots), 1)
    slot = slot_ref[...]
    first = (slot[:, 0:1] == places).astype(F32).astype(BF16)
    second = (slot[:, 1:2] == places).astype(F32).astype(BF16)
    out_ref[:, :width] = dot(first + second, normed, TN).astype(BF16)
    gate_slots = dot(first, three_lanes(one), TN) + dot(second, three_lanes(two), TN)
    out_ref[:, width:] = gate_slots.astype(BF16)


def gelu_and_slope(x):
    inner = 0.7978845608028654 * (x + 0.044715 * (x * x * x))
    bend = jnp.tanh(inner)
    half = 0.5 * (1.0 + bend)
    slope = half + 0.5 * x * (1.0 - bend * bend) * (
        0.7978845608028654 * (1.0 + 3 * 0.044715 * (x * x))
    )
    return x * half, slope


def gather_sides(sources, pulls, rows_all, pulls_all):
    rows, width = pulls[0].shape
    gates = []
    for at, (source, pull) in enumerate(zip(sources, pulls)):
        here = slice(at * rows, (at + 1) * rows)
        rows_all[here, :] = source[:, :width]
        pulls_all[here, :] = pull[...]
        gates.append(lanes_sum(source[:, width:]))
    return jnp.concatenate(gates, axis=0)


def through_slice(rows_all, pulls_all, gate, in_ref, out_ref, hidden_out, pre_out):
    hidden_units = in_ref.shape[1]
    tile = 256
    gate_wide = jnp.zeros((rows_all.shape[0], tile), F32)
    for at in range(0, hidden_units, tile):
        there = slice(at, at + tile)
        pulled = dot(pulls_all[...], out_ref[there, :], NT)
        hidden, slope = gelu_and_slope(dot(rows_all[...], in_ref[:, there]))
        hidden = hidden.astype(BF16)
        hidden_out[:, there] = hidden
        pre_out[:, there] = (pulled * gate * slope).astype(BF16)
        gate_wide = gate_wide + hidden.astype(F32) * pulled
    return jnp.sum(gate_wide, axis=1, keepdims=True)


def own_slice_kernel(
    own_ref,
    mate_ref,
    pull_own,
    pull_mate,
    in_ref,
    out_ref,
    hidden_ref,
    pre_ref,
    total_ref,
    sum_ref,
    rows_all,
    pulls_all,
):
    gate = gather_sides((own_ref, mate_ref), (pull_own, pull_mate), rows_all, pulls_all)
    gate_sum = through_slice(rows_all, pulls_all, gate, in_ref, out_ref, hidden_ref, pre_ref)
    sum_ref[...] = jnp.broadcast_to(gate_sum, sum_ref.shape)
    total_ref[...] = dot(pre_ref[...], in_ref[...], NT)


def far_slice_kernel(
    own_ref,
    mate_ref,
    pull_own,
    pull_mate,
    in_a_ref,
    in_b_ref,
    out_ref,
    total_ref,
    sum_ref,
    hidden_ref,
    keep_ref,
    send_ref,
    in_ref,
    pre_ref,
    rows_all,
    pulls_all,
):
    rows, width = pull_own.shape
    split = in_a_ref.shape[0]
    in_ref[:split, :] = in_a_ref[...]
    in_ref[split:, :] = in_b_ref[...]
    gate = gather_sides((own_ref, mate_ref), (pull_own, pull_mate), rows_all, pulls_all)
    gate_sum = sum_ref[:, 0:1] + through_slice(
        rows_all, pulls_all, gate, in_ref, out_ref, hidden_ref, pre_ref
    )
    total = total_ref[...] + dot(pre_ref[...], in_ref[...], NT)
    keep_ref[:, :width] = total[:rows, :]
    keep_ref[:, width:] = jnp.broadcast_to(gate_sum[:rows], (rows, GATE_LANES))
    send_ref[:, :width] = total[rows:, :].astype(BF16)
    send_ref[:, width:] = three_lanes(gate_sum[rows:])


def turn_slots(sources, pulls, rows_turned, pulls_all, rows_all=None):
    rows, width = pulls[0].shape
    for at, (source, pull) in enumerate(zip(sources, pulls)):
        here = slice(at * rows, (at + 1) * rows)
        rows_turned[:, here] = source[:, :width].T
        gate = lanes_sum(source[:, width:])
        pulls_all[here, :] = (gate * pull[...].astype(F32)).astype(BF16)
        if rows_all is not None:
            rows_all[here, :] = source[:, :width]


def own_grads_kernel(
    own_ref,
    mate_ref,
    pull_own,
    pull_mate,
    hidden_ref,
    pre_ref,
    grad_in,
    grad_out,
    token_ref,
    rows_turned,
    pulls_all,
):
    token_ref[...] = jnp.zeros_like(token_ref)
    turn_slots((own_ref, mate_ref), (pull_own, pull_mate), rows_turned, pulls_all)
    tile = 256
    for unit in range(0, hidden_ref.shape[1], tile):
        there = slice(unit, unit + tile)
        grad_in[:, there] = dot(rows_turned[...], pre_ref[:, there])
        grad_out[there, :] = dot(hidden_ref[:, there], pulls_all[...], TN)


def far_grads_kernel(
    own_ref,
    mate_ref,
    pull_own,
    pull_mate,
    in_ref,
    out_ref,
    own_in,
    own_out,
    grad_in,
    grad_out,
    token_ref,
    rows_turned,
    pulls_all,
    rows_all,
):
    token_ref[...] = jnp.zeros_like(token_ref)
    turn_slots((own_ref, mate_ref), (pull_own, pull_mate), rows_turned, pulls_all, rows_all)
    tile = 256
    for unit in range(0, in_ref.shape[1], tile):
        there = slice(unit, unit + tile)
        hidden, slope = gelu_and_slope(dot(rows_all[...], in_ref[:, there]))
        pulled = dot(pulls_all[...], out_ref[there, :], NT)
        pre_grad = (pulled * slope).astype(BF16)
        grad_in[:, there] = own_in[:, there] + dot(rows_turned[...], pre_grad)
        grad_out[there, :] = own_out[there, :] + dot(hidden.astype(BF16), pulls_all[...], TN)


def expert_out_kernel(hidden_one, hidden_two, out_one, out_two, keep_ref, send_ref):
    rows = keep_ref.shape[0]
    product = dot(hidden_one[...], out_one[...]) + dot(hidden_two[...], out_two[...])
    keep_ref[...] = product[:rows]
    send_ref[...] = product[rows:].astype(BF16)


def merge_kernel(keep_ref, mate_ref, out_ref):
    width = keep_ref.shape[1] - GATE_LANES
    out_ref[:, :width] = (keep_ref[:, :width] + mate_ref[:, :width].astype(F32)).astype(BF16)
    gate = keep_ref[:, width : width + 1] + lanes_sum(mate_ref[:, width:])
    out_ref[:, width:] = three_lanes(gate)


def combine_kernel(
    back_ref,
    slot_ref,
    gates_ref,
    mixed_ref,
    normed_ref,
    router_ref,
    routes_ref,
    grad_ref,
    gain_ref,
    mixed_grad_ref,
    low_ref,
    sums_ref,
):
    tokens, width = grad_ref.shape
    slots = back_ref.shape[0]
    experts = router_ref.shape[0]
    places = iota((tokens, slots), 1)
    slot = slot_ref[...]
    first = (slot[:, 0:1] == places).astype(F32).astype(BF16)
    second = (slot[:, 1:2] == places).astype(F32).astype(BF16)
    lanes = back_ref[:, width:]
    pull_one = jnp.sum(dot(first, lanes), axis=1, keepdims=True)
    pull_two = jnp.sum(dot(second, lanes), axis=1, keepdims=True)
    one, two = gates_ref[:, 0:1], gates_ref[:, 1:2]
    mean_pull = one * pull_one + two * pull_two
    delta_one = one * (pull_one - mean_pull)
    delta_two = two * (pull_two - mean_pull)
    routes = columns_of(routes_ref[...])
    lane = iota((tokens, experts), 1)
    logit_grad = jnp.where(routes[:, 0:1] == lane, delta_one, 0.0) + jnp.where(
        routes[:, 1:2] == lane, delta_two, 0.0
    )
    high = logit_grad.astype(BF16)
    low = (logit_grad - high.astype(F32)).astype(BF16)
    normed = normed_ref[...]
    router = router_ref[...]
    normed_grad = dot(first + second, back_ref[:, :width]) + (
        dot(high, router) + dot(low, router)
    )
    mixed = mixed_ref[...]
    grad = grad_ref[...].astype(F32)
    scale = lax.rsqrt(jnp.mean(mixed * mixed, axis=1, keepdims=True) + 1e-6)
    scaled = normed_grad * gain_ref[...]
    cubed = scale * scale * scale
    mixed_grad = (
        grad
        + scale * scaled
        - mixed * cubed * jnp.mean(scaled * mixed, axis=1, keepdims=True)
    )
    mixed_grad_ref[...] = mixed_grad
    low_ref[...] = mixed_grad.astype(BF16)
    sums_ref[...] = jnp.zeros_like(sums_ref)
    sums_ref[:experts, :] = dot(high, normed, TN) + dot(low, normed, TN)
    sums_ref[experts : experts + 1, :] = jnp.sum(
        normed_grad * mixed * scale, axis=0, keepdims=True
    )


def result_kernel(back_ref, slot_ref, gates_ref, mixed_ref, out_ref, token_ref):
    token_ref[...] = jnp.zeros_like(token_ref)
    tokens = mixed_ref.shape[0]
    slots = back_ref.shape[0]
    places = iota((tokens, slots), 1)
    slot = slot_ref[...]
    first = (slot[:, 0:1] == places).astype(F32).astype(BF16)
    second = (slot[:, 1:2] == places).astype(F32).astype(BF16)
    back = back_ref[...]
    added = gates_ref[:, 0:1] * dot(first, back) + gates_ref[:, 1:2] * dot(second, back)
    out_ref[...] = (mixed_ref[...] + added).astype(BF16)


def backward_kernel(parts, pieces, heads, experts, *refs):
    doc_ref, rel_ref = refs[:2]
    lows = refs[2 : 2 + pieces]
    weight_ref, row_ref, proj_ref, att_ref, lse_ref, gain_ref, sums_ref = refs[
        2 + pieces : 9 + pieces
    ]
    outs = refs[9 + pieces :]
    n_grads = parts // 2 + 2 if parts > 1 else 1
    grad_outs = outs[:n_grads]
    keep_a, keep_b, send_out, sums_out, mixed, grad_proj, normed_grad = outs[n_grads : n_grads + 7]
    keep_out = (keep_a, keep_b)
    piece, mine_dp = lax.axis_index("tensor"), lax.axis_index("dp")
    second = doc_ref[doc_ref.shape[0] - 1]
    cols = heads * HDIM
    for at in range(pieces):
        mixed[pl.ds(pl.multiple_of((piece ^ at) * ROWS, ROWS), ROWS), :] = lows[at][...]
    weight_last = weight_ref[:, 3 * cols :]
    att_grad = dot(mixed[...], weight_last).astype(BF16)
    grad_last = dot(mixed[...], att_ref[...], TN)
    tiles = bias_tiles(rel_ref, piece * heads, heads)
    proj = proj_ref[...]
    length = proj.shape[0]
    blocks = length // BLOCK
    flipped = iota((BLOCK, BLOCK), 0) + iota((BLOCK, BLOCK), 1) == BLOCK - 1
    flipped = flipped.astype(F32).astype(BF16)
    wide = 2 * BLOCK
    lines = []
    grads_q, grads_k, grads_v = [], [], []
    for head in range(heads):
        at = head * HDIM
        key_sum = [jnp.zeros((BLOCK, HDIM), F32) for _ in range(blocks)]
        value_sum = [jnp.zeros((BLOCK, HDIM), F32) for _ in range(blocks)]
        near_sum = None
        query_done = []
        for block in reversed(range(blocks)):
            here = slice(block * BLOCK, (block + 1) * BLOCK)
            upto = slice(0, (block + 1) * BLOCK)
            query = proj[here, at : at + HDIM]
            keys = proj[upto, cols + at : cols + at + HDIM]
            values = proj[upto, 2 * cols + at : 2 * cols + at + HDIM]
            out_grad = att_grad[here, at : at + HDIM]
            scores = masked_scores(query, keys, tiles[head], second, block)
            again = jnp.exp(scores - lse_ref[here, head : head + 1])
            prob_grad = dot(out_grad, values, NT)
            weighted = again * prob_grad
            score_grad = weighted - again * jnp.sum(weighted, axis=1, keepdims=True)
            score_low = score_grad.astype(BF16)
            value_add = dot(again.astype(BF16), out_grad, TN)
            key_add = dot(score_low, query, TN)
            for other in range(block + 1):
                there = slice(other * BLOCK, (other + 1) * BLOCK)
                key_sum[other] = key_sum[other] + key_add[there, :]
                value_sum[other] = value_sum[other] + value_add[there, :]
            if block == 1:
                near_sum = score_grad
            else:
                near_sum = jnp.concatenate(
                    [near_sum[:, :BLOCK], near_sum[:, BLOCK:] + score_grad], axis=1
                )
            query_done.insert(0, dot(score_low, keys) * HDIM**-0.5)
        grads_q.append(jnp.concatenate(query_done, axis=0))
        grads_k.append(jnp.concatenate(key_sum, axis=0) * HDIM**-0.5)
        grads_v.append(jnp.concatenate(value_sum, axis=0))
        near_high = near_sum.astype(BF16)
        near_low = (near_sum - near_high.astype(F32)).astype(BF16)
        turned = dot(flipped, near_high) + dot(flipped, near_low)
        turned = pltpu.roll(turned, BLOCK + 1, 1, stride=1, stride_axis=0)
        lines.append(jnp.sum(turned, axis=0, keepdims=True))
    lines = jnp.concatenate(lines + [jnp.zeros((8 - heads, wide), F32)], axis=0)
    line_bucket = bucket_of((BLOCK - iota((wide, 128), 0)) & (wide - 1))
    spread = (line_bucket == iota((wide, 128), 1)).astype(F32)
    by_bucket = jnp.concatenate(
        [dot(lines, spread, precision=HIGHEST), jnp.zeros((8, HEADS * BUCKETS - 128), F32)], axis=1
    )
    bias_row = jnp.zeros((1, HEADS * BUCKETS), F32)
    for head in range(heads):
        placed = pltpu.roll(by_bucket, (piece * heads + head) * BUCKETS, 1)
        bias_row = bias_row + placed[head : head + 1, :]
    grad_proj[...] = jnp.concatenate(grads_q + grads_k + grads_v, axis=1).astype(BF16)
    x = row_ref[...].astype(F32)
    scale = lax.rsqrt(jnp.mean(x * x, axis=1, keepdims=True) + 1e-6)
    unit = x * scale
    normed = (unit * gain_ref[...]).astype(BF16)
    grad_first = dot(normed, grad_proj[...], TN)
    if parts > 1:
        grads = outs[n_grads + 7]
        depth = grad_first.shape[0] // parts
        grads[:, : 3 * cols] = grad_first
        grads[:, 3 * cols :] = grad_last
        for at in range(parts):
            piece_rows = grads[pl.ds(pl.multiple_of((mine_dp ^ at) * depth, 16), depth), :]
            if at % 2 == 0:
                grad_outs[at // 2][...] = piece_rows
            else:
                grad_outs[parts // 2 + (at == 1)][max(at // 2 - 1, 0)] = piece_rows.astype(BF16)
    else:
        grad_outs[0][:, : 3 * cols] = grad_first
        grad_outs[0][:, 3 * cols :] = grad_last
    normed_grad[...] = dot(grad_proj[...], weight_ref[:, : 3 * cols], NT)
    sums_out[...] = sums_ref[...]
    sums_out[experts + 1 : experts + 2, :] = jnp.sum(
        normed_grad[...] * unit, axis=0, keepdims=True
    )
    sums_out[experts + 2 : experts + 3, : HEADS * BUCKETS] = bias_row
    for at in range(pieces):
        mine = normed_grad[pl.ds(pl.multiple_of((piece ^ at) * ROWS, ROWS), ROWS), :]
        if at % 2 == 0:
            keep_out[at // 2][...] = mine
        else:
            send_out[at // 2 * ROWS : (at // 2 + 1) * ROWS, :] = mine.astype(BF16)
    send_out[pieces // 2 * ROWS :, :] = sums_out[...].astype(BF16)


def fold_back_kernel(keep_ref, near_ref, sums_ref, out_ref, sums_out):
    out_ref[:ROWS, :] = (keep_ref[...] + near_ref[ROWS : 2 * ROWS, :].astype(F32)).astype(BF16)
    sums = sums_ref[...] + near_ref[2 * ROWS :, :].astype(F32)
    sums_out[...] = sums
    out_ref[ROWS:, :] = sums.astype(BF16)


def join_kernel(sums_ref, far_ref, out_ref, low_ref):
    sums = sums_ref[...] + far_ref[ROWS:, :].astype(F32)
    out_ref[...] = sums
    low_ref[...] = sums.astype(BF16)


def input_kernel(own_ref, gain_ref, mixed_grad_ref, part_ref, near_ref, far_ref, out_ref):
    x = own_ref[...].astype(F32)
    scale = lax.rsqrt(jnp.mean(x * x, axis=1, keepdims=True) + 1e-6)
    scaled = (
        part_ref[...] + near_ref[:ROWS, :].astype(F32) + far_ref[:ROWS, :].astype(F32)
    ) * gain_ref[...]
    cubed = scale * scale * scale
    own = scale * scaled - x * cubed * jnp.mean(scaled * x, axis=1, keepdims=True)
    out_ref[...] = (mixed_grad_ref[...] + own).astype(BF16)


def swap(value, axis, size, mask):
    return lax.ppermute(value, axis, [(i, i ^ mask) for i in range(size)])


def gather_weights(shard, senders):
    if senders != 8:
        return [lax.all_gather(shard, "dp", axis=0, tiled=True)]
    parts = {0: shard}
    parts[1] = swap(shard, "dp", senders, 1)
    for mask in (2, 4, 6):
        parts[mask] = swap(shard, "dp", senders, mask)
    for mask in (2, 4, 6):
        parts[mask + 1] = swap(parts[mask], "dp", senders, 1)
    return [parts[i] for i in range(senders)]


def fold_kernel(keep_ref, near_ref, out_ref):
    out_ref[...] = (keep_ref[...] + near_ref[...].astype(F32)).astype(BF16)


def fold(keep, near, name, after=()):
    return call(fold_kernel, [struct(near.shape, BF16)], [], [keep, near], name=name, after=after)[0]


def finish_kernel(cols, keep_ref, near_ref, one_ref, two_ref, three_ref, first_ref, last_ref):
    total = keep_ref[...] + near_ref[...].astype(F32)
    for part in (one_ref, two_ref, three_ref):
        total = total + part[...].astype(F32)
    for at in range(3):
        first_ref[at] = total[:, at * cols : (at + 1) * cols]
    last_ref[...] = total[:, 3 * cols :]


def fold_three_kernel(one_ref, two_ref, three_ref, near_ref, sums_ref, got_ref, *outs):
    *chunks, sums_out = outs
    sums = sums_ref[...] + got_ref[...].astype(F32)
    sums_out[...] = sums
    for at, (keep, out) in enumerate(zip((one_ref, two_ref, three_ref), chunks)):
        depth = keep.shape[0]
        out[:depth, :] = (keep[...] + near_ref[at].astype(F32)).astype(BF16)
        out[depth:, :] = sums.astype(BF16)


def put_small(total, experts, gains_ref, bias_ref, router_ref):
    router_ref[...] = total[:experts]
    gains_ref[0:2, :] = total[experts : experts + 2]
    for head in range(HEADS):
        bias_ref[head : head + 1, :] = total[
            experts + 2 : experts + 3, head * BUCKETS : (head + 1) * BUCKETS
        ]


def finish_kernel(cols, experts, keep_ref, near_ref, sums_ref, *refs):
    *parts, first_ref, last_ref, gains_ref, bias_ref, router_ref = refs
    depth = keep_ref.shape[0]
    total = keep_ref[...] + near_ref[0].astype(F32)
    small = sums_ref[...]
    for part in parts:
        total = total + part[:depth, :].astype(F32)
        small = small + part[depth:, :].astype(F32)
    for at in range(3):
        first_ref[at] = total[:, at * cols : (at + 1) * cols]
    last_ref[...] = total[:, 3 * cols :]
    put_small(small, experts, gains_ref, bias_ref, router_ref)


def sums_kernel(experts, sums_ref, gains_ref, bias_ref, router_ref):
    put_small(sums_ref[...], experts, gains_ref, bias_ref, router_ref)


def last_sums(grads, keep_a, keep_b, near, sums, senders, pieces, cols, experts, before):
    count, width = sums.shape
    if senders == 8:
        near_grads = swap(grads[4], "dp", senders, 1)
        near_last = swap(grads[5], "dp", senders, 1)
    other, sums = call(
        fold_back_kernel,
        [struct((ROWS + count, width), BF16), struct((count, width), F32)],
        [],
        [keep_b, near, sums],
        name="fold_rows",
        prompt=True,
    )
    far = swap(other, "tensor", pieces, 2)
    sums, low = call(
        join_kernel,
        [struct((count, width), F32), struct((count, width), BF16)],
        [],
        [sums, far],
        name="join",
        prompt=True,
    )
    small = [
        struct((8, width), F32),
        struct((HEADS, BUCKETS), F32),
        struct((experts, width), F32),
    ]
    if senders != 8:
        total = lax.psum_scatter(grads[0], "dp", scatter_dimension=0, tiled=True)
        first = jnp.stack([total[:, at * cols : (at + 1) * cols] for at in range(3)])
        weight_sums = (first, total[:, 3 * cols :])
        small = call(
            functools.partial(sums_kernel, experts), small, [], [lax.psum(sums, "dp")], name="sums"
        )
    else:
        depth = grads[0].shape[0]
        got = swap(low, "dp", senders, 1)
        *folded, sums = call(
            fold_three_kernel,
            [struct((depth + count, width), BF16)] * 3 + [struct((count, width), F32)],
            [],
            [grads[1], grads[2], grads[3], near_grads, sums, got],
            name="fold_weights",
            prompt=True,
            after=before,
        )
        arrived = [swap(folded[at], "dp", senders, 2 * at + 2) for at in (2, 1, 0)]
        first, last, *small = call(
            functools.partial(finish_kernel, cols, experts),
            [struct((3, depth, cols), F32), struct((depth, cols), F32)] + small,
            [],
            [grads[0], near_last, sums] + arrived,
            name="finish",
            prompt=True,
        )
        weight_sums = (first, last)
    return weight_sums, (keep_a, near, far), small


def scatter_rows(keep_a, keep_b, near, pieces, after=()):
    other = call(
        lambda keep, got, out: fold_kernel(keep, got.at[1], out),
        [struct(keep_b.shape, BF16)],
        [],
        [keep_b, near],
        name="fold_rows", prompt=True,
        after=after,
    )[0]
    return keep_a, near, swap(other, "tensor", pieces, 2), other


def gather_rows(rows, pieces):
    far = swap(rows, "tensor", pieces, 2)
    near = swap(rows, "tensor", pieces, 1)
    last = swap(far, "tensor", pieces, 1)
    return [rows, near, far, last]


def exchange(blocks, senders, capacity):
    rows, width = blocks.shape
    return lax.all_to_all(
        blocks.reshape(senders, capacity, width), "dp", split_axis=0, concat_axis=0, tiled=True
    ).reshape(rows, width)


def body(
    tokens,
    doc_start,
    routes,
    gain_attn,
    w_qkv,
    w_out,
    rel_bias,
    gain_ffn,
    router,
    w_in,
    w_exp_out,
    out_grad,
):
    pieces = lax.axis_size("tensor")
    senders = lax.axis_size("dp")
    tok_dev, width = tokens.shape
    routes, rel_bias, router = routes.T, rel_bias.T, router.T
    length = tok_dev * pieces
    experts = router.shape[0]
    capacity = max(2, 3 * tok_dev * routes.shape[0] // (2 * experts))
    slots = experts * capacity
    heads = w_out.shape[1] // HDIM
    cols = heads * HDIM
    gain_one = gain_attn.reshape(1, width)
    gain_two = gain_ffn.reshape(1, width)

    shard, in_head = call(
        pack_kernel,
        [
            struct((w_out.shape[0], 4 * cols), BF16),
            struct((width // 3, w_in.shape[2]), BF16),
        ],
        [],
        [w_qkv.transpose(1, 0, 2), w_out, w_in[0]],
        name="pack",
        held=(0, 1, 2),
        parts={2: (width // 3, w_in.shape[2])},
    )
    weights = gather_weights(shard, senders)
    rows = gather_rows(tokens, pieces)
    out_one = w_exp_out[0]
    in_one = w_in[0]
    out_two = swap(out_one, "tensor", pieces, 2)
    in_two_a = swap(in_head, "tensor", pieces, 2)
    in_two_b = swap(in_one[in_head.shape[0] :], "tensor", pieces, 2)

    slot, grad_out = call(
        functools.partial(slots_kernel, capacity),
        [struct((tok_dev, 128), jnp.int32), struct((slots, width), BF16)],
        [],
        [routes, out_grad],
        flops=2 * slots * tok_dev * width,
        name="slots",
        held=(1,),
        kept=(0, 1),
    )

    grad_out = once(grad_out, weights[1::2], "gathered")
    whole_weight, whole_rows, projected, attended, lse, keep_a, keep_b, send = call(
        functools.partial(forward_kernel, len(weights), pieces, heads),
        [
            struct((width, 4 * cols), BF16),
            struct((length, width), BF16),
            struct((length, 3 * cols), BF16),
            struct((length, cols), BF16),
            struct((length, 128), F32),
            struct((tok_dev, width), F32),
            struct((tok_dev, width), F32),
            struct((pieces // 2, tok_dev, width), BF16),
        ],
        [],
        [doc_start, rel_bias] + weights + rows + [gain_one],
        smem=2,
        flops=2 * length * width * 4 * cols + 4 * heads * length * length * HDIM,
        name="attend",
        held=tuple(range(2, 2 + len(weights))),
        kept=(0, 1, 2, 3, 4),
        vmem=12,
    )
    pull_own = exchange(grad_out, senders, capacity)
    pull_mate = swap(pull_own, "tensor", pieces, 1)
    far_pull_own = swap(pull_own, "tensor", pieces, 2)

    near = swap(send, "tensor", pieces, 1)
    part, near, far, _ = scatter_rows(keep_a, keep_b, near, pieces, [out_two, in_two_a])
    mixed, normed_two, gates, outgoing = call(
        dispatch_kernel,
        [
            struct((tok_dev, width), F32),
            struct((tok_dev, width), BF16),
            struct((tok_dev, 128), F32),
            struct((slots, width + GATE_LANES), BF16),
        ],
        [],
        [tokens, part, near, far, gain_two, router, routes, slot],
        flops=2 * slots * tok_dev * width,
        name="dispatch",
        after=[pull_own],
        kept=(0, 1, 2),
    )
    slot_own = exchange(outgoing, senders, capacity)
    slot_mate = swap(slot_own, "tensor", pieces, 1)
    payload = width + GATE_LANES
    units = in_one.shape[1]
    expert_flops = 12 * slots * width * units
    hidden_one, pre_one, row_total, gate_total = call(
        own_slice_kernel,
        [struct((2 * slots, units), BF16)] * 2
        + [struct((2 * slots, width), F32), struct((2 * slots, GATE_LANES), F32)],
        [pltpu.VMEM((2 * slots, width), BF16)] * 2,
        [slot_own, slot_mate, pull_own, pull_mate, in_one, out_one],
        flops=expert_flops,
        name="own_slice",
        prompt=True,
        held=(4, 5),
        kept=(0, 1),
        vmem=18,
    )
    hidden_two, row_keep, row_send = call(
        far_slice_kernel,
        [
            struct((2 * slots, units), BF16),
            struct((slots, payload), F32),
            struct((slots, payload), BF16),
        ],
        [pltpu.VMEM((width, units), BF16), pltpu.VMEM((2 * slots, units), BF16)]
        + [pltpu.VMEM((2 * slots, width), BF16)] * 2,
        [slot_own, slot_mate, pull_own, pull_mate, in_two_a, in_two_b, out_two, row_total, gate_total],
        flops=expert_flops,
        name="far_slice",
        prompt=True,
        held=(4, 5, 6),
        kept=(0,),
        vmem=20,
    )
    row_mate = swap(row_send, "tensor", pieces, 1)
    far_own = swap(slot_own, "tensor", pieces, 2)
    (row_out,) = call(
        merge_kernel,
        [struct((slots, payload), BF16)],
        [],
        [row_keep, row_mate],
        name="merge",
    )
    back = exchange(row_out, senders, capacity)

    far_mate = swap(far_own, "tensor", pieces, 1)
    out_keep, out_send = call(
        expert_out_kernel,
        [struct((slots, width), F32), struct((slots, width), BF16)],
        [],
        [hidden_one, hidden_two, out_one, out_two],
        flops=4 * 2 * slots * width * in_one.shape[1],
        name="expert_out",
        held=(0, 1, 2, 3),
        after=[far_own],
        vmem=10,
    )
    turned = [pltpu.VMEM((width, 2 * slots), BF16), pltpu.VMEM((2 * slots, width), BF16)]
    grads_both = [struct(in_one.shape, F32), struct(out_one.shape, F32), struct((8, 128), F32)]
    own_in, own_out, own_graded = call(
        own_grads_kernel,
        grads_both,
        turned,
        [slot_own, slot_mate, pull_own, pull_mate, hidden_one, pre_one],
        flops=8 * slots * width * units,
        name="own_grads",
        after=[out_send],
        held=(0, 1, 2, 3, 4, 5),
        vmem=24,
    )
    far_pull_own = once(far_pull_own, [own_graded], "pulled")
    far_pull_mate = swap(far_pull_own, "tensor", pieces, 1)
    grad_in, grad_out_sum, graded = call(
        far_grads_kernel,
        grads_both,
        turned + [pltpu.VMEM((2 * slots, width), BF16)],
        [far_own, far_mate, far_pull_own, far_pull_mate, in_one, out_one, own_in, own_out],
        flops=16 * slots * width * units,
        name="far_grads",
        held=(4, 5),
        vmem=30,
    )

    sum_rows = -(-(experts + 3) // 8) * 8
    mixed_grad, mixed_low, sums_two = call(
        combine_kernel,
        [
            struct((tok_dev, width), F32),
            struct((tok_dev, width), BF16),
            struct((sum_rows, width), F32),
        ],
        [],
        [back, slot, gates, mixed, normed_two, router, routes, out_grad, gain_two],
        flops=2 * slots * tok_dev * width,
        name="combine",
        after=[graded],
        held=(1, 2, 3, 4, 7),
    )
    expert_out = fold(out_keep, swap(out_send, "tensor", pieces, 1), "fold_out", [mixed_low])
    returned = exchange(expert_out, senders, capacity)
    result, given = call(
        result_kernel,
        [struct((tok_dev, width), BF16), struct((8, 128), F32)],
        [],
        [returned, slot, gates, mixed],
        flops=4 * slots * tok_dev * width,
        name="result", prompt=True,
        held=(1, 2, 3),
    )

    lows = gather_rows(mixed_low, pieces)
    parts = len(weights)
    if parts > 1:
        depth = width // parts
        grad_shapes = [struct((depth, 4 * cols), F32)] * (parts // 2)
        grad_shapes += [struct((n, depth, 4 * cols), BF16) for n in (parts // 2 - 1, 1)]
        grad_scratch = [pltpu.VMEM((width, 4 * cols), F32)]
    else:
        grad_shapes = [struct((width, 4 * cols), F32)]
        grad_scratch = []
    *weight_grads, keep_a, keep_b, send, sums = call(
        functools.partial(backward_kernel, parts, pieces, heads, experts),
        grad_shapes
        + [
            struct((tok_dev, width), F32),
            struct((tok_dev, width), F32),
            struct((pieces // 2 * tok_dev + sum_rows, width), BF16),
            struct((sum_rows, width), F32),
        ],
        [
            pltpu.VMEM((length, width), BF16),
            pltpu.VMEM((length, 3 * cols), BF16),
            pltpu.VMEM((length, width), F32),
        ]
        + grad_scratch,
        [doc_start, rel_bias]
        + lows
        + [whole_weight, whole_rows, projected, attended, lse, gain_one, sums_two],
        smem=2,
        name="attend_back",
        prompt=True,
        held=tuple(range(2 + pieces, 7 + pieces)),
        vmem=16,
    )
    near = swap(send, "tensor", pieces, 1)
    (first_sum, last_sum), (part, near, far), (gains, bias_grad, router_grad) = last_sums(
        weight_grads, keep_a, keep_b, near, sums, senders, pieces, cols, experts, [given]
    )
    (input_grad,) = call(
        input_kernel,
        [struct((tok_dev, width), BF16)],
        [],
        [tokens, gain_one, mixed_grad, part, near, far],
        name="input_grad", prompt=True,
        held=(0, 2),
    )
    return (
        result,
        input_grad,
        gains[1],
        first_sum.transpose(1, 0, 2),
        last_sum,
        bias_grad.T,
        gains[0],
        router_grad.T,
        grad_in[None],
        grad_out_sum[None],
    )


def solution(mesh):
    in_specs = (
        P(("dp", "tensor"), None),
        P("dp"),
        P(("dp", "tensor"), None),
        P(),
        P("dp", None, "tensor"),
        P("dp", "tensor"),
        P(),
        P(),
        P(),
        P("dp", None, "tensor"),
        P("dp", "tensor", None),
        P(("dp", "tensor"), None),
    )
    out_specs = (
        P(("dp", "tensor"), None),
        P(("dp", "tensor"), None),
        P(),
        P("dp", None, "tensor"),
        P("dp", "tensor"),
        P(),
        P(),
        P(),
        P("dp", None, "tensor"),
        P("dp", "tensor", None),
    )
    return jax.shard_map(body, mesh=mesh, in_specs=in_specs, out_specs=out_specs, check_vma=False)
```

```python
import functools

import jax
import jax.numpy as jnp
import numpy as np
from jax import lax
from jax.experimental import pallas as pl
from jax.experimental.pallas import tpu as pltpu
from jax.sharding import PartitionSpec as P

HEADS = 12
HDIM = 64
BUCKETS = 32
ROWS = 128
BLOCK = 256
GATE_LANES = 128

LIMITS = np.array([19, 21, 24, 27, 31, 35, 40, 46, 52, 59, 67, 77, 87, 99, 113], np.int32)
HIGHEST = lax.Precision.HIGHEST
F32 = jnp.float32
BF16 = jnp.bfloat16
MIB = 1024 * 1024

NN = (((1,), (0,)), ((), ()))
NT = (((1,), (1,)), ((), ()))
TN = (((0,), (0,)), ((), ()))


def dot(left, right, dims=NN, precision=None):
    return lax.dot_general(left, right, dims, preferred_element_type=F32, precision=precision)


def iota(shape, axis):
    return lax.broadcasted_iota(jnp.int32, shape, axis)


def bucket_of(distance):
    bucket = jnp.minimum(distance, 16)
    for limit in LIMITS:
        bucket = bucket + (distance >= int(limit)).astype(jnp.int32)
    return bucket


def in_three(value):
    high = value.astype(BF16)
    rest = value - high.astype(F32)
    middle = rest.astype(BF16)
    low = (rest - middle.astype(F32)).astype(BF16)
    return high, middle, low


def three_lanes(value):
    high, middle, low = in_three(value)
    lane = iota((value.shape[0], GATE_LANES), 1)
    zero = jnp.zeros((value.shape[0], GATE_LANES), F32)
    spread = jnp.where(
        lane == 0,
        high.astype(F32),
        jnp.where(lane == 1, middle.astype(F32), jnp.where(lane == 2, low.astype(F32), zero)),
    )
    return spread.astype(BF16)


def lanes_sum(lanes):
    return jnp.sum(lanes.astype(F32), axis=1, keepdims=True)


def pick(columns, at):
    return columns[:, at : at + 1]


def call(
    kernel,
    outs,
    scratch,
    args,
    smem=0,
    flops=0,
    name=None,
    after=(),
    vmem=6,
    held=(),
    kept=(),
    passed=(),
    prompt=False,
    parts={},
):
    n_in, n_after, n_out = len(args), len(after), len(outs)
    n_pass = len(passed)

    def run(*refs):
        ins, rest = refs[:n_in], refs[n_in + n_after + n_pass :]
        kernel(*ins, *rest[:n_out], *rest[n_out + n_pass :])

    def whole(a):
        shape = getattr(a, "shape", a)
        return pl.BlockSpec(shape, lambda i: (0,) * len(shape))

    moved = sum(a.size * a.dtype.itemsize for a in list(args) + list(outs))
    args = [
        pltpu.with_memory_space_constraint(a, pltpu.HBM) if at in held else a
        for at, a in enumerate(args)
    ]
    after = [
        pltpu.with_memory_space_constraint(a, pltpu.HBM) if a.size > 1 << 18 else a for a in after
    ]
    out_shape = [
        pltpu.HBM(o.shape, o.dtype) if at in kept else jax.ShapeDtypeStruct(o.shape, o.dtype)
        for at, o in enumerate(outs)
    ]
    return pl.pallas_call(
        run,
        grid=(1,),
        out_shape=out_shape + [jax.ShapeDtypeStruct(o.shape, o.dtype) for o in passed],
        in_specs=[pl.BlockSpec(memory_space=pltpu.SMEM)] * smem
        + [whole(parts.get(smem + at, a)) for at, a in enumerate(args[smem:])]
        + [pl.BlockSpec(memory_space=pl.ANY)] * (n_after + n_pass),
        out_specs=[whole(o) for o in outs] + [pl.BlockSpec(memory_space=pl.ANY)] * n_pass,
        scratch_shapes=scratch,
        input_output_aliases={n_in + n_after + at: n_out + at for at in range(n_pass)},
        compiler_params=pltpu.CompilerParams(vmem_limit_bytes=vmem * MIB),
        cost_estimate=pl.CostEstimate(
            flops=1 if prompt else flops,
            bytes_accessed=1 if prompt else moved,
            transcendentals=0,
        ),
        name=name,
    )(*args, *after, *passed)


def once(value, after, name):
    return call(lambda: None, [], [], [], name=name, after=after, passed=[value])[0]


def columns_of(turned):
    filled = jnp.concatenate(
        [turned.astype(F32), jnp.zeros((8 - turned.shape[0], turned.shape[1]), F32)], axis=0
    )
    return filled.T.astype(jnp.int32)


def pack_kernel(first_ref, last_ref, in_ref, out_ref, head_ref):
    head_ref[...] = in_ref[...]
    cols = last_ref.shape[1]
    for at in range(3):
        out_ref[:, at * cols : (at + 1) * cols] = first_ref[at]
    out_ref[:, 3 * cols :] = last_ref[...]


def struct(shape, dtype):
    return jax.ShapeDtypeStruct(shape, dtype)


def slots_kernel(capacity, routes_ref, grad_ref, slot_ref, out_ref):
    tokens = routes_ref.shape[1]
    slots = out_ref.shape[0]
    experts = slots // capacity
    routes = columns_of(routes_ref[...])
    first, second = routes[:, 0:1], routes[:, 1:2]
    lane = iota((tokens, experts), 1)
    one_first = (first == lane).astype(F32)
    one_second = (second == lane).astype(F32)
    member = (one_first + one_second).astype(BF16)
    below = (iota((tokens, tokens), 1) < iota((tokens, tokens), 0)).astype(F32).astype(BF16)
    earlier = dot(below, member)
    slot_first = first * capacity + jnp.sum(one_first * earlier, axis=1, keepdims=True).astype(
        jnp.int32
    )
    slot_second = second * capacity + jnp.sum(one_second * earlier, axis=1, keepdims=True).astype(
        jnp.int32
    )
    wide = iota((tokens, 128), 1)
    slot_ref[...] = jnp.where(wide == 0, slot_first, slot_second)
    places = iota((tokens, slots), 1)
    chosen = ((slot_first == places) | (slot_second == places)).astype(F32).astype(BF16)
    out_ref[...] = dot(chosen, grad_ref[...], TN).astype(BF16)


def bias_tiles(rel_ref, first_head, heads):
    wide = 2 * BLOCK
    distance = (BLOCK - iota((8, wide), 1)) & (wide - 1)
    bucket = bucket_of(distance)
    tiles = []
    for head in range(heads):
        line = jnp.zeros((8, wide), F32)
        for b in range(BUCKETS):
            line = jnp.where(bucket == b, rel_ref[first_head + head, b], line)
        grid = jnp.broadcast_to(line[0:1, :], (BLOCK, wide))
        tiles.append(pltpu.roll(grid, 0, 1, stride=1, stride_axis=0))
    return tiles


def masked_scores(query, keys, tile, second, block):
    width = (block + 1) * BLOCK
    raw = dot(query, keys, NT) * HDIM**-0.5
    bias = tile[:, 2 * BLOCK - width :]
    column = iota((BLOCK, width), 1)
    row = iota((BLOCK, width), 0) + block * BLOCK
    starts = jnp.where(row >= second, second, 0)
    allowed = (column <= row) & (column >= starts)
    return jnp.where(allowed, raw + bias, -1e9)


def forward_kernel(parts, pieces, heads, *refs):
    doc_ref, rel_ref = refs[:2]
    weights = refs[2 : 2 + parts]
    rows = refs[2 + parts : 2 + parts + pieces]
    gain_ref = refs[2 + parts + pieces]
    weight_out, row_out, proj_out, att_out, lse_out, keep_a, keep_b, send_out = refs[
        3 + parts + pieces :
    ]
    keep_out = (keep_a, keep_b)
    piece, mine_dp = lax.axis_index("tensor"), lax.axis_index("dp")
    second = doc_ref[doc_ref.shape[0] - 1]
    cols = heads * HDIM
    for at in range(parts):
        depth = weights[at].shape[0]
        start = (mine_dp ^ at) * depth if parts > 1 else 0
        weight_out[pl.ds(pl.multiple_of(start, 16), depth), :] = weights[at][...]
    for at in range(pieces):
        row_out[pl.ds(pl.multiple_of((piece ^ at) * ROWS, ROWS), ROWS), :] = rows[at][...]
    x = row_out[...].astype(F32)
    scale = lax.rsqrt(jnp.mean(x * x, axis=1, keepdims=True) + 1e-6)
    normed = (x * scale * gain_ref[...]).astype(BF16)
    proj_out[...] = dot(normed, weight_out[:, : 3 * cols]).astype(BF16)
    tiles = bias_tiles(rel_ref, piece * heads, heads)
    blocks = x.shape[0] // BLOCK
    proj = proj_out[...]
    wide = iota((BLOCK, 128), 1)
    for block in range(blocks):
        here = slice(block * BLOCK, (block + 1) * BLOCK)
        upto = slice(0, (block + 1) * BLOCK)
        done = []
        kept = jnp.zeros((BLOCK, 128), F32)
        for head in range(heads):
            at = head * HDIM
            query = proj[here, at : at + HDIM]
            keys = proj[upto, cols + at : cols + at + HDIM]
            values = proj[upto, 2 * cols + at : 2 * cols + at + HDIM]
            scores = masked_scores(query, keys, tiles[head], second, block)
            peak = jnp.max(scores, axis=1, keepdims=True)
            shifted = jnp.exp(scores - peak)
            total = jnp.sum(shifted, axis=1, keepdims=True)
            attention = (shifted * (1.0 / total)).astype(BF16)
            done.append(dot(attention, values).astype(BF16))
            kept = jnp.where(wide == head, peak + jnp.log(total), kept)
        att_out[here, :] = jnp.concatenate(done, axis=1)
        lse_out[here, :] = kept
    weight_last = weight_out[:, 3 * cols :]
    for at in range(pieces):
        mine = att_out[pl.ds(pl.multiple_of((piece ^ at) * ROWS, ROWS), ROWS), :]
        product = dot(mine, weight_last, NT)
        if at % 2 == 0:
            keep_out[at // 2][...] = product
        else:
            send_out[at // 2] = product.astype(BF16)


def dispatch_kernel(
    own_ref,
    part_ref,
    near_ref,
    far_ref,
    gain_ref,
    router_ref,
    routes_ref,
    slot_ref,
    mixed_ref,
    normed_ref,
    gates_ref,
    out_ref,
):
    width = own_ref.shape[1]
    tokens = own_ref.shape[0]
    slots = out_ref.shape[0]
    mixed = own_ref[...].astype(F32) + (
        part_ref[...] + near_ref[0].astype(F32) + far_ref[...].astype(F32)
    )
    mixed_ref[...] = mixed
    scale = lax.rsqrt(jnp.mean(mixed * mixed, axis=1, keepdims=True) + 1e-6)
    normed = (mixed * scale * gain_ref[...]).astype(BF16)
    normed_ref[...] = normed
    logits = dot(normed, router_ref[...], NT)
    routes = columns_of(routes_ref[...])
    lane = iota(logits.shape, 1)
    one = jnp.sum(jnp.where(routes[:, 0:1] == lane, logits, 0.0), axis=1, keepdims=True)
    two = jnp.sum(jnp.where(routes[:, 1:2] == lane, logits, 0.0), axis=1, keepdims=True)
    peak = jnp.maximum(one, two)
    one, two = jnp.exp(one - peak), jnp.exp(two - peak)
    total = one + two
    one, two = one / total, two / total
    wide = iota((tokens, 128), 1)
    gates_ref[...] = jnp.where(wide == 0, one, two)
    places = iota((tokens, slots), 1)
    slot = slot_ref[...]
    first = (slot[:, 0:1] == places).astype(F32).astype(BF16)
    second = (slot[:, 1:2] == places).astype(F32).astype(BF16)
    out_ref[:, :width] = dot(first + second, normed, TN).astype(BF16)
    gate_slots = dot(first, three_lanes(one), TN) + dot(second, three_lanes(two), TN)
    out_ref[:, width:] = gate_slots.astype(BF16)


def gelu_and_slope(x):
    inner = 0.7978845608028654 * (x + 0.044715 * (x * x * x))
    bend = jnp.tanh(inner)
    half = 0.5 * (1.0 + bend)
    slope = half + 0.5 * x * (1.0 - bend * bend) * (
        0.7978845608028654 * (1.0 + 3 * 0.044715 * (x * x))
    )
    return x * half, slope


def gather_sides(sources, pulls, rows_all, pulls_all):
    rows, width = pulls[0].shape
    gates = []
    for at, (source, pull) in enumerate(zip(sources, pulls)):
        here = slice(at * rows, (at + 1) * rows)
        rows_all[here, :] = source[:, :width]
        pulls_all[here, :] = pull[...]
        gates.append(lanes_sum(source[:, width:]))
    return jnp.concatenate(gates, axis=0)


def through_slice(rows_all, pulls_all, gate, in_ref, out_ref, hidden_out, pre_out):
    hidden_units = in_ref.shape[1]
    tile = 256
    gate_wide = jnp.zeros((rows_all.shape[0], tile), F32)
    for at in range(0, hidden_units, tile):
        there = slice(at, at + tile)
        pulled = dot(pulls_all[...], out_ref[there, :], NT)
        hidden, slope = gelu_and_slope(dot(rows_all[...], in_ref[:, there]))
        hidden = hidden.astype(BF16)
        hidden_out[:, there] = hidden
        pre_out[:, there] = (pulled * gate * slope).astype(BF16)
        gate_wide = gate_wide + hidden.astype(F32) * pulled
    return jnp.sum(gate_wide, axis=1, keepdims=True)


def expert_kernel(
    own_ref,
    mate_ref,
    pull_own,
    pull_mate,
    in_ref,
    out_ref,
    far_in_a,
    far_in_b,
    far_out,
    hidden_ref,
    pre_ref,
    far_hidden,
    keep_ref,
    send_ref,
    rows_all,
    pulls_all,
    far_in,
    far_pre,
):
    rows, width = pull_own.shape
    split = far_in_a.shape[0]
    gate = gather_sides((own_ref, mate_ref), (pull_own, pull_mate), rows_all, pulls_all)
    gate_sum = through_slice(rows_all, pulls_all, gate, in_ref, out_ref, hidden_ref, pre_ref)
    far_in[:split, :] = far_in_a[...]
    far_in[split:, :] = far_in_b[...]
    gate_sum = gate_sum + through_slice(
        rows_all, pulls_all, gate, far_in, far_out, far_hidden, far_pre
    )
    total = dot(pre_ref[...], in_ref[...], NT) + dot(far_pre[...], far_in[...], NT)
    keep_ref[:, :width] = total[:rows, :]
    keep_ref[:, width:] = jnp.broadcast_to(gate_sum[:rows], (rows, GATE_LANES))
    send_ref[:, :width] = total[rows:, :].astype(BF16)
    send_ref[:, width:] = three_lanes(gate_sum[rows:])


def turn_slots(sources, pulls, rows_turned, pulls_all, rows_all=None):
    rows, width = pulls[0].shape
    for at, (source, pull) in enumerate(zip(sources, pulls)):
        here = slice(at * rows, (at + 1) * rows)
        rows_turned[:, here] = source[:, :width].T
        gate = lanes_sum(source[:, width:])
        pulls_all[here, :] = (gate * pull[...].astype(F32)).astype(BF16)
        if rows_all is not None:
            rows_all[here, :] = source[:, :width]


def own_grads_kernel(
    own_ref,
    mate_ref,
    pull_own,
    pull_mate,
    hidden_ref,
    pre_ref,
    grad_in,
    grad_out,
    token_ref,
    rows_turned,
    pulls_all,
):
    token_ref[...] = jnp.zeros_like(token_ref)
    turn_slots((own_ref, mate_ref), (pull_own, pull_mate), rows_turned, pulls_all)
    tile = 256
    for unit in range(0, hidden_ref.shape[1], tile):
        there = slice(unit, unit + tile)
        grad_in[:, there] = dot(rows_turned[...], pre_ref[:, there])
        grad_out[there, :] = dot(hidden_ref[:, there], pulls_all[...], TN)


def far_grads_kernel(
    own_ref,
    mate_ref,
    pull_own,
    pull_mate,
    in_ref,
    out_ref,
    own_in,
    own_out,
    grad_in,
    grad_out,
    token_ref,
    rows_turned,
    pulls_all,
    rows_all,
):
    token_ref[...] = jnp.zeros_like(token_ref)
    turn_slots((own_ref, mate_ref), (pull_own, pull_mate), rows_turned, pulls_all, rows_all)
    tile = 256
    for unit in range(0, in_ref.shape[1], tile):
        there = slice(unit, unit + tile)
        hidden, slope = gelu_and_slope(dot(rows_all[...], in_ref[:, there]))
        pulled = dot(pulls_all[...], out_ref[there, :], NT)
        pre_grad = (pulled * slope).astype(BF16)
        grad_in[:, there] = own_in[:, there] + dot(rows_turned[...], pre_grad)
        grad_out[there, :] = own_out[there, :] + dot(hidden.astype(BF16), pulls_all[...], TN)


def expert_out_kernel(hidden_one, hidden_two, out_one, out_two, keep_ref, send_ref):
    rows = keep_ref.shape[0]
    product = dot(hidden_one[...], out_one[...]) + dot(hidden_two[...], out_two[...])
    keep_ref[...] = product[:rows]
    send_ref[...] = product[rows:].astype(BF16)


def merge_kernel(keep_ref, mate_ref, out_ref):
    width = keep_ref.shape[1] - GATE_LANES
    out_ref[:, :width] = (keep_ref[:, :width] + mate_ref[:, :width].astype(F32)).astype(BF16)
    gate = keep_ref[:, width : width + 1] + lanes_sum(mate_ref[:, width:])
    out_ref[:, width:] = three_lanes(gate)


def combine_kernel(
    back_ref,
    slot_ref,
    gates_ref,
    mixed_ref,
    normed_ref,
    router_ref,
    routes_ref,
    grad_ref,
    gain_ref,
    mixed_grad_ref,
    low_ref,
    sums_ref,
):
    tokens, width = grad_ref.shape
    slots = back_ref.shape[0]
    experts = router_ref.shape[0]
    places = iota((tokens, slots), 1)
    slot = slot_ref[...]
    first = (slot[:, 0:1] == places).astype(F32).astype(BF16)
    second = (slot[:, 1:2] == places).astype(F32).astype(BF16)
    lanes = back_ref[:, width:]
    pull_one = jnp.sum(dot(first, lanes), axis=1, keepdims=True)
    pull_two = jnp.sum(dot(second, lanes), axis=1, keepdims=True)
    one, two = gates_ref[:, 0:1], gates_ref[:, 1:2]
    mean_pull = one * pull_one + two * pull_two
    delta_one = one * (pull_one - mean_pull)
    delta_two = two * (pull_two - mean_pull)
    routes = columns_of(routes_ref[...])
    lane = iota((tokens, experts), 1)
    logit_grad = jnp.where(routes[:, 0:1] == lane, delta_one, 0.0) + jnp.where(
        routes[:, 1:2] == lane, delta_two, 0.0
    )
    high = logit_grad.astype(BF16)
    low = (logit_grad - high.astype(F32)).astype(BF16)
    normed = normed_ref[...]
    router = router_ref[...]
    normed_grad = dot(first + second, back_ref[:, :width]) + (
        dot(high, router) + dot(low, router)
    )
    mixed = mixed_ref[...]
    grad = grad_ref[...].astype(F32)
    scale = lax.rsqrt(jnp.mean(mixed * mixed, axis=1, keepdims=True) + 1e-6)
    scaled = normed_grad * gain_ref[...]
    cubed = scale * scale * scale
    mixed_grad = (
        grad
        + scale * scaled
        - mixed * cubed * jnp.mean(scaled * mixed, axis=1, keepdims=True)
    )
    mixed_grad_ref[...] = mixed_grad
    low_ref[...] = mixed_grad.astype(BF16)
    sums_ref[...] = jnp.zeros_like(sums_ref)
    sums_ref[:experts, :] = dot(high, normed, TN) + dot(low, normed, TN)
    sums_ref[experts : experts + 1, :] = jnp.sum(
        normed_grad * mixed * scale, axis=0, keepdims=True
    )


def result_kernel(back_ref, slot_ref, gates_ref, mixed_ref, out_ref, token_ref):
    token_ref[...] = jnp.zeros_like(token_ref)
    tokens = mixed_ref.shape[0]
    slots = back_ref.shape[0]
    places = iota((tokens, slots), 1)
    slot = slot_ref[...]
    first = (slot[:, 0:1] == places).astype(F32).astype(BF16)
    second = (slot[:, 1:2] == places).astype(F32).astype(BF16)
    back = back_ref[...]
    added = gates_ref[:, 0:1] * dot(first, back) + gates_ref[:, 1:2] * dot(second, back)
    out_ref[...] = (mixed_ref[...] + added).astype(BF16)


def backward_kernel(parts, pieces, heads, experts, *refs):
    doc_ref, rel_ref = refs[:2]
    lows = refs[2 : 2 + pieces]
    weight_ref, row_ref, proj_ref, att_ref, lse_ref, gain_ref, sums_ref = refs[
        2 + pieces : 9 + pieces
    ]
    outs = refs[9 + pieces :]
    n_grads = parts // 2 + 2 if parts > 1 else 1
    grad_outs = outs[:n_grads]
    keep_a, keep_b, send_out, sums_out, mixed, grad_proj, normed_grad = outs[n_grads : n_grads + 7]
    keep_out = (keep_a, keep_b)
    piece, mine_dp = lax.axis_index("tensor"), lax.axis_index("dp")
    second = doc_ref[doc_ref.shape[0] - 1]
    cols = heads * HDIM
    for at in range(pieces):
        mixed[pl.ds(pl.multiple_of((piece ^ at) * ROWS, ROWS), ROWS), :] = lows[at][...]
    weight_last = weight_ref[:, 3 * cols :]
    att_grad = dot(mixed[...], weight_last).astype(BF16)
    grad_last = dot(mixed[...], att_ref[...], TN)
    tiles = bias_tiles(rel_ref, piece * heads, heads)
    proj = proj_ref[...]
    length = proj.shape[0]
    blocks = length // BLOCK
    flipped = iota((BLOCK, BLOCK), 0) + iota((BLOCK, BLOCK), 1) == BLOCK - 1
    flipped = flipped.astype(F32).astype(BF16)
    wide = 2 * BLOCK
    lines = []
    grads_q, grads_k, grads_v = [], [], []
    for head in range(heads):
        at = head * HDIM
        key_sum = [jnp.zeros((BLOCK, HDIM), F32) for _ in range(blocks)]
        value_sum = [jnp.zeros((BLOCK, HDIM), F32) for _ in range(blocks)]
        near_sum = None
        query_done = []
        for block in reversed(range(blocks)):
            here = slice(block * BLOCK, (block + 1) * BLOCK)
            upto = slice(0, (block + 1) * BLOCK)
            query = proj[here, at : at + HDIM]
            keys = proj[upto, cols + at : cols + at + HDIM]
            values = proj[upto, 2 * cols + at : 2 * cols + at + HDIM]
            out_grad = att_grad[here, at : at + HDIM]
            scores = masked_scores(query, keys, tiles[head], second, block)
            again = jnp.exp(scores - lse_ref[here, head : head + 1])
            prob_grad = dot(out_grad, values, NT)
            weighted = again * prob_grad
            score_grad = weighted - again * jnp.sum(weighted, axis=1, keepdims=True)
            score_low = score_grad.astype(BF16)
            value_add = dot(again.astype(BF16), out_grad, TN)
            key_add = dot(score_low, query, TN)
            for other in range(block + 1):
                there = slice(other * BLOCK, (other + 1) * BLOCK)
                key_sum[other] = key_sum[other] + key_add[there, :]
                value_sum[other] = value_sum[other] + value_add[there, :]
            if block == 1:
                near_sum = score_grad
            else:
                near_sum = jnp.concatenate(
                    [near_sum[:, :BLOCK], near_sum[:, BLOCK:] + score_grad], axis=1
                )
            query_done.insert(0, dot(score_low, keys) * HDIM**-0.5)
        grads_q.append(jnp.concatenate(query_done, axis=0))
        grads_k.append(jnp.concatenate(key_sum, axis=0) * HDIM**-0.5)
        grads_v.append(jnp.concatenate(value_sum, axis=0))
        near_high = near_sum.astype(BF16)
        near_low = (near_sum - near_high.astype(F32)).astype(BF16)
        turned = dot(flipped, near_high) + dot(flipped, near_low)
        turned = pltpu.roll(turned, BLOCK + 1, 1, stride=1, stride_axis=0)
        lines.append(jnp.sum(turned, axis=0, keepdims=True))
    lines = jnp.concatenate(lines + [jnp.zeros((8 - heads, wide), F32)], axis=0)
    line_bucket = bucket_of((BLOCK - iota((wide, 128), 0)) & (wide - 1))
    spread = (line_bucket == iota((wide, 128), 1)).astype(F32)
    by_bucket = jnp.concatenate(
        [dot(lines, spread, precision=HIGHEST), jnp.zeros((8, HEADS * BUCKETS - 128), F32)], axis=1
    )
    bias_row = jnp.zeros((1, HEADS * BUCKETS), F32)
    for head in range(heads):
        placed = pltpu.roll(by_bucket, (piece * heads + head) * BUCKETS, 1)
        bias_row = bias_row + placed[head : head + 1, :]
    grad_proj[...] = jnp.concatenate(grads_q + grads_k + grads_v, axis=1).astype(BF16)
    x = row_ref[...].astype(F32)
    scale = lax.rsqrt(jnp.mean(x * x, axis=1, keepdims=True) + 1e-6)
    unit = x * scale
    normed = (unit * gain_ref[...]).astype(BF16)
    grad_first = dot(normed, grad_proj[...], TN)
    if parts > 1:
        grads = outs[n_grads + 7]
        depth = grad_first.shape[0] // parts
        grads[:, : 3 * cols] = grad_first
        grads[:, 3 * cols :] = grad_last
        for at in range(parts):
            piece_rows = grads[pl.ds(pl.multiple_of((mine_dp ^ at) * depth, 16), depth), :]
            if at % 2 == 0:
                grad_outs[at // 2][...] = piece_rows
            else:
                grad_outs[parts // 2 + (at == 1)][max(at // 2 - 1, 0)] = piece_rows.astype(BF16)
    else:
        grad_outs[0][:, : 3 * cols] = grad_first
        grad_outs[0][:, 3 * cols :] = grad_last
    normed_grad[...] = dot(grad_proj[...], weight_ref[:, : 3 * cols], NT)
    sums_out[...] = sums_ref[...]
    sums_out[experts + 1 : experts + 2, :] = jnp.sum(
        normed_grad[...] * unit, axis=0, keepdims=True
    )
    sums_out[experts + 2 : experts + 3, : HEADS * BUCKETS] = bias_row
    for at in range(pieces):
        mine = normed_grad[pl.ds(pl.multiple_of((piece ^ at) * ROWS, ROWS), ROWS), :]
        if at % 2 == 0:
            keep_out[at // 2][...] = mine
        else:
            send_out[at // 2 * ROWS : (at // 2 + 1) * ROWS, :] = mine.astype(BF16)
    send_out[pieces // 2 * ROWS :, :] = sums_out[...].astype(BF16)


def fold_back_kernel(keep_ref, near_ref, sums_ref, out_ref, sums_out):
    out_ref[:ROWS, :] = (keep_ref[...] + near_ref[ROWS : 2 * ROWS, :].astype(F32)).astype(BF16)
    sums = sums_ref[...] + near_ref[2 * ROWS :, :].astype(F32)
    sums_out[...] = sums
    out_ref[ROWS:, :] = sums.astype(BF16)


def join_kernel(sums_ref, far_ref, out_ref, low_ref):
    sums = sums_ref[...] + far_ref[ROWS:, :].astype(F32)
    out_ref[...] = sums
    low_ref[...] = sums.astype(BF16)


def input_kernel(own_ref, gain_ref, mixed_grad_ref, part_ref, near_ref, far_ref, out_ref):
    x = own_ref[...].astype(F32)
    scale = lax.rsqrt(jnp.mean(x * x, axis=1, keepdims=True) + 1e-6)
    scaled = (
        part_ref[...] + near_ref[:ROWS, :].astype(F32) + far_ref[:ROWS, :].astype(F32)
    ) * gain_ref[...]
    cubed = scale * scale * scale
    own = scale * scaled - x * cubed * jnp.mean(scaled * x, axis=1, keepdims=True)
    out_ref[...] = (mixed_grad_ref[...] + own).astype(BF16)


def swap(value, axis, size, mask):
    return lax.ppermute(value, axis, [(i, i ^ mask) for i in range(size)])


def gather_weights(shard, senders):
    if senders != 8:
        return [lax.all_gather(shard, "dp", axis=0, tiled=True)]
    parts = {0: shard}
    parts[1] = swap(shard, "dp", senders, 1)
    for mask in (2, 4, 6):
        parts[mask] = swap(shard, "dp", senders, mask)
    for mask in (2, 4, 6):
        parts[mask + 1] = swap(parts[mask], "dp", senders, 1)
    return [parts[i] for i in range(senders)]


def fold_kernel(keep_ref, near_ref, out_ref):
    out_ref[...] = (keep_ref[...] + near_ref[...].astype(F32)).astype(BF16)


def fold(keep, near, name, after=()):
    return call(fold_kernel, [struct(near.shape, BF16)], [], [keep, near], name=name, after=after)[0]


def finish_kernel(cols, keep_ref, near_ref, one_ref, two_ref, three_ref, first_ref, last_ref):
    total = keep_ref[...] + near_ref[...].astype(F32)
    for part in (one_ref, two_ref, three_ref):
        total = total + part[...].astype(F32)
    for at in range(3):
        first_ref[at] = total[:, at * cols : (at + 1) * cols]
    last_ref[...] = total[:, 3 * cols :]


def fold_three_kernel(one_ref, two_ref, three_ref, near_ref, sums_ref, got_ref, *outs):
    *chunks, sums_out = outs
    sums = sums_ref[...] + got_ref[...].astype(F32)
    sums_out[...] = sums
    for at, (keep, out) in enumerate(zip((one_ref, two_ref, three_ref), chunks)):
        depth = keep.shape[0]
        out[:depth, :] = (keep[...] + near_ref[at].astype(F32)).astype(BF16)
        out[depth:, :] = sums.astype(BF16)


def put_small(total, experts, gains_ref, bias_ref, router_ref):
    router_ref[...] = total[:experts]
    gains_ref[0:2, :] = total[experts : experts + 2]
    for head in range(HEADS):
        bias_ref[head : head + 1, :] = total[
            experts + 2 : experts + 3, head * BUCKETS : (head + 1) * BUCKETS
        ]


def finish_kernel(cols, experts, keep_ref, near_ref, sums_ref, *refs):
    *parts, first_ref, last_ref, gains_ref, bias_ref, router_ref = refs
    depth = keep_ref.shape[0]
    total = keep_ref[...] + near_ref[0].astype(F32)
    small = sums_ref[...]
    for part in parts:
        total = total + part[:depth, :].astype(F32)
        small = small + part[depth:, :].astype(F32)
    for at in range(3):
        first_ref[at] = total[:, at * cols : (at + 1) * cols]
    last_ref[...] = total[:, 3 * cols :]
    put_small(small, experts, gains_ref, bias_ref, router_ref)


def sums_kernel(experts, sums_ref, gains_ref, bias_ref, router_ref):
    put_small(sums_ref[...], experts, gains_ref, bias_ref, router_ref)


def last_sums(grads, keep_a, keep_b, near, sums, senders, pieces, cols, experts, before):
    count, width = sums.shape
    if senders == 8:
        near_grads = swap(grads[4], "dp", senders, 1)
        near_last = swap(grads[5], "dp", senders, 1)
    other, sums = call(
        fold_back_kernel,
        [struct((ROWS + count, width), BF16), struct((count, width), F32)],
        [],
        [keep_b, near, sums],
        name="fold_rows",
        prompt=True,
    )
    far = swap(other, "tensor", pieces, 2)
    sums, low = call(
        join_kernel,
        [struct((count, width), F32), struct((count, width), BF16)],
        [],
        [sums, far],
        name="join",
        prompt=True,
    )
    small = [
        struct((8, width), F32),
        struct((HEADS, BUCKETS), F32),
        struct((experts, width), F32),
    ]
    if senders != 8:
        total = lax.psum_scatter(grads[0], "dp", scatter_dimension=0, tiled=True)
        first = jnp.stack([total[:, at * cols : (at + 1) * cols] for at in range(3)])
        weight_sums = (first, total[:, 3 * cols :])
        small = call(
            functools.partial(sums_kernel, experts), small, [], [lax.psum(sums, "dp")], name="sums"
        )
    else:
        depth = grads[0].shape[0]
        got = swap(low, "dp", senders, 1)
        *folded, sums = call(
            fold_three_kernel,
            [struct((depth + count, width), BF16)] * 3 + [struct((count, width), F32)],
            [],
            [grads[1], grads[2], grads[3], near_grads, sums, got],
            name="fold_weights",
            prompt=True,
            after=before,
        )
        arrived = [swap(folded[at], "dp", senders, 2 * at + 2) for at in (2, 1, 0)]
        first, last, *small = call(
            functools.partial(finish_kernel, cols, experts),
            [struct((3, depth, cols), F32), struct((depth, cols), F32)] + small,
            [],
            [grads[0], near_last, sums] + arrived,
            name="finish",
            prompt=True,
        )
        weight_sums = (first, last)
    return weight_sums, (keep_a, near, far), small


def scatter_rows(keep_a, keep_b, near, pieces, after=()):
    other = call(
        lambda keep, got, out: fold_kernel(keep, got.at[1], out),
        [struct(keep_b.shape, BF16)],
        [],
        [keep_b, near],
        name="fold_rows", prompt=True,
        after=after,
    )[0]
    return keep_a, near, swap(other, "tensor", pieces, 2), other


def gather_rows(rows, pieces):
    far = swap(rows, "tensor", pieces, 2)
    near = swap(rows, "tensor", pieces, 1)
    last = swap(far, "tensor", pieces, 1)
    return [rows, near, far, last]


def exchange(blocks, senders, capacity):
    rows, width = blocks.shape
    return lax.all_to_all(
        blocks.reshape(senders, capacity, width), "dp", split_axis=0, concat_axis=0, tiled=True
    ).reshape(rows, width)


def body(
    tokens,
    doc_start,
    routes,
    gain_attn,
    w_qkv,
    w_out,
    rel_bias,
    gain_ffn,
    router,
    w_in,
    w_exp_out,
    out_grad,
):
    pieces = lax.axis_size("tensor")
    senders = lax.axis_size("dp")
    tok_dev, width = tokens.shape
    routes, rel_bias, router = routes.T, rel_bias.T, router.T
    length = tok_dev * pieces
    experts = router.shape[0]
    capacity = max(2, 3 * tok_dev * routes.shape[0] // (2 * experts))
    slots = experts * capacity
    heads = w_out.shape[1] // HDIM
    cols = heads * HDIM
    gain_one = gain_attn.reshape(1, width)
    gain_two = gain_ffn.reshape(1, width)

    shard, in_head = call(
        pack_kernel,
        [
            struct((w_out.shape[0], 4 * cols), BF16),
            struct((width // 3, w_in.shape[2]), BF16),
        ],
        [],
        [w_qkv.transpose(1, 0, 2), w_out, w_in[0]],
        name="pack",
        held=(0, 1, 2),
        parts={2: (width // 3, w_in.shape[2])},
    )
    weights = gather_weights(shard, senders)
    rows = gather_rows(tokens, pieces)
    out_one = w_exp_out[0]
    in_one = w_in[0]
    out_two = swap(out_one, "tensor", pieces, 2)
    in_two_a = swap(in_head, "tensor", pieces, 2)
    in_two_b = swap(in_one[in_head.shape[0] :], "tensor", pieces, 2)

    slot, grad_out = call(
        functools.partial(slots_kernel, capacity),
        [struct((tok_dev, 128), jnp.int32), struct((slots, width), BF16)],
        [],
        [routes, out_grad],
        flops=2 * slots * tok_dev * width,
        name="slots",
        held=(1,),
        kept=(0, 1),
    )

    grad_out = once(grad_out, weights[1::2], "gathered")
    whole_weight, whole_rows, projected, attended, lse, keep_a, keep_b, send = call(
        functools.partial(forward_kernel, len(weights), pieces, heads),
        [
            struct((width, 4 * cols), BF16),
            struct((length, width), BF16),
            struct((length, 3 * cols), BF16),
            struct((length, cols), BF16),
            struct((length, 128), F32),
            struct((tok_dev, width), F32),
            struct((tok_dev, width), F32),
            struct((pieces // 2, tok_dev, width), BF16),
        ],
        [],
        [doc_start, rel_bias] + weights + rows + [gain_one],
        smem=2,
        flops=2 * length * width * 4 * cols + 4 * heads * length * length * HDIM,
        name="attend",
        held=tuple(range(2, 2 + len(weights))),
        kept=(0, 1, 2, 3, 4),
        vmem=12,
    )
    pull_own = exchange(grad_out, senders, capacity)
    pull_mate = swap(pull_own, "tensor", pieces, 1)
    far_pull_own = swap(pull_own, "tensor", pieces, 2)

    near = swap(send, "tensor", pieces, 1)
    part, near, far, _ = scatter_rows(keep_a, keep_b, near, pieces, [out_two, in_two_a])
    mixed, normed_two, gates, outgoing = call(
        dispatch_kernel,
        [
            struct((tok_dev, width), F32),
            struct((tok_dev, width), BF16),
            struct((tok_dev, 128), F32),
            struct((slots, width + GATE_LANES), BF16),
        ],
        [],
        [tokens, part, near, far, gain_two, router, routes, slot],
        flops=2 * slots * tok_dev * width,
        name="dispatch",
        after=[pull_own],
        kept=(0, 1, 2),
    )
    slot_own = exchange(outgoing, senders, capacity)
    slot_mate = swap(slot_own, "tensor", pieces, 1)
    payload = width + GATE_LANES
    units = in_one.shape[1]
    hidden_one, pre_one, hidden_two, row_keep, row_send = call(
        expert_kernel,
        [struct((2 * slots, units), BF16)] * 3
        + [struct((slots, payload), F32), struct((slots, payload), BF16)],
        [
            pltpu.VMEM((2 * slots, width), BF16),
            pltpu.VMEM((2 * slots, width), BF16),
            pltpu.VMEM((width, units), BF16),
            pltpu.VMEM((2 * slots, units), BF16),
        ],
        [
            slot_own,
            slot_mate,
            pull_own,
            pull_mate,
            in_one,
            out_one,
            in_two_a,
            in_two_b,
            out_two,
        ],
        name="experts",
        prompt=True,
        held=(4, 5, 6, 7, 8),
        kept=(0, 1, 2),
        vmem=30,
    )
    row_mate = swap(row_send, "tensor", pieces, 1)
    far_own = swap(slot_own, "tensor", pieces, 2)
    (row_out,) = call(
        merge_kernel,
        [struct((slots, payload), BF16)],
        [],
        [row_keep, row_mate],
        name="merge",
    )
    back = exchange(row_out, senders, capacity)

    far_mate = swap(far_own, "tensor", pieces, 1)
    out_keep, out_send = call(
        expert_out_kernel,
        [struct((slots, width), F32), struct((slots, width), BF16)],
        [],
        [hidden_one, hidden_two, out_one, out_two],
        flops=4 * 2 * slots * width * in_one.shape[1],
        name="expert_out",
        held=(0, 1, 2, 3),
        after=[row_out],
        vmem=10,
    )
    turned = [pltpu.VMEM((width, 2 * slots), BF16), pltpu.VMEM((2 * slots, width), BF16)]
    grads_both = [struct(in_one.shape, F32), struct(out_one.shape, F32), struct((8, 128), F32)]
    own_in, own_out, own_graded = call(
        own_grads_kernel,
        grads_both,
        turned,
        [slot_own, slot_mate, pull_own, pull_mate, hidden_one, pre_one],
        flops=8 * slots * width * units,
        name="own_grads",
        after=[out_send, far_own],
        held=(0, 1, 2, 3, 4, 5),
        vmem=24,
    )
    far_pull_own = once(far_pull_own, [own_graded], "pulled")
    far_pull_mate = swap(far_pull_own, "tensor", pieces, 1)
    grad_in, grad_out_sum, graded = call(
        far_grads_kernel,
        grads_both,
        turned + [pltpu.VMEM((2 * slots, width), BF16)],
        [far_own, far_mate, far_pull_own, far_pull_mate, in_one, out_one, own_in, own_out],
        flops=16 * slots * width * units,
        name="far_grads",
        held=(4, 5),
        vmem=30,
    )

    sum_rows = -(-(experts + 3) // 8) * 8
    mixed_grad, mixed_low, sums_two = call(
        combine_kernel,
        [
            struct((tok_dev, width), F32),
            struct((tok_dev, width), BF16),
            struct((sum_rows, width), F32),
        ],
        [],
        [back, slot, gates, mixed, normed_two, router, routes, out_grad, gain_two],
        flops=2 * slots * tok_dev * width,
        name="combine",
        after=[graded],
        held=(1, 2, 3, 4, 7),
    )
    expert_out = fold(out_keep, swap(out_send, "tensor", pieces, 1), "fold_out", [mixed_low])
    returned = exchange(expert_out, senders, capacity)
    result, given = call(
        result_kernel,
        [struct((tok_dev, width), BF16), struct((8, 128), F32)],
        [],
        [returned, slot, gates, mixed],
        flops=4 * slots * tok_dev * width,
        name="result", prompt=True,
        held=(1, 2, 3),
    )

    lows = gather_rows(mixed_low, pieces)
    parts = len(weights)
    if parts > 1:
        depth = width // parts
        grad_shapes = [struct((depth, 4 * cols), F32)] * (parts // 2)
        grad_shapes += [struct((n, depth, 4 * cols), BF16) for n in (parts // 2 - 1, 1)]
        grad_scratch = [pltpu.VMEM((width, 4 * cols), F32)]
    else:
        grad_shapes = [struct((width, 4 * cols), F32)]
        grad_scratch = []
    *weight_grads, keep_a, keep_b, send, sums = call(
        functools.partial(backward_kernel, parts, pieces, heads, experts),
        grad_shapes
        + [
            struct((tok_dev, width), F32),
            struct((tok_dev, width), F32),
            struct((pieces // 2 * tok_dev + sum_rows, width), BF16),
            struct((sum_rows, width), F32),
        ],
        [
            pltpu.VMEM((length, width), BF16),
            pltpu.VMEM((length, 3 * cols), BF16),
            pltpu.VMEM((length, width), F32),
        ]
        + grad_scratch,
        [doc_start, rel_bias]
        + lows
        + [whole_weight, whole_rows, projected, attended, lse, gain_one, sums_two],
        smem=2,
        name="attend_back",
        prompt=True,
        held=tuple(range(2 + pieces, 7 + pieces)),
        vmem=16,
    )
    near = swap(send, "tensor", pieces, 1)
    (first_sum, last_sum), (part, near, far), (gains, bias_grad, router_grad) = last_sums(
        weight_grads, keep_a, keep_b, near, sums, senders, pieces, cols, experts, [given]
    )
    (input_grad,) = call(
        input_kernel,
        [struct((tok_dev, width), BF16)],
        [],
        [tokens, gain_one, mixed_grad, part, near, far],
        name="input_grad", prompt=True,
        held=(0, 2),
    )
    return (
        result,
        input_grad,
        gains[1],
        first_sum.transpose(1, 0, 2),
        last_sum,
        bias_grad.T,
        gains[0],
        router_grad.T,
        grad_in[None],
        grad_out_sum[None],
    )


def solution(mesh):
    in_specs = (
        P(("dp", "tensor"), None),
        P("dp"),
        P(("dp", "tensor"), None),
        P(),
        P("dp", None, "tensor"),
        P("dp", "tensor"),
        P(),
        P(),
        P(),
        P("dp", None, "tensor"),
        P("dp", "tensor", None),
        P(("dp", "tensor"), None),
    )
    out_specs = (
        P(("dp", "tensor"), None),
        P(("dp", "tensor"), None),
        P(),
        P("dp", None, "tensor"),
        P("dp", "tensor"),
        P(),
        P(),
        P(),
        P("dp", None, "tensor"),
        P("dp", "tensor", None),
    )
    return jax.shard_map(body, mesh=mesh, in_specs=in_specs, out_specs=out_specs, check_vma=False)
```
